32 devices in a mesh: dp: 8 (over y, x, core), mp: 4 (over z).
Axes of the slice: x: 2, y: 2, z: 4, core: 2. Of those that a mesh axis runs over, the one named last changes fastest.
Arguments:
- inputs: bfloat16 [16384, 1024], P(('dp', 'mp')), may hold values from -6 to 6
- w_query: bfloat16 [1024, 1024], P(None, 'mp'), may hold values from -0.1875 to 0.1875
- w_key: bfloat16 [1024, 1024], P(None, 'mp'), may hold values from -0.1875 to 0.1875
- w_value: bfloat16 [1024, 1024], P(None, 'mp'), may hold values from -0.1875 to 0.1875
- w_gate: bfloat16 [1024, 1024], P(None, 'mp'), may hold values from -0.1875 to 0.1875
- head_gain: float32 [1024], P('mp'), may hold values from 0.1 to 1.9
- w_out: bfloat16 [1024, 1024], P('mp'), may hold values from -0.25 to 0.25
- w_first: bfloat16 [1024, 2816], P(None, 'mp'), may hold values from -0.1875 to 0.1875
- w_second: bfloat16 [1024, 2816], P(None, 'mp'), may hold values from -0.1875 to 0.1875
- w_third: bfloat16 [2816, 1024], P('mp'), may hold values from -0.109375 to 0.109375
- cotangent: bfloat16 [16384, 1024], P(('dp', 'mp')), may hold values from -6 to 6
Outputs:
- output: float32 [16384, 1024], P(('dp', 'mp'))
- grad_inputs: float32 [16384, 1024], P(('dp', 'mp'))
- grad_w_query: float32 [1024, 1024], P(None, 'mp')
- grad_w_key: float32 [1024, 1024], P(None, 'mp')
- grad_w_value: float32 [1024, 1024], P(None, 'mp')
- grad_w_gate: float32 [1024, 1024], P(None, 'mp')
- grad_head_gain: float32 [1024], P('mp')
- grad_w_out: float32 [1024, 1024], P('mp')
- grad_w_first: float32 [1024, 2816], P(None, 'mp')
- grad_w_second: float32 [1024, 2816], P(None, 'mp')
- grad_w_third: float32 [2816, 1024], P('mp')
The draws below stay inside these ranges and needn't reach their ends.
All inputs are finite; a program needn't handle non-finite values.
Results may differ from the reference program's by a relative error of at most 0.014.
Values may be sent and summed in bfloat16 or wider, within the bound.
A program may use at most 192 MiB of HBM per device.

```python
import jax
import jax.numpy as jnp
from jax import lax

D = 1024
H = 16
DH = 64
FF = 2816
BLK = 64
LEN = 2048
HD = 1024
TOKENS = 16384


def shard_levels(stream_key, extent, shards, low, top_value):
    def one(position, shards_of):
        heights = jax.random.uniform(jax.random.fold_in(jax.random.fold_in(stream_key, 6), position), (shards_of,), jnp.float32, low / len(shards), top_value / len(shards))
        return jnp.repeat(jnp.exp(heights), extent[position] // shards_of).reshape((-1,) + (1,) * (len(extent) - position - 1))

    level = one(*shards[0])
    for cut in shards[1:]:
        level = level * one(*cut)
    return level


def bell_draw(stream_key, shape, deviation, most, cuts=(), held_as=jnp.bfloat16):
    level = shard_levels(stream_key, shape, cuts, -0.22, 0.18) if cuts else 1.0
    entries = jax.random.normal(stream_key, shape, jnp.float32) * deviation * level
    return jnp.minimum(jnp.maximum(entries, -most), most).astype(held_as)


def setup_inputs(seed: int = 0) -> dict:
    key_list = jax.random.split(jax.random.key(seed), 12)
    inputs = bell_draw(key_list[0], (TOKENS, D), 1.0, 6.0, ((0, 32),))
    w_query = bell_draw(key_list[1], (D, HD), D ** -0.5, 0.1875, ((1, 4),))
    w_key = bell_draw(key_list[2], (D, HD), D ** -0.5, 0.1875, ((1, 4),))
    w_value = bell_draw(key_list[3], (D, HD), D ** -0.5, 0.1875, ((1, 4),))
    w_gate = bell_draw(key_list[4], (D, HD), D ** -0.5, 0.1875, ((1, 4),))
    head_gain = jnp.clip(1.0 + 0.18 * jax.random.normal(key_list[5], (HD,), jnp.float32), 0.1, 1.9)
    w_out = bell_draw(key_list[6], (HD, D), (HD // 2) ** -0.5, 0.25, ((0, 4),))
    w_first = bell_draw(key_list[7], (D, FF), D ** -0.5, 0.1875, ((1, 4),))
    w_second = bell_draw(key_list[8], (D, FF), D ** -0.5, 0.1875, ((1, 4),))
    w_third = bell_draw(key_list[9], (FF, D), FF ** -0.5, 0.109375, ((0, 4),))
    cotangent = bell_draw(key_list[10], (TOKENS, D), 1.0, 6.0, ((0, 32),))
    return dict(inputs=inputs, w_query=w_query, w_key=w_key, w_value=w_value, w_gate=w_gate, head_gain=head_gain, w_out=w_out, w_first=w_first, w_second=w_second, w_third=w_third, cotangent=cotangent)


EPSILON = 1e-06
PRECISION = lax.Precision.HIGHEST

@jax.custom_vjp
def low(v):
    return lax.optimization_barrier(v.astype(jnp.bfloat16)).astype(jnp.float32)

@jax.custom_vjp
def low_back(v):
    return v

def low_keep(v):
    return (low(v), None)

def low_pass(kept, grad):
    return (grad,)

def back_keep(v):
    return (v, None)

def back_low(kept, grad):
    return (low(grad),)
low.defvjp(low_keep, low_pass)
low_back.defvjp(back_keep, back_low)

def simple_norm(values):
    return values * lax.rsqrt(lax.optimization_barrier(jnp.mean(values * values, axis=-1, keepdims=True)) + EPSILON)

def product_high(left, right):
    return jnp.dot(left, right, precision=PRECISION)

def layer(inputs, w_query, w_key, w_value, w_gate, head_gain, w_out, w_first, w_second, w_third):
    length = inputs.shape[0]
    block_shape = (length // BLK, BLK, H, DH)
    normed_in = low(simple_norm(inputs))
    queries = low(low_back(product_high(normed_in, w_query)))
    key_rows = low(low_back(product_high(normed_in, w_key)))
    values = low(low_back(product_high(normed_in, w_value)))
    gate_pre = low_back(product_high(normed_in, w_gate))
    scores = low_back(jnp.einsum('bqhd,bkhd->bhqk', queries.reshape(block_shape), key_rows.reshape(block_shape), precision=PRECISION) * DH ** (-0.5))
    causal = lax.broadcasted_iota(jnp.int32, (BLK, BLK), 0) >= lax.broadcasted_iota(jnp.int32, (BLK, BLK), 1)
    softmax_out = low(jax.nn.softmax(jnp.where(causal, scores, -jnp.inf), axis=-1))
    attended = low_back(jnp.einsum('bhqk,bkhd->bqhd', softmax_out, values.reshape(block_shape), precision=PRECISION).reshape(length, H * DH))
    per_head = attended.reshape(length, H, DH)
    normed = (per_head * lax.rsqrt(lax.optimization_barrier(jnp.mean(per_head * per_head, axis=-1, keepdims=True)) + EPSILON)).reshape(length, H * DH)
    gated = low(normed * head_gain * jax.nn.silu(gate_pre))
    hidden_res = inputs + low_back(product_high(gated, w_out))
    ffn_in = low(simple_norm(hidden_res))
    proj_first = low_back(product_high(ffn_in, w_first))
    proj_second = low_back(product_high(ffn_in, w_second))
    product = low(proj_first * proj_second)
    return hidden_res + low_back(product_high(product, w_third))

def reference(inputs, w_query, w_key, w_value, w_gate, head_gain, w_out, w_first, w_second, w_third, cotangent):
    weights = (w_query.astype(jnp.float32), w_key.astype(jnp.float32), w_value.astype(jnp.float32), w_gate.astype(jnp.float32), head_gain.astype(jnp.float32), w_out.astype(jnp.float32), w_first.astype(jnp.float32), w_second.astype(jnp.float32), w_third.astype(jnp.float32))
    model_width = inputs.shape[1]
    sequences = inputs.shape[0] // LEN
    seq_inputs = inputs.astype(jnp.float32).reshape(sequences, LEN, model_width)
    seq_cotangent = cotangent.astype(jnp.float32).reshape(sequences, LEN, model_width)

    def one_sequence(totals, pieces):
        result, pullback = jax.vjp(layer, pieces[0], *weights)
        gradients = pullback(pieces[1])
        totals = tuple((summed + update for summed, update in zip(totals, gradients[1:])))
        return (totals, (result, gradients[0]))
    initial = tuple((jnp.zeros_like(weight) for weight in weights))
    totals, (results, grad_rows) = lax.scan(one_sequence, initial, (seq_inputs, seq_cotangent))
    return (results.reshape(-1, model_width), grad_rows.reshape(-1, model_width), totals[0], totals[1], totals[2], totals[3], totals[4], totals[5], totals[6], totals[7], totals[8])
```

```python
import jax
import jax.numpy as jnp
from jax import lax
from jax.sharding import PartitionSpec as P

DH = 64
BLK = 64


EPSILON = 1e-06


def simple_norm(values):
    return values * lax.rsqrt(jnp.mean(values * values, axis=-1, keepdims=True) + EPSILON)


def norm_back(values, gradient):
    factor = lax.rsqrt(jnp.mean(values * values, axis=-1, keepdims=True) + EPSILON)
    normed = values * factor
    return factor * (gradient - normed * jnp.mean(gradient * normed, axis=-1, keepdims=True))


def matmul(left, right):
    return jnp.dot(left, right, preferred_element_type=jnp.float32)


def matmul_tn(left, right):
    return lax.dot_general(
        left, right, (((0,), (0,)), ((), ())), preferred_element_type=jnp.float32
    )


def matmul_nt(left, right):
    return lax.dot_general(
        left, right, (((1,), (1,)), ((), ())), preferred_element_type=jnp.float32
    )


def blocked(matrix):
    return matrix.reshape(matrix.shape[0] // BLK, BLK, matrix.shape[1] // DH, DH)


def attention_weights(queries, key_rows):
    scores = jnp.einsum(
        "bqhd,bkhd->bhqk", blocked(queries), blocked(key_rows), preferred_element_type=jnp.float32
    ) * DH ** (-0.5)
    causal = lax.broadcasted_iota(jnp.int32, (BLK, BLK), 0) >= lax.broadcasted_iota(
        jnp.int32, (BLK, BLK), 1
    )
    scores = jnp.where(causal, scores, -jnp.inf)
    shifted = jnp.exp(scores - jnp.max(scores, axis=-1, keepdims=True))
    return shifted / jnp.sum(shifted, axis=-1, keepdims=True)


ALL = ("mp", "dp")


def gather_weight(weight):
    rows = weight.shape[0] // lax.axis_size("dp")
    part = lax.dynamic_slice_in_dim(weight, lax.axis_index("dp") * rows, rows, 0)
    full = lax.all_gather(part, ALL, axis=0, tiled=True)
    return full.reshape(lax.axis_size("mp"), weight.shape[0], weight.shape[1])


def reduce_gradient(stacked):
    shards_, rows, columns = stacked.shape
    part = lax.psum_scatter(stacked.reshape(shards_ * rows, columns), ALL, scatter_dimension=0, tiled=True)
    return lax.all_gather(part, "dp", axis=0, tiled=True)


def shards(
    inputs, w_query, w_key, w_value, w_gate, head_gain, w_out, w_first, w_second, w_third, cotangent
):
    low = jnp.bfloat16
    parts = lax.axis_size("mp")
    heads_wide = w_query.shape[1]
    w_in = gather_weight(jnp.concatenate([w_query, w_key, w_value, w_gate], axis=1))
    full_out = gather_weight(w_out).reshape(-1, w_out.shape[1])
    full_first = gather_weight(w_first)
    full_second = gather_weight(w_second)
    full_third = gather_weight(w_third).reshape(-1, w_third.shape[1])
    gain = lax.all_gather(head_gain, "mp", axis=0, tiled=True)

    residual = inputs.astype(jnp.float32)
    attn_in = simple_norm(residual).astype(low)
    proj = [matmul(attn_in, w_in[m]) for m in range(parts)]

    def field(i):
        return jnp.concatenate([p[:, i * heads_wide : (i + 1) * heads_wide] for p in proj], axis=1)

    queries = field(0).astype(low)
    key_rows = field(1).astype(low)
    values = field(2).astype(low)
    gate_pre = field(3)
    flat_shape = gate_pre.shape
    softmax_out = attention_weights(queries, key_rows)
    softmax_low = softmax_out.astype(low)
    attended = jnp.einsum(
        "bhqk,bkhd->bqhd", softmax_low, blocked(values), preferred_element_type=jnp.float32
    )
    per_head = attended.reshape(flat_shape[0], flat_shape[1] // DH, DH)
    factor = lax.rsqrt(jnp.mean(per_head * per_head, axis=-1, keepdims=True) + EPSILON)
    normed = per_head * factor
    normed_flat = normed.reshape(flat_shape)
    activated = jax.nn.silu(gate_pre)
    gated = (normed_flat * gain * activated).astype(low)
    hidden_res = residual + matmul(gated, full_out)
    ffn_in = simple_norm(hidden_res).astype(low)
    proj_first = jnp.concatenate([matmul(ffn_in, full_first[m]) for m in range(parts)], axis=1)
    proj_second = jnp.concatenate([matmul(ffn_in, full_second[m]) for m in range(parts)], axis=1)
    product = (proj_first * proj_second).astype(low)
    output = hidden_res + matmul(product, full_third)
    grad_product = matmul_nt(cotangent, full_third)
    grad_first = (grad_product * proj_second).astype(low)
    grad_second = (grad_product * proj_first).astype(low)
    hidden_part = w_first.shape[1]

    def cut(array, m, width):
        return array[:, m * width : (m + 1) * width]

    grad_ffn_in = sum(
        matmul_nt(cut(grad_first, m, hidden_part), full_first[m])
        + matmul_nt(cut(grad_second, m, hidden_part), full_second[m])
        for m in range(parts)
    )
    grad_w_third = reduce_gradient(matmul_tn(product, cotangent).astype(low).reshape(parts, hidden_part, -1))
    grad_w_first = reduce_gradient(
        jnp.stack([matmul_tn(ffn_in, cut(grad_first, m, hidden_part)).astype(low) for m in range(parts)])
    )
    grad_w_second = reduce_gradient(
        jnp.stack([matmul_tn(ffn_in, cut(grad_second, m, hidden_part)).astype(low) for m in range(parts)])
    )
    grad_hidden = cotangent.astype(jnp.float32) + norm_back(hidden_res, grad_ffn_in)
    hidden_low = grad_hidden.astype(low)
    grad_gated = matmul_nt(hidden_low, full_out)
    grad_w_out = reduce_gradient(matmul_tn(gated, hidden_low).astype(low).reshape(parts, heads_wide, -1))
    logistic = jax.nn.sigmoid(gate_pre)
    grad_head_gain = jnp.sum(grad_gated * activated * normed_flat, axis=0)
    grad_gate = (
        grad_gated * normed_flat * gain * logistic * (1.0 + gate_pre * (1.0 - logistic))
    ).astype(low)
    grad_normed = (grad_gated * activated * gain).reshape(normed.shape)
    grad_attended = factor * (
        grad_normed - normed * jnp.mean(grad_normed * normed, axis=-1, keepdims=True)
    )
    grad_blocks = blocked(grad_attended.reshape(flat_shape).astype(low))
    grad_values = (
        jnp.einsum("bhqk,bqhd->bkhd", softmax_low, grad_blocks, preferred_element_type=jnp.float32)
        .reshape(flat_shape)
        .astype(low)
    )
    grad_softmax = jnp.einsum(
        "bqhd,bkhd->bhqk", grad_blocks, blocked(values), preferred_element_type=jnp.float32
    )
    grad_scores = (
        softmax_out * (grad_softmax - jnp.sum(grad_softmax * softmax_out, axis=-1, keepdims=True))
    ).astype(low)
    grad_queries = (
        (
            jnp.einsum("bhqk,bkhd->bqhd", grad_scores, blocked(key_rows), preferred_element_type=jnp.float32)
            * DH ** (-0.5)
        )
        .reshape(flat_shape)
        .astype(low)
    )
    grad_keys = (
        (
            jnp.einsum("bhqk,bqhd->bkhd", grad_scores, blocked(queries), preferred_element_type=jnp.float32)
            * DH ** (-0.5)
        )
        .reshape(flat_shape)
        .astype(low)
    )
    grad_proj = [
        jnp.concatenate(
            [cut(g, m, heads_wide) for g in (grad_queries, grad_keys, grad_values, grad_gate)], axis=1
        )
        for m in range(parts)
    ]
    grad_attn_in = sum(matmul_nt(grad_proj[m], w_in[m]) for m in range(parts))
    grad_inputs = grad_hidden + norm_back(residual, grad_attn_in)
    grad_w_in = reduce_gradient(jnp.stack([matmul_tn(attn_in, grad_proj[m]).astype(low) for m in range(parts)]))
    grad_head_gain = lax.psum(grad_head_gain, ALL)
    grad_head_gain = lax.dynamic_slice_in_dim(grad_head_gain, lax.axis_index("mp") * heads_wide, heads_wide, 0)
    wide = jnp.float32
    return (
        output,
        grad_inputs,
        cut(grad_w_in, 0, heads_wide).astype(wide),
        cut(grad_w_in, 1, heads_wide).astype(wide),
        cut(grad_w_in, 2, heads_wide).astype(wide),
        cut(grad_w_in, 3, heads_wide).astype(wide),
        grad_head_gain,
        grad_w_out.astype(wide),
        grad_w_first.astype(wide),
        grad_w_second.astype(wide),
        grad_w_third.astype(wide),
    )


def solution(mesh):
    placed = (
        P(("dp", "mp"), None),
        P(None, "mp"),
        P(None, "mp"),
        P(None, "mp"),
        P(None, "mp"),
        P("mp"),
        P("mp", None),
        P(None, "mp"),
        P(None, "mp"),
        P("mp", None),
        P(("dp", "mp"), None),
    )
    return jax.shard_map(
        shards,
        mesh=mesh,
        in_specs=placed,
        out_specs=(
            P(("dp", "mp"), None),
            P(("dp", "mp"), None),
            P(None, "mp"),
            P(None, "mp"),
            P(None, "mp"),
            P(None, "mp"),
            P("mp"),
            P("mp", None),
            P(None, "mp"),
            P(None, "mp"),
            P("mp", None),
        ),
        check_vma=False,
    )
```

```python
import functools

import jax
import jax.numpy as jnp
from jax import lax
from jax.experimental import pallas as pl
from jax.experimental.pallas import tpu as pltpu
from jax.sharding import PartitionSpec as P

DH = 64
BLK = 64


EPSILON = 1e-06


def simple_norm(values):
    return values * lax.rsqrt(jnp.mean(values * values, axis=-1, keepdims=True) + EPSILON)


def norm_back(values, gradient):
    factor = lax.rsqrt(jnp.mean(values * values, axis=-1, keepdims=True) + EPSILON)
    normed = values * factor
    return factor * (gradient - normed * jnp.mean(gradient * normed, axis=-1, keepdims=True))


def matmul(left, right):
    return jnp.dot(left, right, preferred_element_type=jnp.float32)


def matmul_tn(left, right):
    return lax.dot_general(
        left, right, (((0,), (0,)), ((), ())), preferred_element_type=jnp.float32
    )


def matmul_nt(left, right):
    return lax.dot_general(
        left, right, (((1,), (1,)), ((), ())), preferred_element_type=jnp.float32
    )


def blocked(matrix):
    return matrix.reshape(matrix.shape[0] // BLK, BLK, matrix.shape[1] // DH, DH)


def attention_weights(queries, key_rows):
    scores = jnp.einsum(
        "bqhd,bkhd->bhqk", blocked(queries), blocked(key_rows), preferred_element_type=jnp.float32
    ) * DH ** (-0.5)
    causal = lax.broadcasted_iota(jnp.int32, (BLK, BLK), 0) >= lax.broadcasted_iota(
        jnp.int32, (BLK, BLK), 1
    )
    scores = jnp.where(causal, scores, -jnp.inf)
    shifted = jnp.exp(scores - jnp.max(scores, axis=-1, keepdims=True))
    return shifted / jnp.sum(shifted, axis=-1, keepdims=True)


ALL = ("mp", "dp")


MESH = pl.DeviceIdType.MESH
W = [(1024,256)]*4 + [(256,1024), (1024,704),(1024,704),(704,1024)]
CH = [(0,0,0,0,256),(1,0,256,0,256),(2,0,512,0,256),(3,0,768,0,256),(4,1,0,0,64),(5,2,0,0,128),(5,2,0,128,128),(6,3,0,0,128),(6,3,0,128,128),(7,4,0,0,96),(7,4,0,96,80)]
NC = len(CH)
BUF = [(1024,1024),(256,1024),(1024,704),(1024,704),(704,1024)]
LA = 2
def split(rows):
    q = rows//4
    h = (q//2 + 15)//16*16
    return q, h

def gather_kernel(order, *refs):
    ins = refs[:8]; outs = refs[8:13]; bufs = refs[13:18]; zs, zr, xs, xr, ys, yr, fs, fr, fzs, loc = refs[18:]
    dp = lax.axis_index("dp"); z = lax.axis_index("mp")
    c = dp % 2; bx = (dp//2)%2; by = (dp//4)%2; p = by*2+bx
    xn = dp + 2 - 4*bx; yn = dp + 4 - 8*by
    px = by*2 + 1-bx; py = (1-by)*2 + bx; pd = (1-by)*2 + 1-bx
    bar = pltpu.get_barrier_semaphore()
    base = dp - 2*p
    peers = []
    for k in range(4):
        for zz in range(4):
            pl.semaphore_signal(bar, inc=1, device_id=(base+2*k, zz), device_id_type=MESH)
    pl.semaphore_wait(bar, 16)
    innet = z//2 == c
    own = z % 2
    def sl(ref, j, ch, row, rows):
        i, b, co, _, _ = ch
        cols = W[i][1]
        if BUF[b][1] == cols: return bufs[b].at[j, pl.ds(pl.multiple_of(row,16), rows), :]
        return bufs[b].at[j, pl.ds(pl.multiple_of(row,16), rows), pl.ds(co, cols)]
    def rc(src, dst, s, r, d): return pltpu.make_async_remote_copy(src, dst, s, r, device_id=d, device_id_type=MESH)
    def part(ch, who):
        q = W[ch[0]][0]//4
        h = (ch[4]//2+15)//16*16
        return who*q + ch[3], ch[4], h
    def zsrc(k, d):
        ch = CH[k]; r0, n, h = part(ch, p)
        return rc(ins[ch[0]].at[pl.ds(pl.multiple_of(r0,16), n), :], sl(None, own, ch, r0, n), zs.at[k, d], zr.at[k, own], (dp, z+1-2*d))
    def zfwd(k, j, d):
        ch = CH[k]; r0, n, h = part(ch, p); r = sl(None, j, ch, r0, n)
        return rc(r, r, fzs.at[k, j], zr.at[k, j], (dp, z+1-2*d))
    @pl.when(innet)
    def _():
        for k in range(NC):
            @pl.when(z<3)
            def _(): zsrc(k, 0).start()
            @pl.when(z>0)
            def _(): zsrc(k, 1).start()
        for i, (b, co) in enumerate([(0,0),(0,256),(0,512),(0,768),(1,0),(2,0),(3,0),(4,0)]):
            dst = bufs[b].at[own] if b else bufs[b].at[own, :, pl.ds(co,256)]
            pltpu.make_async_copy(ins[i], dst, loc.at[i]).start()
    def xdesc(k, j):
        ch = CH[k]; r0, n, h = part(ch, p); r = sl(None, j, ch, r0, n)
        return rc(r, r, xs.at[k,j], xr.at[k,j], (xn, z))
    def ydesc(k, j):
        ch = CH[k]; r0, n, h = part(ch, p); r = sl(None, j, ch, r0, n)
        return rc(r, r, ys.at[k,j], yr.at[k,j], (yn, z))
    def fdesc0(k, j):
        ch = CH[k]; r0, n, h = part(ch, px); r = sl(None, j, ch, r0, h)
        return rc(r, r, fs.at[0,k,j], fr.at[0,k,j], (yn, z))
    def fdesc1(k, j):
        ch = CH[k]; r0, n, h = part(ch, py); r = sl(None, j, ch, r0+h, n-h)
        return rc(r, r, fs.at[1,k,j], fr.at[1,k,j], (xn, z))
    def A(k, j):
        s = 2*c + j
        zfwd(k, j, 0).wait_recv()
        @pl.when((z > s) & (z < 3))
        def _(): zfwd(k, j, 0).start()
        @pl.when((z < s) & (z > 0))
        def _(): zfwd(k, j, 1).start()
        xdesc(k, j).start(); ydesc(k, j).start()
    def B(k, j):
        xdesc(k, j).wait_recv(); fdesc0(k, j).start()
        ydesc(k, j).wait_recv(); fdesc1(k, j).start()
    def C(k, j):
        fdesc0(k, j).wait_recv(); fdesc1(k, j).wait_recv()
    j0 = jnp.where(innet, 1-own, 1-c)
    def steps(F, k):
        F(k, j0)
        @pl.when(jnp.logical_not(innet))
        def _(): F(k, 1-j0)
    for t in range(NC+2*LA):
        if t < NC: steps(A, t)
        if 0 <= t-LA < NC: steps(B, t-LA)
        if 0 <= t-2*LA < NC: steps(C, t-2*LA)
    @pl.when(innet)
    def _():
        for k in range(NC):
            @pl.when(z<3)
            def _(): zsrc(k, 0).wait_send()
            @pl.when(z>0)
            def _(): zsrc(k, 1).wait_send()
        for i, (b, co) in enumerate([(0,0),(0,256),(0,512),(0,768),(1,0),(2,0),(3,0),(4,0)]):
            dst = bufs[b].at[own] if b else bufs[b].at[own, :, pl.ds(co,256)]
            pltpu.make_async_copy(ins[i], dst, loc.at[i]).wait()
    def D(k, j):
        s = 2*c + j
        @pl.when(((z > s) & (z < 3)) | ((z < s) & (z > 0)))
        def _(): zfwd(k, j, 0).wait_send()
        xdesc(k, j).wait_send(); ydesc(k,j).wait_send(); fdesc0(k,j).wait_send(); fdesc1(k,j).wait_send()
    for k in range(NC): steps(D, k)
    for b in range(5):
        pltpu.make_async_copy(bufs[b], outs[b], loc.at[b]).start()
    for b in range(5):
        pltpu.make_async_copy(bufs[b], outs[b], loc.at[b]).wait()

def ring_weights(*ins):
    return pl.pallas_call(functools.partial(gather_kernel, None),
        out_shape=[jax.ShapeDtypeStruct((2,)+s, jnp.bfloat16) for s in BUF],
        in_specs=[pl.BlockSpec(memory_space=pl.ANY)]*8, out_specs=[pl.BlockSpec(memory_space=pl.ANY)]*5,
        scratch_shapes=[pltpu.VMEM((2,)+s, jnp.bfloat16) for s in BUF] + [pltpu.SemaphoreType.DMA((NC,2)), pltpu.SemaphoreType.DMA((NC,2))] + [pltpu.SemaphoreType.DMA((NC,2))]*4 + [pltpu.SemaphoreType.DMA((2,NC,2))]*2 + [pltpu.SemaphoreType.DMA((NC,2)), pltpu.SemaphoreType.DMA((8,))],
        compiler_params=pltpu.CompilerParams(collective_id=0, has_side_effects=True, vmem_limit_bytes=60*2**20), name="ag")(*ins)


def gather_weight(weight):
    rows = weight.shape[0] // lax.axis_size("dp")
    part = lax.dynamic_slice_in_dim(weight, lax.axis_index("dp") * rows, rows, 0)
    full = lax.all_gather(part, ALL, axis=0, tiled=True)
    return full.reshape(lax.axis_size("mp"), weight.shape[0], weight.shape[1])


def reduce_gradient(stacked):
    shards_, rows, columns = stacked.shape
    part = lax.psum_scatter(stacked.reshape(shards_ * rows, columns), ALL, scatter_dimension=0, tiled=True)
    return lax.all_gather(part, "dp", axis=0, tiled=True)


def shards(
    inputs, w_query, w_key, w_value, w_gate, head_gain, w_out, w_first, w_second, w_third, cotangent
):
    low = jnp.bfloat16
    parts = lax.axis_size("mp")
    heads_wide = w_query.shape[1]
    mine = ring_weights(w_query, w_key, w_value, w_gate, w_out, w_first, w_second, w_third)
    count = lax.axis_size("dp")
    pairs = [(i, i + 1 - 2 * (i % 2)) for i in range(count)]
    first = lax.axis_index("dp") % 2 == 0

    def both(array):
        other = lax.ppermute(array, "dp", pairs)
        return jnp.concatenate([jnp.where(first, array, other), jnp.where(first, other, array)])

    w_in, full_out, full_first, full_second, full_third = [both(m) for m in mine]
    full_out = full_out.reshape(-1, w_out.shape[1])
    full_third = full_third.reshape(-1, w_third.shape[1])
    gain = lax.all_gather(head_gain, "mp", axis=0, tiled=True)

    residual = inputs.astype(jnp.float32)
    attn_in = simple_norm(residual).astype(low)
    proj = [matmul(attn_in, w_in[m]) for m in range(parts)]

    def field(i):
        return jnp.concatenate([p[:, i * heads_wide : (i + 1) * heads_wide] for p in proj], axis=1)

    queries = field(0).astype(low)
    key_rows = field(1).astype(low)
    values = field(2).astype(low)
    gate_pre = field(3)
    flat_shape = gate_pre.shape
    softmax_out = attention_weights(queries, key_rows)
    softmax_low = softmax_out.astype(low)
    attended = jnp.einsum(
        "bhqk,bkhd->bqhd", softmax_low, blocked(values), preferred_element_type=jnp.float32
    )
    per_head = attended.reshape(flat_shape[0], flat_shape[1] // DH, DH)
    factor = lax.rsqrt(jnp.mean(per_head * per_head, axis=-1, keepdims=True) + EPSILON)
    normed = per_head * factor
    normed_flat = normed.reshape(flat_shape)
    activated = jax.nn.silu(gate_pre)
    gated = (normed_flat * gain * activated).astype(low)
    hidden_res = residual + matmul(gated, full_out)
    ffn_in = simple_norm(hidden_res).astype(low)
    proj_first = jnp.concatenate([matmul(ffn_in, full_first[m]) for m in range(parts)], axis=1)
    proj_second = jnp.concatenate([matmul(ffn_in, full_second[m]) for m in range(parts)], axis=1)
    product = (proj_first * proj_second).astype(low)
    output = hidden_res + matmul(product, full_third)
    grad_product = matmul_nt(cotangent, full_third)
    grad_first = (grad_product * proj_second).astype(low)
    grad_second = (grad_product * proj_first).astype(low)
    hidden_part = w_first.shape[1]

    def cut(array, m, width):
        return array[:, m * width : (m + 1) * width]

    grad_ffn_in = sum(
        matmul_nt(cut(grad_first, m, hidden_part), full_first[m])
        + matmul_nt(cut(grad_second, m, hidden_part), full_second[m])
        for m in range(parts)
    )
    grad_w_third = reduce_gradient(matmul_tn(product, cotangent).astype(low).reshape(parts, hidden_part, -1))
    grad_w_first = reduce_gradient(
        jnp.stack([matmul_tn(ffn_in, cut(grad_first, m, hidden_part)).astype(low) for m in range(parts)])
    )
    grad_w_second = reduce_gradient(
        jnp.stack([matmul_tn(ffn_in, cut(grad_second, m, hidden_part)).astype(low) for m in range(parts)])
    )
    grad_hidden = cotangent.astype(jnp.float32) + norm_back(hidden_res, grad_ffn_in)
    hidden_low = grad_hidden.astype(low)
    grad_gated = matmul_nt(hidden_low, full_out)
    grad_w_out = reduce_gradient(matmul_tn(gated, hidden_low).astype(low).reshape(parts, heads_wide, -1))
    logistic = jax.nn.sigmoid(gate_pre)
    grad_head_gain = jnp.sum(grad_gated * activated * normed_flat, axis=0)
    grad_gate = (
        grad_gated * normed_flat * gain * logistic * (1.0 + gate_pre * (1.0 - logistic))
    ).astype(low)
    grad_normed = (grad_gated * activated * gain).reshape(normed.shape)
    grad_attended = factor * (
        grad_normed - normed * jnp.mean(grad_normed * normed, axis=-1, keepdims=True)
    )
    grad_blocks = blocked(grad_attended.reshape(flat_shape).astype(low))
    grad_values = (
        jnp.einsum("bhqk,bqhd->bkhd", softmax_low, grad_blocks, preferred_element_type=jnp.float32)
        .reshape(flat_shape)
        .astype(low)
    )
    grad_softmax = jnp.einsum(
        "bqhd,bkhd->bhqk", grad_blocks, blocked(values), preferred_element_type=jnp.float32
    )
    grad_scores = (
        softmax_out * (grad_softmax - jnp.sum(grad_softmax * softmax_out, axis=-1, keepdims=True))
    ).astype(low)
    grad_queries = (
        (
            jnp.einsum("bhqk,bkhd->bqhd", grad_scores, blocked(key_rows), preferred_element_type=jnp.float32)
            * DH ** (-0.5)
        )
        .reshape(flat_shape)
        .astype(low)
    )
    grad_keys = (
        (
            jnp.einsum("bhqk,bqhd->bkhd", grad_scores, blocked(queries), preferred_element_type=jnp.float32)
            * DH ** (-0.5)
        )
        .reshape(flat_shape)
        .astype(low)
    )
    grad_proj = [
        jnp.concatenate(
            [cut(g, m, heads_wide) for g in (grad_queries, grad_keys, grad_values, grad_gate)], axis=1
        )
        for m in range(parts)
    ]
    grad_attn_in = sum(matmul_nt(grad_proj[m], w_in[m]) for m in range(parts))
    grad_inputs = grad_hidden + norm_back(residual, grad_attn_in)
    grad_w_in = reduce_gradient(jnp.stack([matmul_tn(attn_in, grad_proj[m]).astype(low) for m in range(parts)]))
    grad_head_gain = lax.psum(grad_head_gain, ALL)
    grad_head_gain = lax.dynamic_slice_in_dim(grad_head_gain, lax.axis_index("mp") * heads_wide, heads_wide, 0)
    wide = jnp.float32
    return (
        output,
        grad_inputs,
        cut(grad_w_in, 0, heads_wide).astype(wide),
        cut(grad_w_in, 1, heads_wide).astype(wide),
        cut(grad_w_in, 2, heads_wide).astype(wide),
        cut(grad_w_in, 3, heads_wide).astype(wide),
        grad_head_gain,
        grad_w_out.astype(wide),
        grad_w_first.astype(wide),
        grad_w_second.astype(wide),
        grad_w_third.astype(wide),
    )


def solution(mesh):
    placed = (
        P(("dp", "mp"), None),
        P(None, "mp"),
        P(None, "mp"),
        P(None, "mp"),
        P(None, "mp"),
        P("mp"),
        P("mp", None),
        P(None, "mp"),
        P(None, "mp"),
        P("mp", None),
        P(("dp", "mp"), None),
    )
    return jax.shard_map(
        shards,
        mesh=mesh,
        in_specs=placed,
        out_specs=(
            P(("dp", "mp"), None),
            P(("dp", "mp"), None),
            P(None, "mp"),
            P(None, "mp"),
            P(None, "mp"),
            P(None, "mp"),
            P("mp"),
            P("mp", None),
            P(None, "mp"),
            P(None, "mp"),
            P("mp", None),
        ),
        check_vma=False,
    )
```

```python
import functools

import jax
import jax.numpy as jnp
from jax import lax
from jax.experimental import pallas as pl
from jax.experimental.pallas import tpu as pltpu
from jax.sharding import PartitionSpec as P

DH = 64
BLK = 64
EPSILON = 1e-06
MESH = pl.DeviceIdType.MESH
F32 = jnp.float32
BF16 = jnp.bfloat16
UNIT = 128
VMEM_LIMIT = 60 * 2**20


def rms_factor(values):
    return lax.rsqrt(jnp.mean(values * values, axis=-1, keepdims=True) + EPSILON)


def dot(left, right):
    return jnp.dot(left, right, preferred_element_type=F32)


def dot_tn(left, right):
    return lax.dot_general(left, right, (((0,), (0,)), ((), ())), preferred_element_type=F32)


def dot_nt(left, right):
    return lax.dot_general(left, right, (((1,), (1,)), ((), ())), preferred_element_type=F32)


def remote(src, dst, send, recv, device):
    return pltpu.make_async_remote_copy(src, dst, send, recv, device_id=device, device_id_type=MESH)


def rows_of(start, count):
    return pl.ds(pl.multiple_of(start, 16), count)


class Place:
    def __init__(self):
        dp, self.z = lax.axis_index("dp"), lax.axis_index("mp")
        self.dp = dp
        self.c = dp % 2
        self.bx, self.by = (dp // 2) % 2, (dp // 4) % 2
        self.p = self.by * 2 + self.bx
        self.px, self.py = self.by * 2 + 1 - self.bx, (1 - self.by) * 2 + self.bx
        self.pd = (1 - self.by) * 2 + 1 - self.bx
        self.sib = (dp + 1 - 2 * self.c, self.z)
        self.xn = (dp + 2 - 4 * self.bx, self.z)
        self.yn = (dp + 4 - 8 * self.by, self.z)
        self.own = self.z % 2
        self.innet = self.z // 2 == self.c

    def up(self):
        return (self.dp, self.z + 1)

    def down(self):
        return (self.dp, self.z - 1)


def half_of(count):
    return (count // 2 + 15) // 16 * 16


def gather_plan(shapes):
    plan = []
    for i, (rows, _) in enumerate(shapes):
        quarter = rows // 4
        if i < 4:
            parts = [quarter]
        elif i == 4:
            parts = [quarter]
        else:
            first = half_of(quarter)
            parts = [first, quarter - first]
        start = 0
        for count in parts:
            plan.append((i, max(i - 3, 0), i * shapes[0][1] if i < 4 else 0, start, count))
            start += count
    return plan


def forward_kernel(plan, shapes, *refs):
    nw = 8
    x_in, cot_in, gain_in = refs[:3]
    w_in = refs[3 : 3 + nw]
    outs = refs[3 + nw : 3 + nw + 18]
    (w_out, a_out, qkv_out, u_out, o_out, p_out, z_out, h_out, b_out, m_out, d1_out, d2_out, cot_out, gain_out) = (
        outs[:5], *outs[5:]
    )
    scratch = refs[3 + nw + 18 :]
    bufs = scratch[:5]
    (x_ref, cot, a_ref, qkv, u_ref, o_ref, p_ref, z_ref, hs, hr, h_ref, b_ref, m_ref, d1, d2, gain) = scratch[5:21]
    (zs, zr, fzs, xs, xr, ys, yr, fs, fr, loc, gs, gr, es, er, sv) = scratch[21:]
    me = Place()
    z, c, own, innet = me.z, me.c, me.own, me.innet
    T = x_in.shape[0]
    TT = 2 * T
    count = len(plan)
    wide = shapes[0][1]

    bar = pltpu.get_barrier_semaphore()
    for d in (me.sib, me.xn, me.yn):
        pl.semaphore_signal(bar, inc=1, device_id=d, device_id_type=MESH)

    @pl.when(z < 3)
    def _():
        pl.semaphore_signal(bar, inc=1, device_id=me.up(), device_id_type=MESH)

    @pl.when(z > 0)
    def _():
        pl.semaphore_signal(bar, inc=1, device_id=me.down(), device_id_type=MESH)

    pl.semaphore_wait(bar, 3 + jnp.where(z < 3, 1, 0) + jnp.where(z > 0, 1, 0))

    def piece(k, who):
        i, _, _, start, rows = plan[k]
        return who * (shapes[i][0] // 4) + start, rows

    def part(j, k, row, rows):
        _, buf, col, _, _ = plan[k]
        ref = bufs[buf]
        if buf:
            return ref.at[j, rows_of(row, rows), :]
        return ref.at[j, rows_of(row, rows), pl.ds(col, wide)]

    def z_first(k, d):
        row, rows = piece(k, me.p)
        src = w_in[plan[k][0]].at[rows_of(row, rows), :]
        return remote(src, part(own, k, row, rows), zs.at[k, d], zr.at[k, own], (me.dp, z + 1 - 2 * d))

    def z_next(k, j, d):
        row, rows = piece(k, me.p)
        r = part(j, k, row, rows)
        return remote(r, r, fzs.at[k, j], zr.at[k, j], (me.dp, z + 1 - 2 * d))

    def to_x(k, j):
        row, rows = piece(k, me.p)
        r = part(j, k, row, rows)
        return remote(r, r, xs.at[k, j], xr.at[k, j], me.xn)

    def to_y(k, j):
        row, rows = piece(k, me.p)
        r = part(j, k, row, rows)
        return remote(r, r, ys.at[k, j], yr.at[k, j], me.yn)

    def x_then_y(k, j):
        row, rows = piece(k, me.px)
        r = part(j, k, row, half_of(rows))
        return remote(r, r, fs.at[0, k, j], fr.at[0, k, j], me.yn)

    def y_then_x(k, j):
        row, rows = piece(k, me.py)
        h = half_of(rows)
        r = part(j, k, row + h, rows - h)
        return remote(r, r, fs.at[1, k, j], fr.at[1, k, j], me.xn)

    def gain_copy(j, d, src):
        return remote(src, gain.at[j], gs.at[j, d], gr.at[j], (me.dp, z + 1 - 2 * d))

    def own_copies():
        copies = []
        for i in range(nw):
            dst = bufs[i - 3].at[own] if i > 3 else bufs[0].at[own, :, pl.ds(i * wide, wide)]
            copies.append(pltpu.make_async_copy(w_in[i], dst, loc.at[i]))
        copies.append(pltpu.make_async_copy(gain_in, gain.at[own], loc.at[nw]))
        return copies

    both = [
        remote(x_in, x_ref.at[pl.ds(T, T), :], es.at[0], er.at[0], me.sib),
        remote(cot_in, cot.at[pl.ds(T, T), :], es.at[1], er.at[1], me.sib),
    ]
    mine = [
        pltpu.make_async_copy(x_in, x_ref.at[pl.ds(0, T), :], loc.at[nw + 1]),
        pltpu.make_async_copy(cot_in, cot.at[pl.ds(0, T), :], loc.at[nw + 2]),
    ]
    mine[0].start()
    both[0].start()

    @pl.when(innet)
    def _():
        @pl.when(z < 3)
        def _():
            gain_copy(own, 0, gain_in).start()

        @pl.when(z > 0)
        def _():
            gain_copy(own, 1, gain_in).start()

        for k in range(count):
            @pl.when(z < 3)
            def _():
                z_first(k, 0).start()

            @pl.when(z > 0)
            def _():
                z_first(k, 1).start()

        for copy in own_copies():
            copy.start()

    mine[1].start()
    both[1].start()

    def upward(j):
        return (z > 2 * c + j) & (z < 3)

    def downward(j):
        return (z < 2 * c + j) & (z > 0)

    def others(step, *args):
        for j in (0, 1):
            @pl.when(z != 2 * c + j)
            def _():
                step(*args, j)

    def step_gain(j):
        gain_copy(j, 0, gain.at[j]).wait_recv()

        @pl.when(upward(j))
        def _():
            gain_copy(j, 0, gain.at[j]).start()

        @pl.when(downward(j))
        def _():
            gain_copy(j, 1, gain.at[j]).start()

    def step_a(k, j):
        z_next(k, j, 0).wait_recv()

        @pl.when(upward(j))
        def _():
            z_next(k, j, 0).start()

        @pl.when(downward(j))
        def _():
            z_next(k, j, 1).start()

        to_x(k, j).start()
        to_y(k, j).start()

    def step_b(k, j):
        to_x(k, j).wait_recv()
        x_then_y(k, j).start()
        to_y(k, j).wait_recv()
        y_then_x(k, j).start()

    def step_c(k, j):
        x_then_y(k, j).wait_recv()
        y_then_x(k, j).wait_recv()

    ahead = 2
    steps = []
    for t in range(count + 2 * ahead):
        for step, lag in ((step_a, 0), (step_b, ahead), (step_c, 2 * ahead)):
            if 0 <= t - lag < count:
                steps.append((step, t - lag))
    done = [0]

    def pump(until=None, number=0):
        while done[0] < len(steps) and (number > 0 or until is not None):
            step, k = steps[done[0]]
            others(step, k)
            done[0] += 1
            number -= 1
            if step is step_c and until is not None and k >= until:
                until = None

    saves = []

    def save(src, dst):
        copy = pltpu.make_async_copy(src, dst, sv.at[len(saves)])
        copy.start()
        saves.append(copy)

    mine[0].wait()
    both[0].wait_recv()

    def norm_rows(t, carry):
        rows = rows_of(t * UNIT, UNIT)
        values = x_ref[rows, :].astype(F32)
        a_ref[rows, :] = (values * rms_factor(values)).astype(BF16)
        return carry

    lax.fori_loop(0, TT // UNIT, norm_rows, 0)
    save(a_ref, a_out)

    @pl.when(innet)
    def _():
        for copy in own_copies():
            copy.wait()

    others(step_gain)

    lane = lax.broadcasted_iota(jnp.int32, (UNIT, UNIT), 1)
    low_half = lane < DH
    keep = [low_half.astype(F32).astype(BF16), (lane >= DH).astype(F32).astype(BF16)]
    row2 = lax.broadcasted_iota(jnp.int32, (2 * UNIT, UNIT), 0) % UNIT
    col2 = lax.broadcasted_iota(jnp.int32, (2 * UNIT, UNIT), 1)
    seen = (row2 // BLK == col2 // BLK) & (col2 <= row2)

    def attend(j):
        def project(r, carry):
            rows = rows_of(r * 256, 256)
            acc = dot(a_ref[rows, :], bufs[0][j])
            qkv[j, rows, :] = acc[:, : 3 * wide].astype(BF16)
            u_ref[j, rows, :] = acc[:, 3 * wide :]
            return carry

        lax.fori_loop(0, TT // 256, project, 0)

        def unit(t, carry):
            rows = rows_of(t * UNIT, UNIT)
            for pair in range(wide // UNIT):
                q, k, v = (qkv[j, rows, pl.ds(f * wide + pair * UNIT, UNIT)] for f in range(3))
                cols = pl.ds(pair * UNIT, UNIT)
                scores = dot_nt(jnp.concatenate([q * keep[0], q * keep[1]], axis=0), k) * DH ** (-0.5)
                scores = jnp.where(seen, scores, -1e30)
                shifted = jnp.exp(scores - jnp.max(scores, axis=-1, keepdims=True))
                soft = (shifted / jnp.sum(shifted, axis=-1, keepdims=True)).astype(BF16)
                p_ref[j, pair, t] = soft
                attended = dot(
                    jnp.concatenate([soft[:UNIT], soft[UNIT:]], axis=1),
                    jnp.concatenate([v * keep[0], v * keep[1]], axis=0),
                )
                o_ref[j, rows, cols] = attended
                square = attended * attended
                mean0 = jnp.sum(jnp.where(low_half, square, 0.0), axis=-1, keepdims=True) / DH
                mean1 = jnp.sum(jnp.where(low_half, 0.0, square), axis=-1, keepdims=True) / DH
                normed = attended * lax.rsqrt(jnp.where(low_half, mean0, mean1) + EPSILON)
                u = u_ref[j, rows, cols]
                g = gain[j, 0:1, cols]
                z_ref[j, rows, cols] = (normed * g * (u * jax.nn.sigmoid(u))).astype(BF16)
            return carry

        lax.fori_loop(0, TT // UNIT, unit, 0)

    pump(until=3)
    attend(0)
    pump(number=3)
    attend(1)
    pump(until=4)
    for src, dst in ((qkv, qkv_out), (u_ref, u_out), (o_ref, o_out), (p_ref, p_out), (z_ref, z_out), (gain, gain_out)):
        save(src, dst)
    save(bufs[0], w_out[0])
    save(bufs[1], w_out[1])

    def out_rows(row):
        rows = rows_of(row, 256)
        return dot(z_ref[0, rows, :], bufs[1][0]) + dot(z_ref[1, rows, :], bufs[1][1])

    swaps = []
    for i in range(T // 256):
        hs[pl.ds(i * 256, 256), :] = out_rows(T + i * 256)
        part_rows = pl.ds(i * 256, 256)
        swaps.append(remote(hs.at[part_rows, :], hr.at[part_rows, :], es.at[2 + i], er.at[2 + i], me.sib))
        swaps[-1].start()
    for i in range(T // 256):
        h_ref[pl.ds(i * 256, 256), :] = x_ref[pl.ds(i * 256, 256), :].astype(F32) + out_rows(i * 256)
    pump(number=3)
    for i, swap in enumerate(list(swaps)):
        swap.wait_recv()

        def add_rows(t, carry):
            rows = rows_of(i * 256 + t * UNIT, UNIT)
            values = h_ref[rows, :] + hr[rows, :]
            h_ref[rows, :] = values
            b_ref[rows, :] = (values * rms_factor(values)).astype(BF16)
            return carry

        lax.fori_loop(0, 256 // UNIT, add_rows, 0)
        b_rows = pl.ds(i * 256, 256)
        swaps.append(remote(b_ref.at[b_rows, :], b_ref.at[pl.ds(T + i * 256, 256), :], es.at[4 + i], er.at[4 + i], me.sib))
        swaps[-1].start()
    save(h_ref, h_out)
    pump(number=3)
    for swap in swaps[len(swaps) // 2 :]:
        swap.wait_recv()
    save(b_ref, b_out)

    first_parts = [k for k in range(count) if plan[k][1] == 2]
    second_parts = [k for k in range(count) if plan[k][1] == 3]
    third_parts = [k for k in range(count) if plan[k][1] == 4]

    def rows_loop(body):
        lax.fori_loop(0, TT // 256, lambda r, carry: (body(rows_of(r * 256, 256)), carry)[1], 0)

    pump(until=first_parts[-1])
    save(bufs[2], w_out[2])
    for j in (0, 1):
        def first(rows):
            d2[j, rows, :] = dot(b_ref[rows, :], bufs[2][j]).astype(BF16)

        rows_loop(first)
        pump(number=2)
    pump(until=second_parts[-1])
    save(bufs[3], w_out[3])
    for j in (0, 1):
        def second(rows):
            g2 = dot(b_ref[rows, :], bufs[3][j])
            d1[j, rows, :] = g2.astype(BF16)
            m_ref[j, rows, :] = (d2[j, rows, :].astype(F32) * g2).astype(BF16)

        rows_loop(second)
        pump(number=2)
    save(m_ref, m_out)
    mine[1].wait()
    both[1].wait_recv()
    save(cot, cot_out)
    pump(until=third_parts[-1])
    save(bufs[4], w_out[4])
    for j in (0, 1):
        def third(rows):
            dm = dot_nt(cot[rows, :], bufs[4][j])
            g2, g1 = d1[j, rows, :].astype(F32), d2[j, rows, :].astype(F32)
            d1[j, rows, :] = (dm * g2).astype(BF16)
            d2[j, rows, :] = (dm * g1).astype(BF16)

        rows_loop(third)
        save(d1.at[j], d1_out.at[j])
        save(d2.at[j], d2_out.at[j])

    @pl.when(innet)
    def _():
        for d, inside in ((0, z < 3), (1, z > 0)):
            @pl.when(inside)
            def _():
                gain_copy(own, d, gain_in).wait_send()
                for k in range(count):
                    z_first(k, d).wait_send()

    def ends(j):
        @pl.when(upward(j) | downward(j))
        def _():
            for k in range(count):
                z_next(k, j, 0).wait_send()

        @pl.when(upward(j))
        def _():
            gain_copy(j, 0, gain.at[j]).wait_send()

        @pl.when(downward(j))
        def _():
            gain_copy(j, 1, gain.at[j]).wait_send()

        for k in range(count):
            for copy in (to_x, to_y, x_then_y, y_then_x):
                copy(k, j).wait_send()

    others(ends)
    for copy in both + swaps:
        copy.wait_send()
    for copy in saves:
        copy.wait()


def any_spec(count):
    return [pl.BlockSpec(memory_space=pl.ANY)] * count


def run_forward(x, cot, gain, weights):
    T, D = x.shape
    TT = 2 * T
    shapes = [w.shape for w in weights]
    plan = gather_plan(shapes)
    wide, hidden = shapes[0][1], shapes[5][1]
    units, pairs = TT // UNIT, wide // UNIT
    buffers = [(2, D, 4 * wide), (2, wide, D), (2, D, hidden), (2, D, hidden), (2, hidden, D)]
    kept = [
        ((TT, D), BF16),
        ((2, TT, 3 * wide), BF16),
        ((2, TT, wide), F32),
        ((2, TT, wide), F32),
        ((2, pairs, units, 2 * UNIT, UNIT), BF16),
        ((2, TT, wide), BF16),
        ((T, D), F32),
        ((TT, D), BF16),
        ((2, TT, hidden), BF16),
        ((2, TT, hidden), BF16),
        ((2, TT, hidden), BF16),
        ((TT, D), BF16),
        ((2, 8, wide), F32),
    ]
    vmem = [pltpu.VMEM(s, BF16) for s in buffers] + [
        pltpu.VMEM((TT, D), BF16),
        pltpu.VMEM((TT, D), BF16),
        pltpu.VMEM((TT, D), BF16),
        pltpu.VMEM((2, TT, 3 * wide), BF16),
        pltpu.VMEM((2, TT, wide), F32),
        pltpu.VMEM((2, TT, wide), F32),
        pltpu.VMEM((2, pairs, units, 2 * UNIT, UNIT), BF16),
        pltpu.VMEM((2, TT, wide), BF16),
        pltpu.VMEM((T, D), F32),
        pltpu.VMEM((T, D), F32),
        pltpu.VMEM((T, D), F32),
        pltpu.VMEM((TT, D), BF16),
        pltpu.VMEM((2, TT, hidden), BF16),
        pltpu.VMEM((2, TT, hidden), BF16),
        pltpu.VMEM((2, TT, hidden), BF16),
        pltpu.VMEM((2, 8, wide), F32),
    ]
    n = len(plan)
    dma = pltpu.SemaphoreType.DMA
    sems = [dma((n, 2))] * 7 + [dma((2, n, 2))] * 2 + [dma((11,)), dma((2, 2)), dma((2,)), dma((6,)), dma((6,)), dma((24,))]
    return pl.pallas_call(
        functools.partial(forward_kernel, plan, shapes),
        out_shape=[jax.ShapeDtypeStruct(s, BF16) for s in buffers] + [jax.ShapeDtypeStruct(s, t) for s, t in kept],
        in_specs=any_spec(3 + len(weights)),
        out_specs=any_spec(len(buffers) + len(kept)),
        scratch_shapes=vmem + sems,
        compiler_params=pltpu.CompilerParams(collective_id=0, has_side_effects=True, vmem_limit_bytes=VMEM_LIMIT),
        cost_estimate=pl.CostEstimate(flops=16 * 10**9, bytes_accessed=80 * 10**6, transcendentals=10**6),
        name="forward",
    )(x, cot, gain, *weights)


def backward_kernel(shapes, spare, *refs):
    (x_in, w0_in, wo_in, w1_in, w2_in, w3_in, a_in, qkv_in, u_in, o_in, p_in, z_in, h_in, b_in, m_in, d1_in, d2_in) = refs[:17]
    cot_in, gain_in = refs[17:19]
    out_out, dx_out = refs[19:21]
    final = refs[21:26]
    gain_out = refs[26]
    scratch = refs[27:]
    if spare:
        rq, scratch = scratch[:5], scratch[5:]
    gb, ra1, rb1, ra2, rb2, rz = (scratch[5 * i : 5 * i + 5] for i in range(6))
    (hs, hr, es_da, er_da, er_out, dh, dhl, gacc, gx, gy, gz, gq, stage) = scratch[30:43]
    (s1, r1, s2, r2, sz, rzs, sx, rx, sy, ry, sf, rf, ss, rs, sq, rqs, ld, es, er, gss, grs) = scratch[43:]
    me = Place()
    z, c, own, innet, p = me.z, me.c, me.own, me.innet, me.p
    bx, by = me.bx, me.by
    T, D = x_in.shape
    TT = 2 * T
    wide = wo_in.shape[1]
    hidden = w1_in.shape[2]
    arrays = range(5)

    def other_quad(e):
        bit = 8 << e
        return (me.dp + bit - 2 * bit * ((me.dp // bit) % 2), z)

    def other_z(t):
        return (me.dp, lax.rem(z + t, 4))

    bar = pltpu.get_barrier_semaphore()
    greeted = [me.sib, me.xn, me.yn] + [other_z(t) for t in (1, 2, 3)] + [other_quad(e) for e in range(spare)]
    for d in greeted:
        pl.semaphore_signal(bar, inc=1, device_id=d, device_id_type=MESH)
    pl.semaphore_wait(bar, len(greeted))

    quarters = [s[0] // 4 for s in shapes]
    halves = [half_of(q) for q in quarters]

    def add_rows(dst, sources, rows):
        def body(t, carry):
            r = rows_of(t * 16, 16)
            total = dst[r, :].astype(F32)
            for src in sources:
                total = total + src[r, :].astype(F32)
            dst[r, :] = total.astype(BF16)
            return carry

        lax.fori_loop(0, rows // 16, body, 0)

    def first_half(i, j, who):
        return gb[i].at[j, rows_of(who * quarters[i], halves[i]), :]

    def second_half(i, j, who):
        return gb[i].at[j, rows_of(who * quarters[i] + halves[i], quarters[i] - halves[i]), :]

    def whole(i, j, who):
        return gb[i].at[j, rows_of(who * quarters[i], quarters[i]), :]

    def round1(i, j):
        copies = []
        for b in (0, 1):
            copies.append(
                remote(first_half(i, j, b * 2 + 1 - bx), ra1[i].at[j, b], s1.at[i, j, b], r1.at[i, j, b], me.xn)
            )
            copies.append(
                remote(second_half(i, j, (1 - by) * 2 + b), rb1[i].at[j, b], s1.at[i, j, 2 + b], r1.at[i, j, 2 + b], me.yn)
            )
        return copies

    def round2(i, j):
        return [
            remote(first_half(i, j, (1 - by) * 2 + bx), ra2[i].at[j], s2.at[i, j, 0], r2.at[i, j, 0], me.yn),
            remote(second_half(i, j, by * 2 + 1 - bx), rb2[i].at[j], s2.at[i, j, 1], r2.at[i, j, 1], me.xn),
        ]

    def round_z(i, j):
        slot = lax.rem(z - (2 * c + j) + 3 + 4, 4)
        return remote(whole(i, j, p), rz[i].at[slot], sz.at[i, j], rzs.at[i, slot], (me.dp, 2 * c + j))

    def landed_z(i, slot):
        return remote(rz[i].at[slot], rz[i].at[slot], sz.at[i, 0], rzs.at[i, slot], me.sib)

    def spread(i, j):
        src = whole(i, j, p)
        dst = final[i].at[rows_of(p * quarters[i], quarters[i]), :]
        return [
            remote(src, dst, sx.at[i], rx.at[i], me.xn),
            remote(src, dst, sy.at[i], ry.at[i], me.yn),
            remote(src, dst, ss.at[i, 0], rs.at[i, 0], me.sib),
        ], pltpu.make_async_copy(src, dst, ld.at[32 + i])

    def quarter_rows(i, who, second=None):
        q, h = quarters[i], halves[i]
        if second is None:
            return final[i].at[rows_of(who * q, q), :]
        if second:
            return final[i].at[rows_of(who * q + h, q - h), :]
        return final[i].at[rows_of(who * q, h), :]

    def hand_on(i, slot, ref):
        return remote(ref, ref, ss.at[i, slot], rs.at[i, slot], me.sib)

    def pass_x(i):
        r = quarter_rows(i, me.px, False)
        return remote(r, r, sf.at[i, 0], rf.at[i, 0], me.yn), hand_on(i, 1, quarter_rows(i, me.px))

    def pass_y(i):
        r = quarter_rows(i, me.py, True)
        return remote(r, r, sf.at[i, 1], rf.at[i, 1], me.xn), hand_on(i, 2, quarter_rows(i, me.py))

    def pass_last(i):
        return hand_on(i, 3, quarter_rows(i, me.pd, False)), hand_on(i, 4, quarter_rows(i, me.pd, True))

    def step_1(i, j):
        for copy in round1(i, j):
            copy.start()

    def step_2(i, j):
        for copy in round1(i, j):
            copy.wait_recv()
        add_rows(first_half(i, j, (1 - by) * 2 + bx), [ra1[i].at[j, 1 - by]], halves[i])
        add_rows(second_half(i, j, by * 2 + 1 - bx), [rb1[i].at[j, 1 - bx]], quarters[i] - halves[i])
        for copy in round2(i, j):
            copy.start()

    def step_3(i, j):
        for copy in round2(i, j):
            copy.wait_recv()
        add_rows(first_half(i, j, p), [ra1[i].at[j, by], ra2[i].at[j]], halves[i])
        add_rows(second_half(i, j, p), [rb1[i].at[j, bx], rb2[i].at[j]], quarters[i] - halves[i])

        @pl.when(z != 2 * c + j)
        def _():
            round_z(i, j).start()

    def step_4(i, j):
        @pl.when(z == 2 * c + j)
        def _():
            for slot in range(3):
                landed_z(i, slot).wait_recv()
            add_rows(whole(i, j, p), [rz[i].at[slot] for slot in range(3)], quarters[i])
            for e in range(spare):
                copy = remote(whole(i, j, p), rq[i].at[e], sq.at[i, e], rqs.at[i, e], other_quad(e))
                copy.start()
                copy.wait()
                h = halves[i]
                for k, (part, src) in enumerate(
                    ((ra2[i].at[j], rq[i].at[e, pl.ds(0, h), :]), (rb2[i].at[j], rq[i].at[e, pl.ds(h, quarters[i] - h), :]))
                ):
                    local = pltpu.make_async_copy(src, part, sq.at[i, k])
                    local.start()
                    local.wait()
                add_rows(first_half(i, j, p), [ra2[i].at[j]], h)
                add_rows(second_half(i, j, p), [rb2[i].at[j]], quarters[i] - h)
            copies, local = spread(i, j)
            for copy in copies:
                copy.start()
            local.start()

    def step_5(i, j):
        @pl.when(z == 2 * c + j)
        def _():
            copies, _ = spread(i, j)
            copies[0].wait_recv()
            for copy in pass_x(i):
                copy.start()
            copies[1].wait_recv()
            for copy in pass_y(i):
                copy.start()

    def step_6(i, j):
        @pl.when(z == 2 * c + j)
        def _():
            pass_x(i)[0].wait_recv()
            pass_y(i)[0].wait_recv()
            for copy in pass_last(i):
                copy.start()

    items = [(4, 0), (4, 1), (2, 0), (2, 1), (3, 0), (3, 1), (1, 0), (1, 1), (0, 0), (0, 1)]
    steps = []
    stages = ((step_2, 2), (step_3, 4), (step_4, 6), (step_5, 7), (step_6, 8))
    for t in range(len(items) + 9):
        for step, lag in stages:
            if 0 <= t - lag < len(items):
                steps.append((step, items[t - lag]))
    sent = [0]
    done = [0]

    def send(i, j):
        step_1(i, j)
        sent[0] += 1

    def pump(number):
        while done[0] < len(steps) and number > 0:
            step, item = steps[done[0]]
            if items.index(item) >= sent[0]:
                return
            step(*item)
            done[0] += 1
            number -= 1

    loads = [0]

    def load(src, dst):
        copy = pltpu.make_async_copy(src, dst, ld.at[loads[0]])
        copy.start()
        loads[0] += 1
        return copy

    h_load = load(h_in, stage.at[0])

    def loop(count, body):
        lax.fori_loop(0, count, lambda t, carry: (body(t), carry)[1], 0)

    def feed_forward(b_ref, d1, d2):
        b_load, d1_load, d2_load = load(b_in, b_ref), load(d1_in, d1), load(d2_in, d2)

        def third(m_ref, cot):
            for copy in (load(m_in, m_ref), load(cot_in, cot)):
                copy.wait()
            for j in (0, 1):
                for start in range(0, hidden, 256):
                    size = min(256, hidden - start)
                    gb[4][j, pl.ds(start, size), :] = dot_tn(m_ref[j, :, pl.ds(start, size)], cot[...]).astype(BF16)
                send(4, j)

        pl.run_scoped(third, pltpu.VMEM((2, TT, hidden), BF16), pltpu.VMEM((TT, D), BF16))

        def first_two(w1, w2):
            w_loads = [load(w1_in, w1), load(w2_in, w2)]
            for copy in (b_load, d1_load, d2_load):
                copy.wait()
            for i, d in ((2, d1), (3, d2)):
                for j in (0, 1):
                    def block(t):
                        rows = pl.ds(pl.multiple_of(t * 256, 256), 256)
                        gb[i][j, rows, :] = dot_tn(b_ref[:, rows], d[j]).astype(BF16)

                    loop(D // 256, block)
                    send(i, j)
                    pump(1 if i == 2 else 2)
            for copy in w_loads:
                copy.wait()

            def db_rows(row):
                rows = rows_of(row, 256)
                total = dot_nt(d1[0, rows, :], w1[0]) + dot_nt(d2[0, rows, :], w2[0])
                return total + dot_nt(d1[1, rows, :], w1[1]) + dot_nt(d2[1, rows, :], w2[1])

            for t in range(T // 256):
                part = pl.ds(t * 256, 256)
                hs[part, :] = db_rows(T + t * 256)
                swap(t).start()
                pump(1)
            for t in range(T // 256):
                dh[pl.ds(t * 256, 256), :] = db_rows(t * 256)
                pump(1)

        pl.run_scoped(first_two, pltpu.VMEM((2, D, hidden), BF16), pltpu.VMEM((2, D, hidden), BF16))

    def swap(t):
        part = pl.ds(t * 256, 256)
        return remote(hs.at[part, :], hr.at[part, :], es.at[t], er.at[t], me.sib)

    def swap_low(t):
        part = pl.ds(t * 256, 256)
        return remote(dhl.at[part, :], dhl.at[pl.ds(T + t * 256, 256), :], es.at[2 + t], er.at[2 + t], me.sib)

    def swap_da(t):
        part = pl.ds(t * 256, 256)
        return remote(es_da.at[part, :], er_da.at[part, :], es.at[4 + t], er.at[4 + t], me.sib)

    def swap_out(t):
        part = pl.ds(t * 256, 256)
        return remote(es_da.at[part, :], er_out.at[part, :], es.at[6 + t], er.at[6 + t], me.sib)

    pl.run_scoped(
        feed_forward, pltpu.VMEM((TT, D), BF16), pltpu.VMEM((2, TT, hidden), BF16), pltpu.VMEM((2, TT, hidden), BF16)
    )

    lane = lax.broadcasted_iota(jnp.int32, (UNIT, UNIT), 1)
    low_half = lane < DH
    keep = [low_half.astype(F32).astype(BF16), (lane >= DH).astype(F32).astype(BF16)]

    def stacked(values):
        return jnp.concatenate([values * keep[0], values * keep[1]], axis=0)

    def head_mean(values):
        mean0 = jnp.sum(jnp.where(low_half, values, 0.0), axis=-1, keepdims=True) / DH
        mean1 = jnp.sum(jnp.where(low_half, 0.0, values), axis=-1, keepdims=True) / DH
        return jnp.where(low_half, mean0, mean1)

    def attention(dproj, a_ref):
        a_load = load(a_in, a_ref)

        def inner(qkv, u_ref, o_ref, p_ref, wo, gain):
            copies = [
                load(src, dst)
                for src, dst in (
                    (cot_in.at[pl.ds(0, T), :], es_da), (wo_in, wo), (u_in, u_ref),
                    (o_in, o_ref), (p_in, p_ref), (qkv_in, qkv), (gain_in, gain),
                )
            ]
            h_load.wait()
            copies[0].wait()
            for t in range(T // 256):
                swap(t).wait_recv()

                def rows_body(r):
                    rows = rows_of(t * 256 + r * 64, 64)
                    db = dh[rows, :] + hr[rows, :]
                    h = stage[0, rows, :]
                    factor = rms_factor(h)
                    normed = h * factor
                    grad = es_da[rows, :].astype(F32) + factor * (
                        db - normed * jnp.mean(db * normed, axis=-1, keepdims=True)
                    )
                    dh[rows, :] = grad
                    dhl[rows, :] = grad.astype(BF16)

                loop(4, rows_body)
                swap_low(t).start()
                pump(1)
            for copy in copies[1:]:
                copy.wait()
            gacc[...] = jnp.zeros_like(gacc)

            def out_grads(z_ref):
                z_load = load(z_in, z_ref)
                for t in range(T // 256):
                    swap_low(t).wait_recv()
                z_load.wait()
                for j in (0, 1):
                    gb[1][j] = dot_tn(z_ref[j], dhl[...]).astype(BF16)
                    send(1, j)
                    pump(1)

            pl.run_scoped(out_grads, pltpu.VMEM((2, TT, wide), BF16))
            pl.run_scoped(functools.partial(heads, qkv, u_ref, o_ref, p_ref, wo, gain), pltpu.VMEM((TT, wide), F32))

        def heads(qkv, u_ref, o_ref, p_ref, wo, gain, dz_ref):
            for j in (0, 1):
                def dz_rows(t):
                    rows = rows_of(t * 256, 256)
                    dz_ref[rows, :] = dot_nt(dhl[rows, :], wo[j])

                loop(TT // 256, dz_rows)

                def unit(t):
                    rows = rows_of(t * UNIT, UNIT)
                    for pair in range(wide // UNIT):
                        cols = pl.ds(pair * UNIT, UNIT)
                        q, k, v = (qkv[j, rows, pl.ds(f * wide + pair * UNIT, UNIT)] for f in range(3))
                        o, u, dz = o_ref[j, rows, cols], u_ref[j, rows, cols], dz_ref[rows, cols]
                        gain_row = gain[j, 0:1, cols]
                        factor = lax.rsqrt(head_mean(o * o) + EPSILON)
                        normed = o * factor
                        s = jax.nn.sigmoid(u)
                        act = u * s
                        dzn = dz * normed
                        gacc[j, :, cols] += jnp.sum((dzn * act).reshape(UNIT // 8, 8, UNIT), axis=0)
                        du = (dzn * gain_row * s * (1.0 + u * (1.0 - s))).astype(BF16)
                        dn = dz * act * gain_row
                        do = stacked((factor * (dn - normed * head_mean(dn * normed))).astype(BF16))
                        soft_low = p_ref[j, pair, t]
                        soft = soft_low.astype(F32)
                        dv = dot_tn(soft_low, do)
                        dp = dot_nt(do, v)
                        ds = (soft * (dp - jnp.sum(dp * soft, axis=-1, keepdims=True))).astype(BF16)
                        dq = dot(jnp.concatenate([ds[:UNIT], ds[UNIT:]], axis=1), stacked(k)) * DH ** (-0.5)
                        dk = dot_tn(ds, stacked(q)) * DH ** (-0.5)
                        for f, value in enumerate((dq, dk, dv)):
                            dproj[j, rows, pl.ds(f * wide + pair * UNIT, UNIT)] = value.astype(BF16)
                        dproj[j, rows, pl.ds(3 * wide + pair * UNIT, UNIT)] = du

                loop(TT // UNIT, unit)
                if j == 0:
                    a_load.wait()
                pump(1)

                def block(t):
                    rows = pl.ds(pl.multiple_of(t * 256, 256), 256)
                    gb[0][j, rows, :] = dot_tn(a_ref[:, rows], dproj[j]).astype(BF16)

                loop(D // 256, block)
                send(0, j)
                pump(2)

        pl.run_scoped(
            inner,
            pltpu.VMEM((2, TT, 3 * wide), BF16),
            pltpu.VMEM((2, TT, wide), F32),
            pltpu.VMEM((2, TT, wide), F32),
            pltpu.VMEM((2, wide // UNIT, TT // UNIT, 2 * UNIT, UNIT), BF16),
            pltpu.VMEM((2, wide, D), BF16),
            pltpu.VMEM((2, 8, wide), F32),
        )

        def inputs_part(w0, x_ref):
            for copy in (load(w0_in, w0), load(x_in, x_ref)):
                copy.wait()

            def da_rows(row):
                rows = rows_of(row, 256)
                return dot_nt(dproj[0, rows, :], w0[0]) + dot_nt(dproj[1, rows, :], w0[1])

            for t in range(T // 256):
                es_da[pl.ds(t * 256, 256), :] = da_rows(T + t * 256).astype(BF16)
                swap_da(t).start()
                pump(1)
            for t in range(T // 256):
                hs[pl.ds(t * 256, 256), :] = da_rows(t * 256)
                pump(1)
            for t in range(T // 256):
                swap_da(t).wait_recv()

                def rows_body(r):
                    rows = rows_of(t * 256 + r * 64, 64)
                    da = hs[rows, :] + er_da[rows, :].astype(F32)
                    x = x_ref[rows, :].astype(F32)
                    factor = rms_factor(x)
                    normed = x * factor
                    dh[rows, :] = dh[rows, :] + factor * (
                        da - normed * jnp.mean(da * normed, axis=-1, keepdims=True)
                    )

                loop(4, rows_body)
                pump(1)

        for t in range(T // 256):
            swap(t).wait_send()
        pl.run_scoped(inputs_part, pltpu.VMEM((2, D, 4 * wide), BF16), pltpu.VMEM((T, D), BF16))

    pl.run_scoped(attention, pltpu.VMEM((2, TT, 4 * wide), BF16), pltpu.VMEM((TT, D), BF16))
    dx_save = load(dh, dx_out)

    def gain_sum(k, src, dst, device, total):
        copy = remote(src, dst, gss.at[k], grs.at[k], device)
        copy.start()
        copy.wait()
        total[...] += dst[...]

    gain_sum(0, gacc, gx, me.xn, gacc)
    pump(2)
    gain_sum(1, gacc, gy, me.yn, gacc)

    def gain_z(j):
        slot = lax.rem(z - (2 * c + j) + 3 + 4, 4)
        return remote(gacc.at[j], gz.at[slot], gss.at[2 + j], grs.at[4 + slot], (me.dp, 2 * c + j))

    for j in (0, 1):
        @pl.when(z != 2 * c + j)
        def _():
            gain_z(j).start()

    def output_part(m_ref, w3):
        for copy in (load(m_in, m_ref), load(w3_in, w3)):
            copy.wait()
        for t in range(T // 256):
            swap_da(t).wait_send()

        def out_rows(row):
            rows = rows_of(row, 256)
            return dot(m_ref[0, rows, :], w3[0]) + dot(m_ref[1, rows, :], w3[1])

        for t in range(T // 256):
            es_da[pl.ds(t * 256, 256), :] = out_rows(T + t * 256).astype(BF16)
            swap_out(t).start()
            pump(1)
        for t in range(T // 256):
            rows = pl.ds(t * 256, 256)
            stage[0, rows, :] = stage[0, rows, :] + out_rows(t * 256)
            pump(1)
        for t in range(T // 256):
            swap_out(t).wait_recv()
            rows = pl.ds(t * 256, 256)
            stage[0, rows, :] = stage[0, rows, :] + er_out[rows, :].astype(F32)

    pl.run_scoped(output_part, pltpu.VMEM((2, TT, hidden), BF16), pltpu.VMEM((2, hidden, D), BF16))
    out_save = load(stage.at[0], out_out)

    def gain_final():
        return remote(gacc.at[own], gain_out, gss.at[7], grs.at[7], me.sib)

    @pl.when(innet)
    def _():
        for slot in range(3):
            remote(gz.at[slot], gz.at[slot], gss.at[2], grs.at[4 + slot], me.sib).wait_recv()
            gacc[own] += gz[slot]
        for e in range(spare):
            copy = remote(gacc.at[own], gq.at[e], gss.at[8 + e], grs.at[8 + e], other_quad(e))
            copy.start()
            copy.wait()
            gacc[own] += gq[e]
        local = pltpu.make_async_copy(gacc.at[own], gain_out, ld.at[37])
        local.start()
        gain_final().start()
        local.wait()
        gain_final().wait_send()

    pump(len(steps))

    @pl.when(jnp.logical_not(innet))
    def _():
        gain_final().wait_recv()
        for i in arrays:
            spread(i, 0)[0][2].wait_recv()
            pass_x(i)[1].wait_recv()
            pass_y(i)[1].wait_recv()
            for copy in pass_last(i):
                copy.wait_recv()

    @pl.when(innet)
    def _():
        for i in arrays:
            copies, local = spread(i, own)
            for copy in copies:
                copy.wait_send()
            local.wait()
            for copies in (pass_x(i), pass_y(i), pass_last(i)):
                for copy in copies:
                    copy.wait_send()

    for i, j in items:
        for copy in round1(i, j) + round2(i, j):
            copy.wait_send()

        @pl.when(z != 2 * c + j)
        def _():
            round_z(i, j).wait_send()

    for j in (0, 1):
        @pl.when(z != 2 * c + j)
        def _():
            gain_z(j).wait_send()

    for t in range(T // 256):
        swap_low(t).wait_send()
        swap_out(t).wait_send()
    dx_save.wait()
    out_save.wait()


def run_backward(x, kept, spare):
    T, D = x.shape
    TT = 2 * T
    w0, wo, w1, w2, w3 = kept[:5]
    wide, hidden = wo.shape[1], w1.shape[2]
    shapes = [w.shape[1:] for w in (w0, wo, w1, w2, w3)]
    q = [s[0] // 4 for s in shapes]
    h = [half_of(n) for n in q]
    cols = [s[1] for s in shapes]
    n = range(5)
    extra = max(spare, 1)
    vmem = (
        [pltpu.VMEM((2,) + s, BF16) for s in shapes]
        + [pltpu.VMEM((2, 2, h[i], cols[i]), BF16) for i in n]
        + [pltpu.VMEM((2, 2, q[i] - h[i], cols[i]), BF16) for i in n]
        + [pltpu.VMEM((2, h[i], cols[i]), BF16) for i in n]
        + [pltpu.VMEM((2, q[i] - h[i], cols[i]), BF16) for i in n]
        + [pltpu.VMEM((3, q[i], cols[i]), BF16) for i in n]
        + [
            pltpu.VMEM((T, D), F32),
            pltpu.VMEM((T, D), F32),
            pltpu.VMEM((T, D), BF16),
            pltpu.VMEM((T, D), BF16),
            pltpu.VMEM((T, D), BF16),
            pltpu.VMEM((T, D), F32),
            pltpu.VMEM((TT, D), BF16),
            pltpu.VMEM((2, 8, wide), F32),
            pltpu.VMEM((2, 8, wide), F32),
            pltpu.VMEM((2, 8, wide), F32),
            pltpu.VMEM((3, 8, wide), F32),
            pltpu.VMEM((extra, 8, wide), F32),
            pltpu.VMEM((1, T, D), F32),
        ]
    )
    dma = pltpu.SemaphoreType.DMA
    sems = [
        dma((5, 2, 4)), dma((5, 2, 4)), dma((5, 2, 2)), dma((5, 2, 2)), dma((5, 2)), dma((5, 3)),
        dma((5,)), dma((5,)), dma((5,)), dma((5,)), dma((5, 2)), dma((5, 2)), dma((5, 5)), dma((5, 5)),
        dma((5, 2 + extra)), dma((5, extra)), dma((38,)), dma((8,)), dma((8,)), dma((8 + extra,)), dma((8 + extra,)),
    ]
    outs = [((T, D), F32), ((T, D), F32)] + [(s, BF16) for s in shapes] + [((8, wide), F32)]
    if spare:
        outs += [((spare, q[i], cols[i]), BF16) for i in n]
    return pl.pallas_call(
        functools.partial(backward_kernel, shapes, spare),
        out_shape=[jax.ShapeDtypeStruct(s, t) for s, t in outs],
        in_specs=any_spec(1 + len(kept)),
        out_specs=any_spec(len(outs)),
        scratch_shapes=vmem + sems,
        compiler_params=pltpu.CompilerParams(collective_id=1, has_side_effects=True, vmem_limit_bytes=VMEM_LIMIT),
        cost_estimate=pl.CostEstimate(flops=30 * 10**9, bytes_accessed=80 * 10**6, transcendentals=10**6),
        name="backward",
    )(x, *kept)


def shards(
    inputs, w_query, w_key, w_value, w_gate, head_gain, w_out, w_first, w_second, w_third, cotangent
):
    wide = w_query.shape[1]
    weights = [w_query, w_key, w_value, w_gate, w_out, w_first, w_second, w_third]
    gain = jnp.broadcast_to(head_gain[None], (8, wide))
    kept = run_forward(inputs, cotangent, gain, weights)
    spare = (lax.axis_size("dp") // 8).bit_length() - 1
    output, grad_inputs, g_in, g_out, g_first, g_second, g_third, g_gain = run_backward(inputs, kept, spare)[:8]
    return (
        output,
        grad_inputs,
        *(g_in[:, i * wide : (i + 1) * wide].astype(F32) for i in range(4)),
        jnp.sum(g_gain, axis=0),
        *(g.astype(F32) for g in (g_out, g_first, g_second, g_third)),
    )


def solution(mesh):
    rows, columns = P(("dp", "mp"), None), P(None, "mp")
    heads = P("mp", None)
    return jax.shard_map(
        shards,
        mesh=mesh,
        in_specs=(rows, columns, columns, columns, columns, P("mp"), heads, columns, columns, heads, rows),
        out_specs=(rows, rows, columns, columns, columns, columns, P("mp"), heads, columns, columns, heads),
        check_vma=False,
    )
```

```python
import functools

import jax
import jax.numpy as jnp
from jax import lax
from jax.experimental import pallas as pl
from jax.experimental.pallas import tpu as pltpu
from jax.sharding import PartitionSpec as P

DH = 64
BLK = 64
EPSILON = 1e-06
MESH = pl.DeviceIdType.MESH
F32 = jnp.float32
BF16 = jnp.bfloat16
UNIT = 128
VMEM_LIMIT = 61 * 2**20


GATHER = (
    (0, 1, 3, 16, 17, 19,),
    (2, 18,),
    (6,),
    (),
    (32, 33, 34, 35,),
    (7,),
    (),
    (22,),
    (4, ),
    (),
    (5,),
    (38,),
    (9, ),
    (),
    (),
    (),
    (),
    (8,),
    (),
    (),
    (21, 23,),
    (24,),
    (),
    (25, 37,),
    (10, 39,),
    (40,),
    (41,),
    (26,),
    (),
    (),
    (),
    (),
    (),
    (),
    (42,),
)
LEAD = 4


def rms_factor(values):
    return lax.rsqrt(jnp.mean(values * values, axis=-1, keepdims=True) + EPSILON)


def dot(left, right):
    return jnp.dot(left, right, preferred_element_type=F32)


def dot_tn(left, right):
    return lax.dot_general(left, right, (((0,), (0,)), ((), ())), preferred_element_type=F32)


def dot_nt(left, right):
    return lax.dot_general(left, right, (((1,), (1,)), ((), ())), preferred_element_type=F32)


def remote(src, dst, send, recv, device):
    return pltpu.make_async_remote_copy(src, dst, send, recv, device_id=device, device_id_type=MESH)


def rows_of(start, count):
    return pl.ds(pl.multiple_of(start, 16), count)


class Place:
    def __init__(self):
        dp, self.z = lax.axis_index("dp"), lax.axis_index("mp")
        self.dp = dp
        self.c = dp % 2
        self.bx, self.by = (dp // 2) % 2, (dp // 4) % 2
        self.p = self.by * 2 + self.bx
        self.px, self.py = self.by * 2 + 1 - self.bx, (1 - self.by) * 2 + self.bx
        self.pd = (1 - self.by) * 2 + 1 - self.bx
        self.sib = (dp + 1 - 2 * self.c, self.z)
        self.xn = (dp + 2 - 4 * self.bx, self.z)
        self.yn = (dp + 4 - 8 * self.by, self.z)
        self.own = self.z % 2
        self.innet = self.z // 2 == self.c

    def up(self):
        return (self.dp, self.z + 1)

    def down(self):
        return (self.dp, self.z - 1)


def half_of(count):
    return (count // 2 + 15) // 16 * 16


def gather_plan(shapes):
    plan = []
    for i, (rows, _) in enumerate(shapes):
        quarter = rows // 4
        if i < 4:
            parts = [quarter]
        elif i == 4:
            parts = [rows]
        else:
            first = half_of(quarter)
            parts = [first, quarter - first]
        start = 0
        for count in parts:
            plan.append((i, max(i - 3, 0), i * shapes[0][1] if i < 4 else 0, start, count))
            start += count
    return plan


def forward_kernel(plan, shapes, *refs):
    nw = 8
    x_in, cot_in, gain_in = refs[:3]
    w_in = refs[3 : 3 + nw]
    outs = refs[3 + nw : 3 + nw + 19]
    (w_out, a_out, qkv_out, u_out, o_out, p_out, z_out, h_out, b_out, m_out, d1_out, d2_out, cot_out, gain_out, g3_out) = (
        outs[:5], *outs[5:]
    )
    scratch = refs[3 + nw + 19 :]
    bufs = scratch[:5]
    (x_ref, cot, a_ref, qkv, u_ref, o_ref, p_ref, z_ref, hs, hr, h_ref, b_ref, m_ref, d1, d2, gain, g3) = scratch[5:22]
    (zs, zr, fzs, xs, xr, ys, yr, fs, fr, loc, gs, gr, es, er, sv) = scratch[22:]
    me = Place()
    z, c, own, innet = me.z, me.c, me.own, me.innet
    T = x_in.shape[0]
    TT = 2 * T
    count = len(plan)
    wide = shapes[0][1]

    bar = pltpu.get_barrier_semaphore()
    for d in (me.sib, me.xn, me.yn):
        pl.semaphore_signal(bar, inc=1, device_id=d, device_id_type=MESH)

    @pl.when(z < 3)
    def _():
        pl.semaphore_signal(bar, inc=1, device_id=me.up(), device_id_type=MESH)

    @pl.when(z > 0)
    def _():
        pl.semaphore_signal(bar, inc=1, device_id=me.down(), device_id_type=MESH)

    pl.semaphore_wait(bar, 3 + jnp.where(z < 3, 1, 0) + jnp.where(z > 0, 1, 0))

    def z_only(k):
        return plan[k][4] == shapes[plan[k][0]][0]

    def piece(k, who):
        i, _, _, start, rows = plan[k]
        return (0 if z_only(k) else who * (shapes[i][0] // 4) + start), rows

    def part(j, k, row, rows):
        _, buf, col, _, _ = plan[k]
        ref = bufs[buf]
        if buf:
            return ref.at[j, rows_of(row, rows), :]
        return ref.at[j, rows_of(row, rows), pl.ds(col, wide)]

    def z_first(k, d):
        row, rows = piece(k, me.p)
        src = w_in[plan[k][0]].at[rows_of(row, rows), :]
        return remote(src, part(own, k, row, rows), zs.at[k, d], zr.at[k, own], (me.dp, z + 1 - 2 * d))

    def z_next(k, j, d):
        row, rows = piece(k, me.p)
        r = part(j, k, row, rows)
        return remote(r, r, fzs.at[k, j], zr.at[k, j], (me.dp, z + 1 - 2 * d))

    def to_x(k, j):
        row, rows = piece(k, me.p)
        r = part(j, k, row, rows)
        return remote(r, r, xs.at[k, j], xr.at[k, j], me.xn)

    def to_y(k, j):
        row, rows = piece(k, me.p)
        r = part(j, k, row, rows)
        return remote(r, r, ys.at[k, j], yr.at[k, j], me.yn)

    def x_then_y(k, j):
        row, rows = piece(k, me.px)
        r = part(j, k, row, half_of(rows))
        return remote(r, r, fs.at[0, k, j], fr.at[0, k, j], me.yn)

    def y_then_x(k, j):
        row, rows = piece(k, me.py)
        h = half_of(rows)
        r = part(j, k, row + h, rows - h)
        return remote(r, r, fs.at[1, k, j], fr.at[1, k, j], me.xn)

    def gain_copy(j, d, src):
        return remote(src, gain.at[j], gs.at[j, d], gr.at[j], (me.dp, z + 1 - 2 * d))

    def own_copies():
        copies = []
        for i in range(nw):
            dst = bufs[i - 3].at[own] if i > 3 else bufs[0].at[own, :, pl.ds(i * wide, wide)]
            copies.append(pltpu.make_async_copy(w_in[i], dst, loc.at[i]))
        copies.append(pltpu.make_async_copy(gain_in, gain.at[own], loc.at[nw]))
        return copies

    both = [
        remote(x_in, x_ref.at[pl.ds(T, T), :], es.at[0], er.at[0], me.sib),
        remote(cot_in, cot.at[pl.ds(T, T), :], es.at[1], er.at[1], me.sib),
    ]
    mine = [
        pltpu.make_async_copy(x_in, x_ref.at[pl.ds(0, T), :], loc.at[nw + 1]),
        pltpu.make_async_copy(cot_in, cot.at[pl.ds(0, T), :], loc.at[nw + 2]),
    ]
    mine[0].start()
    both[0].start()

    order = [code for codes in GATHER for code in codes if code < 16]

    def z_starts(k):
        @pl.when(z < 3)
        def _():
            z_first(k, 0).start()

        @pl.when(z > 0)
        def _():
            z_first(k, 1).start()

    @pl.when(innet)
    def _():
        @pl.when(z < 3)
        def _():
            gain_copy(own, 0, gain_in).start()

        @pl.when(z > 0)
        def _():
            gain_copy(own, 1, gain_in).start()

        for k in order[:LEAD]:
            z_starts(k)
        for copy in own_copies():
            copy.start()

    mine[1].start()
    both[1].start()

    def upward(j):
        return (z > 2 * c + j) & (z < 3)

    def downward(j):
        return (z < 2 * c + j) & (z > 0)

    def others(step, *args):
        for j in (0, 1):
            @pl.when(z != 2 * c + j)
            def _():
                step(*args, j)

    def step_gain(j):
        gain_copy(j, 0, gain.at[j]).wait_recv()

        @pl.when(upward(j))
        def _():
            gain_copy(j, 0, gain.at[j]).start()

        @pl.when(downward(j))
        def _():
            gain_copy(j, 1, gain.at[j]).start()

    def step_a(k, j):
        z_next(k, j, 0).wait_recv()

        @pl.when(upward(j))
        def _():
            z_next(k, j, 0).start()

        @pl.when(downward(j))
        def _():
            z_next(k, j, 1).start()

        if not z_only(k):
            to_x(k, j).start()
            to_y(k, j).start()

    def step_b(k, j):
        to_x(k, j).wait_recv()
        x_then_y(k, j).start()
        to_y(k, j).wait_recv()
        y_then_x(k, j).start()

    def step_c(k, j):
        x_then_y(k, j).wait_recv()
        y_then_x(k, j).wait_recv()

    mark = [0]

    def checkpoint():
        for code in GATHER[mark[0]]:
            others((step_a, step_b, step_c)[code // 16], code % 16)
            after = order.index(code) + LEAD if code < 16 else count
            if after < count:
                pl.when(innet)(functools.partial(z_starts, order[after]))
        mark[0] += 1

    saves = []

    def save(src, dst):
        copy = pltpu.make_async_copy(src, dst, sv.at[len(saves)])
        copy.start()
        saves.append(copy)

    checkpoint()
    mine[0].wait()
    both[0].wait_recv()
    checkpoint()

    def norm_rows(t, carry):
        rows = rows_of(t * UNIT, UNIT)
        values = x_ref[rows, :].astype(F32)
        a_ref[rows, :] = (values * rms_factor(values)).astype(BF16)
        return carry

    for n in range(2):
        lax.fori_loop(n * TT // UNIT // 2, (n + 1) * TT // UNIT // 2, norm_rows, 0)
        checkpoint()
    save(a_ref, a_out)

    @pl.when(innet)
    def _():
        for copy in own_copies():
            copy.wait()

    others(step_gain)

    lane = lax.broadcasted_iota(jnp.int32, (UNIT, UNIT), 1)
    low_half = lane < DH
    keep = [low_half.astype(F32).astype(BF16), (lane >= DH).astype(F32).astype(BF16)]
    row2 = lax.broadcasted_iota(jnp.int32, (2 * UNIT, UNIT), 0) % UNIT
    col2 = lax.broadcasted_iota(jnp.int32, (2 * UNIT, UNIT), 1)
    seen = (row2 // BLK == col2 // BLK) & (col2 <= row2)

    def attend(j):
        def project(r, carry):
            rows = rows_of(r * 256, 256)
            acc = dot(a_ref[rows, :], bufs[0][j])
            qkv[j, rows, :] = acc[:, : 3 * wide].astype(BF16)
            u_ref[j, rows, :] = acc[:, 3 * wide :]
            return carry

        lax.fori_loop(0, TT // 256, project, 0)
        checkpoint()

        def unit(t, carry):
            rows = rows_of(t * UNIT, UNIT)
            for pair in range(wide // UNIT):
                q, k, v = (qkv[j, rows, pl.ds(f * wide + pair * UNIT, UNIT)] for f in range(3))
                cols = pl.ds(pair * UNIT, UNIT)
                scores = dot_nt(jnp.concatenate([q * keep[0], q * keep[1]], axis=0), k) * DH ** (-0.5)
                scores = jnp.where(seen, scores, -1e30)
                shifted = jnp.exp(scores - jnp.max(scores, axis=-1, keepdims=True))
                soft = (shifted / jnp.sum(shifted, axis=-1, keepdims=True)).astype(BF16)
                p_ref[j, pair, t] = soft
                attended = dot(
                    jnp.concatenate([soft[:UNIT], soft[UNIT:]], axis=1),
                    jnp.concatenate([v * keep[0], v * keep[1]], axis=0),
                )
                o_ref[j, rows, cols] = attended
                square = attended * attended
                mean0 = jnp.sum(jnp.where(low_half, square, 0.0), axis=-1, keepdims=True) / DH
                mean1 = jnp.sum(jnp.where(low_half, 0.0, square), axis=-1, keepdims=True) / DH
                normed = attended * lax.rsqrt(jnp.where(low_half, mean0, mean1) + EPSILON)
                u = u_ref[j, rows, cols]
                g = gain[j, :, cols]
                z_ref[j, rows, cols] = (normed * g * (u * jax.nn.sigmoid(u))).astype(BF16)
            return carry

        span = TT // UNIT // 4
        for n in range(4):
            lax.fori_loop(n * span, n * span + span, unit, 0)
            checkpoint()

    checkpoint()
    attend(0)
    attend(1)
    checkpoint()
    for src, dst in ((qkv, qkv_out), (u_ref, u_out), (o_ref, o_out), (p_ref, p_out), (z_ref, z_out), (gain, gain_out)):
        save(src, dst)
    save(bufs[0], w_out[0])
    save(bufs[1], w_out[1])

    def out_rows(row):
        rows = rows_of(row, 256)
        return dot(z_ref[0, rows, :], bufs[1][0]) + dot(z_ref[1, rows, :], bufs[1][1])

    swaps = []
    for i in range(T // 256):
        hs[pl.ds(i * 256, 256), :] = out_rows(T + i * 256)
        part_rows = pl.ds(i * 256, 256)
        swaps.append(remote(hs.at[part_rows, :], hr.at[part_rows, :], es.at[2 + i], er.at[2 + i], me.sib))
        swaps[-1].start()
        checkpoint()
    for i in range(T // 256):
        h_ref[pl.ds(i * 256, 256), :] = x_ref[pl.ds(i * 256, 256), :].astype(F32) + out_rows(i * 256)
        checkpoint()
    checkpoint()
    for i, swap in enumerate(list(swaps)):
        swap.wait_recv()

        def add_rows(t, carry):
            rows = rows_of(i * 256 + t * UNIT, UNIT)
            values = h_ref[rows, :] + hr[rows, :]
            h_ref[rows, :] = values
            b_ref[rows, :] = (values * rms_factor(values)).astype(BF16)
            return carry

        lax.fori_loop(0, 256 // UNIT, add_rows, 0)
        b_rows = pl.ds(i * 256, 256)
        swaps.append(remote(b_ref.at[b_rows, :], b_ref.at[pl.ds(T + i * 256, 256), :], es.at[4 + i], er.at[4 + i], me.sib))
        swaps[-1].start()
        checkpoint()
    save(h_ref, h_out)
    for swap in swaps[len(swaps) // 2 :]:
        swap.wait_recv()
    save(b_ref, b_out)

    def rows_loop(body):
        lax.fori_loop(0, TT // 256, lambda r, carry: (body(rows_of(r * 256, 256)), carry)[1], 0)

    checkpoint()
    save(bufs[2], w_out[2])
    for j in (0, 1):
        def first(rows):
            d2[j, rows, :] = dot_nt(b_ref[rows, :], bufs[2][j]).astype(BF16)

        rows_loop(first)
        checkpoint()
    save(bufs[3], w_out[3])
    for j in (0, 1):
        def second(rows):
            g2 = dot_nt(b_ref[rows, :], bufs[3][j])
            d1[j, rows, :] = g2.astype(BF16)
            m_ref[j, rows, :] = (d2[j, rows, :].astype(F32) * g2).astype(BF16)

        rows_loop(second)
        checkpoint()
    for src, dst in ((m_ref, m_out), (d1, d1_out), (d2, d2_out)):
        save(src, dst)
    mine[1].wait()
    both[1].wait_recv()
    save(cot, cot_out)
    hidden = m_ref.shape[2]
    for j in (0, 1):
        for start in range(0, hidden, 256):
            size = min(256, hidden - start)
            g3[j, pl.ds(start, size), :] = dot_tn(m_ref[j, :, pl.ds(start, size)], cot[...]).astype(BF16)
            checkpoint()
    save(g3, g3_out)
    checkpoint()
    save(bufs[4], w_out[4])

    @pl.when(innet)
    def _():
        for d, inside in ((0, z < 3), (1, z > 0)):
            @pl.when(inside)
            def _():
                gain_copy(own, d, gain_in).wait_send()
                for k in range(count):
                    z_first(k, d).wait_send()

    def ends(j):
        @pl.when(upward(j) | downward(j))
        def _():
            for k in range(count):
                z_next(k, j, 0).wait_send()

        @pl.when(upward(j))
        def _():
            gain_copy(j, 0, gain.at[j]).wait_send()

        @pl.when(downward(j))
        def _():
            gain_copy(j, 1, gain.at[j]).wait_send()

        for k in range(count):
            if not z_only(k):
                for copy in (to_x, to_y, x_then_y, y_then_x):
                    copy(k, j).wait_send()

    others(ends)
    for copy in both + swaps:
        copy.wait_send()
    for copy in saves:
        copy.wait()


def any_spec(count):
    return [pl.BlockSpec(memory_space=pl.ANY)] * count


def run_forward(x, cot, gain, weights):
    T, D = x.shape
    TT = 2 * T
    shapes = [w.shape for w in weights]
    plan = gather_plan(shapes)
    wide, hidden = shapes[0][1], shapes[5][0]
    units, pairs = TT // UNIT, wide // UNIT
    buffers = [(2, D, 4 * wide), (2, wide, D), (2, hidden, D), (2, hidden, D), (2, hidden, D)]
    kept = [
        ((TT, D), BF16),
        ((2, TT, 3 * wide), BF16),
        ((2, TT, wide), F32),
        ((2, TT, wide), F32),
        ((2, pairs, units, 2 * UNIT, UNIT), BF16),
        ((2, TT, wide), BF16),
        ((T, D), F32),
        ((TT, D), BF16),
        ((2, TT, hidden), BF16),
        ((2, TT, hidden), BF16),
        ((2, TT, hidden), BF16),
        ((TT, D), BF16),
        ((2, 1, wide), F32),
        ((2, hidden, D), BF16),
    ]
    vmem = [pltpu.VMEM(s, BF16) for s in buffers] + [
        pltpu.VMEM((TT, D), BF16),
        pltpu.VMEM((TT, D), BF16),
        pltpu.VMEM((TT, D), BF16),
        pltpu.VMEM((2, TT, 3 * wide), BF16),
        pltpu.VMEM((2, TT, wide), F32),
        pltpu.VMEM((2, TT, wide), F32),
        pltpu.VMEM((2, pairs, units, 2 * UNIT, UNIT), BF16),
        pltpu.VMEM((2, TT, wide), BF16),
        pltpu.VMEM((T, D), F32),
        pltpu.VMEM((T, D), F32),
        pltpu.VMEM((T, D), F32),
        pltpu.VMEM((TT, D), BF16),
        pltpu.VMEM((2, TT, hidden), BF16),
        pltpu.VMEM((2, TT, hidden), BF16),
        pltpu.VMEM((2, TT, hidden), BF16),
        pltpu.VMEM((2, 1, wide), F32),
        pltpu.VMEM((2, hidden, D), BF16),
    ]
    n = len(plan)
    dma = pltpu.SemaphoreType.DMA
    sems = [dma((n, 2))] * 7 + [dma((2, n, 2))] * 2 + [dma((11,)), dma((2, 2)), dma((2,)), dma((6,)), dma((6,)), dma((24,))]
    return pl.pallas_call(
        functools.partial(forward_kernel, plan, shapes),
        out_shape=[jax.ShapeDtypeStruct(s, BF16) for s in buffers] + [jax.ShapeDtypeStruct(s, t) for s, t in kept],
        in_specs=any_spec(3 + len(weights)),
        out_specs=any_spec(len(buffers) + len(kept)),
        scratch_shapes=vmem + sems,
        compiler_params=pltpu.CompilerParams(collective_id=0, has_side_effects=True, vmem_limit_bytes=VMEM_LIMIT),
        cost_estimate=pl.CostEstimate(flops=16 * 10**9, bytes_accessed=80 * 10**6, transcendentals=10**6),
        name="forward",
    )(x, cot, gain, *weights)


SCHEDULE = (
    (),
    (),
    (),
    (),
    (18,),
    (),
    (),
    (19,),
    (20,),
    (),
    (),
    (),
    (),
    (35, 34,),
    (),
    (),
    (),
    (21, 36,),
    (),
    (),
    (),
    (),
    (),
    (),
    (),
    (),
    (37,),
    (),
    (),
    (),
    (),
    (27, 16, 43, 24, 32, 23, 22, 1, 26, 52, 50, 51, 40, 48, 25, 53, 39, 59, 38, 64, 17, 69, 68, 56, 67, 75, 55, 66, 33, 42, 54, 41, 83, 82, 71, 72, 58, 65, 74, 87, 84, 91, 85, 90, 80, 70, 81, 57, 73, 86, 88, 89,),
)
Z_FIRST = 1


def backward_kernel(shapes, spare, *refs):
    (x_in, w0_in, wo_in, w1_in, w2_in, w3_in, a_in, qkv_in, u_in, o_in, p_in, z_in, h_in, b_in, m_in, d1_in, d2_in) = refs[:17]
    cot_in, gain_in, g3_in = refs[17:20]
    out_out, dx_out = refs[20:22]
    final = refs[22:28]
    gain_out = refs[28]
    scratch = refs[29:]
    if spare:
        rq, scratch = scratch[:6], scratch[6:]
    gb, ra1, rb1, ra2, rb2, rz = (scratch[6 * i : 6 * i + 6] for i in range(6))
    (hs, hr, es_da, er_da, er_out, dh, dhl, gacc, gx, gy, gz, gq, gain_sent) = scratch[36:49]
    (s1, r1, s2, r2, sz, rzs, sx, rx, sy, ry, sf, rf, ss, rs, sq, rqs, ld, es, er, gss, grs) = scratch[49:]
    me = Place()
    z, c, own, innet, p = me.z, me.c, me.own, me.innet, me.p
    bx, by = me.bx, me.by
    T, D = x_in.shape
    TT = 2 * T
    wide = wo_in.shape[1]
    hidden = w1_in.shape[1]
    arrays = range(6)
    third = 5

    def other_quad(e):
        bit = 8 << e
        return (me.dp + bit - 2 * bit * ((me.dp // bit) % 2), z)

    def other_z(t):
        return (me.dp, lax.rem(z + t, 4))

    bar = pltpu.get_barrier_semaphore()
    greeted = [me.sib, me.xn, me.yn] + [other_z(t) for t in (1, 2, 3)] + [other_quad(e) for e in range(spare)]
    for d in greeted:
        pl.semaphore_signal(bar, inc=1, device_id=d, device_id_type=MESH)
    pl.semaphore_wait(bar, len(greeted))

    quarters = [s[0] // 4 for s in shapes]
    halves = [half_of(q) for q in quarters]

    def add_rows(dst, sources, rows):
        def body(t, carry):
            r = rows_of(t * 16, 16)
            total = dst[r, :].astype(F32)
            for src in sources:
                total = total + src[r, :].astype(F32)
            dst[r, :] = total.astype(BF16)
            return carry

        lax.fori_loop(0, rows // 16, body, 0)

    def z_first(i, j):
        return i == third and j == Z_FIRST

    def first_half(i, j, who):
        return gb[i].at[j, rows_of(who * quarters[i], halves[i]), :]

    def second_half(i, j, who):
        return gb[i].at[j, rows_of(who * quarters[i] + halves[i], quarters[i] - halves[i]), :]

    def whole(i, j, who):
        return gb[i].at[j, rows_of(who * quarters[i], quarters[i]), :]

    def round1(i, j):
        copies = []
        for b in (0, 1):
            copies.append(
                remote(first_half(i, j, b * 2 + 1 - bx), ra1[i].at[j, b], s1.at[i, j, b], r1.at[i, j, b], me.xn)
            )
            copies.append(
                remote(second_half(i, j, (1 - by) * 2 + b), rb1[i].at[j, b], s1.at[i, j, 2 + b], r1.at[i, j, 2 + b], me.yn)
            )
        return copies

    def round2(i, j):
        return [
            remote(first_half(i, j, (1 - by) * 2 + bx), ra2[i].at[j], s2.at[i, j, 0], r2.at[i, j, 0], me.yn),
            remote(second_half(i, j, by * 2 + 1 - bx), rb2[i].at[j], s2.at[i, j, 1], r2.at[i, j, 1], me.xn),
        ]

    def round_z(i, j):
        slot = lax.rem(z - (2 * c + j) + 3 + 4, 4)
        src = gb[i].at[j] if z_first(i, j) else whole(i, j, p)
        return remote(src, landing(i, j, slot), sz.at[i, j], rzs.at[i, slot], (me.dp, 2 * c + j))

    def landing(i, j, slot):
        if i == third and not z_first(i, j):
            return rz[i].at[slot, pl.ds(0, quarters[i]), :]
        return rz[i].at[slot]

    def landed_z(i, j, slot):
        return remote(landing(i, j, slot), landing(i, j, slot), sz.at[i, j], rzs.at[i, slot], me.sib)

    def spread(i, j):
        src = whole(i, j, p)
        dst = final[i].at[rows_of(p * quarters[i], quarters[i]), :]
        return [
            remote(src, dst, sx.at[i], rx.at[i], me.xn),
            remote(src, dst, sy.at[i], ry.at[i], me.yn),
            remote(src, dst, ss.at[i, 0], rs.at[i, 0], me.sib),
        ], pltpu.make_async_copy(src, dst, ld.at[33 + i])

    def quarter_rows(i, who, second=None):
        q, h = quarters[i], halves[i]
        if second is None:
            return final[i].at[rows_of(who * q, q), :]
        if second:
            return final[i].at[rows_of(who * q + h, q - h), :]
        return final[i].at[rows_of(who * q, h), :]

    def hand_on(i, slot, ref):
        return remote(ref, ref, ss.at[i, slot], rs.at[i, slot], me.sib)

    def pass_x(i):
        r = quarter_rows(i, me.px, False)
        return remote(r, r, sf.at[i, 0], rf.at[i, 0], me.yn), hand_on(i, 1, quarter_rows(i, me.px))

    def pass_y(i):
        r = quarter_rows(i, me.py, True)
        return remote(r, r, sf.at[i, 1], rf.at[i, 1], me.xn), hand_on(i, 2, quarter_rows(i, me.py))

    def pass_last(i):
        return hand_on(i, 3, quarter_rows(i, me.pd, False)), hand_on(i, 4, quarter_rows(i, me.pd, True))

    def step_1(i, j):
        for copy in round1(i, j):
            copy.start()

    def step_2(i, j):
        for copy in round1(i, j):
            copy.wait_recv()
        add_rows(first_half(i, j, (1 - by) * 2 + bx), [ra1[i].at[j, 1 - by]], halves[i])
        add_rows(second_half(i, j, by * 2 + 1 - bx), [rb1[i].at[j, 1 - bx]], quarters[i] - halves[i])
        for copy in round2(i, j):
            copy.start()

    def step_3(i, j):
        for copy in round2(i, j):
            copy.wait_recv()
        add_rows(first_half(i, j, p), [ra1[i].at[j, by], ra2[i].at[j]], halves[i])
        add_rows(
            second_half(i, j, p), [rb1[i].at[j, bx], rb2[i].at[j]], quarters[i] - halves[i]
        )

    def step_z(i, j):
        for slot in range(3):
            landed_z(i, j, slot).wait_recv()
        sources = [landing(i, j, slot) for slot in range(3)]
        if z_first(i, j):
            add_rows(gb[i].at[j], sources, 4 * quarters[i])
        else:
            add_rows(whole(i, j, p), sources, quarters[i])

    def step_spread(i, j):
        for e in range(spare):
            copy = remote(whole(i, j, p), rq[i].at[e], sq.at[i, e], rqs.at[i, e], other_quad(e))
            copy.start()
            copy.wait()
            h = halves[i]
            for k, (part, src) in enumerate(
                (
                    (ra2[i].at[j], rq[i].at[e, pl.ds(0, h), :]),
                    (rb2[i].at[j], rq[i].at[e, pl.ds(h, quarters[i] - h), :]),
                )
            ):
                local = pltpu.make_async_copy(src, part, sq.at[i, spare + k])
                local.start()
                local.wait()
            add_rows(first_half(i, j, p), [ra2[i].at[j]], h)
            add_rows(second_half(i, j, p), [rb2[i].at[j]], quarters[i] - h)
        copies, local = spread(i, j)
        for copy in copies:
            copy.start()
        local.start()

    def step_5(i, j):
        copies, _ = spread(i, j)
        copies[0].wait_recv()
        for copy in pass_x(i):
            copy.start()
        copies[1].wait_recv()
        for copy in pass_y(i):
            copy.start()

    def step_6(i, j):
        pass_x(i)[0].wait_recv()
        pass_y(i)[0].wait_recv()
        for copy in pass_last(i):
            copy.start()

    items = [
        (5, 0), (5, 1), (3, 0), (4, 0), (3, 1), (4, 1), (2, 0), (2, 1), (0, 0), (1, 0), (0, 1), (1, 1)
    ]

    def send(i, j):
        if z_first(i, j):
            @pl.when(z != 2 * c + j)
            def _():
                round_z(i, j).start()
        else:
            step_1(i, j)

    def step(code):
        stage, (i, j) = code // 16, items[code % 16]
        mine = z == 2 * c + j
        if not z_first(i, j) and stage == 1:
            step_2(i, j)
        elif not z_first(i, j) and stage == 2:
            step_3(i, j)

            @pl.when(jnp.logical_not(mine))
            def _():
                round_z(i, j).start()
        else:
            order = {0: (step_z, step_1), 1: (step_2,), 2: (step_3, step_spread), 3: (step_z, step_spread)}

            @pl.when(mine)
            def _():
                for part in order.get(stage, (step_5,) if stage == 4 else (step_6,)):
                    part(i, j)

    mark = [0]

    def checkpoint():
        for code in SCHEDULE[mark[0]]:
            step(code)
        mark[0] += 1

    loads = [0]

    def load(src, dst):
        copy = pltpu.make_async_copy(src, dst, ld.at[loads[0]])
        copy.start()
        loads[0] += 1
        return copy

    g3_load = load(g3_in, gb[5])

    def loop(count, body):
        lax.fori_loop(0, count, lambda t, carry: (body(t), carry)[1], 0)

    def feed_forward(b_ref, d1, d2):
        b_load, d1_load, d2_load = load(b_in, b_ref), load(d1_in, d1), load(d2_in, d2)

        def grads(w3, cot):
            copies = [load(w3_in, w3), load(cot_in, cot), b_load, d1_load, d2_load]
            g3_load.wait()
            for j in (0, 1):
                send(5, j)
            for copy in copies:
                copy.wait()
            for j in (0, 1):
                def rows_body(t):
                    rows = rows_of(t * 256, 256)
                    dm = dot_nt(cot[rows, :], w3[j])
                    d1[j, rows, :] = (dm * d1[j, rows, :].astype(F32)).astype(BF16)
                    d2[j, rows, :] = (dm * d2[j, rows, :].astype(F32)).astype(BF16)

                loop(TT // 256, rows_body)
                for i, d in ((3, d1), (4, d2)):
                    for start in range(0, hidden, 256):
                        size = min(256, hidden - start)
                        gb[i][j, pl.ds(start, size), :] = dot_tn(d[j, :, pl.ds(start, size)], b_ref[...]).astype(BF16)
                    send(i, j)
                    checkpoint()

        pl.run_scoped(grads, pltpu.VMEM((2, hidden, D), BF16), pltpu.VMEM((TT, D), BF16))

        def first_two(w1, w2):
            for copy in (load(w1_in, w1), load(w2_in, w2)):
                copy.wait()

            def db_rows(row):
                rows = rows_of(row, 256)
                total = dot(d1[0, rows, :], w1[0]) + dot(d2[0, rows, :], w2[0])
                return total + dot(d1[1, rows, :], w1[1]) + dot(d2[1, rows, :], w2[1])

            for t in range(T // 256):
                part = pl.ds(t * 256, 256)
                hs[part, :] = db_rows(T + t * 256)
                swap(t).start()
                checkpoint()
            for t in range(T // 256):
                dh[pl.ds(t * 256, 256), :] = db_rows(t * 256)
                checkpoint()

        pl.run_scoped(first_two, pltpu.VMEM((2, hidden, D), BF16), pltpu.VMEM((2, hidden, D), BF16))

    def swap(t):
        part = pl.ds(t * 256, 256)
        return remote(hs.at[part, :], hr.at[part, :], es.at[t], er.at[t], me.sib)

    def swap_low(t):
        part = pl.ds(t * 256, 256)
        return remote(dhl.at[part, :], dhl.at[pl.ds(T + t * 256, 256), :], es.at[2 + t], er.at[2 + t], me.sib)

    def swap_da(t):
        part = pl.ds(t * 256, 256)
        return remote(es_da.at[part, :], er_da.at[part, :], es.at[4 + t], er.at[4 + t], me.sib)

    def swap_out(t):
        part = pl.ds(t * 256, 256)
        return remote(es_da.at[part, :], er_out.at[part, :], es.at[6 + t], er.at[6 + t], me.sib)

    pl.run_scoped(
        feed_forward, pltpu.VMEM((TT, D), BF16), pltpu.VMEM((2, TT, hidden), BF16), pltpu.VMEM((2, TT, hidden), BF16)
    )

    lane = lax.broadcasted_iota(jnp.int32, (UNIT, UNIT), 1)
    low_half = lane < DH
    keep = [low_half.astype(F32).astype(BF16), (lane >= DH).astype(F32).astype(BF16)]

    def stacked(values):
        return jnp.concatenate([values * keep[0], values * keep[1]], axis=0)

    def head_mean(values):
        mean0 = jnp.sum(jnp.where(low_half, values, 0.0), axis=-1, keepdims=True) / DH
        mean1 = jnp.sum(jnp.where(low_half, 0.0, values), axis=-1, keepdims=True) / DH
        return jnp.where(low_half, mean0, mean1)

    def attention(dproj, a_ref):
        a_load = load(a_in, a_ref)

        def inner(qkv, u_ref, o_ref, p_ref, wo, gain):
            copies = [
                load(src, dst)
                for src, dst in (
                    (wo_in, wo), (u_in, u_ref), (o_in, o_ref), (p_in, p_ref), (qkv_in, qkv), (gain_in, gain)
                )
            ]
            pl.run_scoped(hidden_grads, pltpu.VMEM((T, D), F32))
            for copy in copies:
                copy.wait()
            gacc[...] = jnp.zeros_like(gacc)
            pl.run_scoped(out_grads, pltpu.VMEM((2, TT, wide), BF16))
            pl.run_scoped(functools.partial(heads, qkv, u_ref, o_ref, p_ref, wo, gain), pltpu.VMEM((TT, wide), F32))

        def hidden_grads(h_ref):
            for copy in (load(h_in, h_ref), load(cot_in.at[pl.ds(0, T), :], es_da)):
                copy.wait()
            for t in range(T // 256):
                swap(t).wait_recv()

                def rows_body(r):
                    rows = rows_of(t * 256 + r * 64, 64)
                    db = dh[rows, :] + hr[rows, :]
                    h = h_ref[rows, :]
                    factor = rms_factor(h)
                    normed = h * factor
                    grad = es_da[rows, :].astype(F32) + factor * (
                        db - normed * jnp.mean(db * normed, axis=-1, keepdims=True)
                    )
                    dh[rows, :] = grad
                    dhl[rows, :] = grad.astype(BF16)

                loop(4, rows_body)
                swap_low(t).start()
                checkpoint()
        def out_grads(z_ref):
            z_load = load(z_in, z_ref)
            for t in range(T // 256):
                swap_low(t).wait_recv()
            z_load.wait()
            for j in (0, 1):
                gb[2][j] = dot_tn(z_ref[j], dhl[...]).astype(BF16)
                send(2, j)
                checkpoint()

        def heads(qkv, u_ref, o_ref, p_ref, wo, gain, dz_ref):
            for j in (0, 1):
                def dz_rows(t):
                    rows = rows_of(t * 256, 256)
                    dz_ref[rows, :] = dot_nt(dhl[rows, :], wo[j])

                loop(TT // 256, dz_rows)

                def unit(t):
                    rows = rows_of(t * UNIT, UNIT)
                    for pair in range(wide // UNIT):
                        cols = pl.ds(pair * UNIT, UNIT)
                        q, k, v = (qkv[j, rows, pl.ds(f * wide + pair * UNIT, UNIT)] for f in range(3))
                        o, u, dz = o_ref[j, rows, cols], u_ref[j, rows, cols], dz_ref[rows, cols]
                        gain_row = gain[j, :, cols]
                        factor = lax.rsqrt(head_mean(o * o) + EPSILON)
                        normed = o * factor
                        s = jax.nn.sigmoid(u)
                        act = u * s
                        dzn = dz * normed
                        gacc[j, :, cols] += jnp.sum((dzn * act).reshape(UNIT // 8, 8, UNIT), axis=0)
                        du = (dzn * gain_row * s * (1.0 + u * (1.0 - s))).astype(BF16)
                        dn = dz * act * gain_row
                        do = stacked((factor * (dn - normed * head_mean(dn * normed))).astype(BF16))
                        soft_low = p_ref[j, pair, t]
                        soft = soft_low.astype(F32)
                        dv = dot_tn(soft_low, do)
                        dp = dot_nt(do, v)
                        ds = (soft * (dp - jnp.sum(dp * soft, axis=-1, keepdims=True))).astype(BF16)
                        dq = dot(jnp.concatenate([ds[:UNIT], ds[UNIT:]], axis=1), stacked(k)) * DH ** (-0.5)
                        dk = dot_tn(ds, stacked(q)) * DH ** (-0.5)
                        for f, value in enumerate((dq, dk, dv)):
                            dproj[j, rows, pl.ds(f * wide + pair * UNIT, UNIT)] = value.astype(BF16)
                        dproj[j, rows, pl.ds(3 * wide + pair * UNIT, UNIT)] = du

                for part in range(2):
                    loop(TT // UNIT // 2, lambda t: unit(t + part * (TT // UNIT // 2)))
                    checkpoint()
                if j == 0:
                    a_load.wait()
                for i in (0, 1):
                    def block(t):
                        rows = pl.ds(pl.multiple_of(t * 256, 256), 256)
                        cols = pl.ds(i * 2 * wide, 2 * wide)
                        gb[i][j, rows, :] = dot_tn(a_ref[:, rows], dproj[j, :, cols]).astype(BF16)

                    loop(D // 256, block)
                    send(i, j)
                    checkpoint()

        pl.run_scoped(
            inner,
            pltpu.VMEM((2, TT, 3 * wide), BF16),
            pltpu.VMEM((2, TT, wide), F32),
            pltpu.VMEM((2, TT, wide), F32),
            pltpu.VMEM((2, wide // UNIT, TT // UNIT, 2 * UNIT, UNIT), BF16),
            pltpu.VMEM((2, wide, D), BF16),
            pltpu.VMEM((2, 1, wide), F32),
        )

        def inputs_part(w0, x_ref):
            for copy in (load(w0_in, w0), load(x_in, x_ref)):
                copy.wait()

            def da_rows(row):
                rows = rows_of(row, 256)
                return dot_nt(dproj[0, rows, :], w0[0]) + dot_nt(dproj[1, rows, :], w0[1])

            for t in range(T // 256):
                es_da[pl.ds(t * 256, 256), :] = da_rows(T + t * 256).astype(BF16)
                swap_da(t).start()
                checkpoint()
            for t in range(T // 256):
                hs[pl.ds(t * 256, 256), :] = da_rows(t * 256)
                checkpoint()
            for t in range(T // 256):
                swap_da(t).wait_recv()

                def rows_body(r):
                    rows = rows_of(t * 256 + r * 64, 64)
                    da = hs[rows, :] + er_da[rows, :].astype(F32)
                    x = x_ref[rows, :].astype(F32)
                    factor = rms_factor(x)
                    normed = x * factor
                    dh[rows, :] = dh[rows, :] + factor * (
                        da - normed * jnp.mean(da * normed, axis=-1, keepdims=True)
                    )

                loop(4, rows_body)
                checkpoint()

        for t in range(T // 256):
            swap(t).wait_send()
        pl.run_scoped(inputs_part, pltpu.VMEM((2, D, 4 * wide), BF16), pltpu.VMEM((T, D), BF16))

    pl.run_scoped(attention, pltpu.VMEM((2, TT, 4 * wide), BF16), pltpu.VMEM((TT, D), BF16))
    dx_save = load(dh, dx_out)

    def gain_sum(k, src, dst, device, total):
        copy = remote(src, dst, gss.at[k], grs.at[k], device)
        copy.start()
        copy.wait()
        total[...] += dst[...]

    gain_sum(0, gacc, gx, me.xn, gacc)
    checkpoint()
    gain_sum(1, gacc, gy, me.yn, gacc)

    def gain_z(j):
        slot = lax.rem(z - (2 * c + j) + 3 + 4, 4)
        return remote(gacc.at[j], gz.at[slot], gss.at[2 + j], grs.at[4 + slot], (me.dp, 2 * c + j))

    for j in (0, 1):
        @pl.when(z != 2 * c + j)
        def _():
            gain_z(j).start()

    def output_part(m_ref, w3, stage):
        for copy in (load(m_in, m_ref), load(w3_in, w3), load(h_in, stage)):
            copy.wait()
        for t in range(T // 256):
            swap_da(t).wait_send()

        def out_rows(row):
            rows = rows_of(row, 256)
            return dot(m_ref[0, rows, :], w3[0]) + dot(m_ref[1, rows, :], w3[1])

        for t in range(T // 256):
            es_da[pl.ds(t * 256, 256), :] = out_rows(T + t * 256).astype(BF16)
            swap_out(t).start()
            checkpoint()
        for t in range(T // 256):
            rows = pl.ds(t * 256, 256)
            stage[rows, :] = stage[rows, :] + out_rows(t * 256)
            checkpoint()
        for t in range(T // 256):
            swap_out(t).wait_recv()
            rows = pl.ds(t * 256, 256)
            stage[rows, :] = stage[rows, :] + er_out[rows, :].astype(F32)

        load(stage, out_out).wait()

    pl.run_scoped(
        output_part, pltpu.VMEM((2, TT, hidden), BF16), pltpu.VMEM((2, hidden, D), BF16), pltpu.VMEM((T, D), F32)
    )

    def gain_final():
        return remote(gain_sent, gain_out, gss.at[7], grs.at[7], me.sib)

    @pl.when(innet)
    def _():
        for slot in range(3):
            remote(gz.at[slot], gz.at[slot], gss.at[2], grs.at[4 + slot], me.sib).wait_recv()
            gacc[own] += gz[slot]
        for e in range(spare):
            copy = remote(gacc.at[own], gq.at[e], gss.at[8 + e], grs.at[8 + e], other_quad(e))
            copy.start()
            copy.wait()
            gacc[own] += gq[e]
        gain_sent[...] = jnp.sum(gacc[own], axis=0, keepdims=True)
        local = pltpu.make_async_copy(gain_sent, gain_out, ld.at[39])
        local.start()
        gain_final().start()
        local.wait()
        gain_final().wait_send()

    checkpoint()

    @pl.when(jnp.logical_not(innet))
    def _():
        gain_final().wait_recv()
        for i in arrays:
            spread(i, 0)[0][2].wait_recv()
            pass_x(i)[1].wait_recv()
            pass_y(i)[1].wait_recv()
            for copy in pass_last(i):
                copy.wait_recv()

    @pl.when(innet)
    def _():
        for i in arrays:
            copies, local = spread(i, own)
            for copy in copies:
                copy.wait_send()
            local.wait()
            for copies in (pass_x(i), pass_y(i), pass_last(i)):
                for copy in copies:
                    copy.wait_send()

    for i, j in items:
        def ends():
            for copy in round1(i, j) + round2(i, j):
                copy.wait_send()

        if z_first(i, j):
            pl.when(z == 2 * c + j)(ends)
        else:
            ends()

        @pl.when(z != 2 * c + j)
        def _():
            round_z(i, j).wait_send()

    for j in (0, 1):
        @pl.when(z != 2 * c + j)
        def _():
            gain_z(j).wait_send()

    for t in range(T // 256):
        swap_low(t).wait_send()
        swap_out(t).wait_send()
    dx_save.wait()


def run_backward(x, kept, spare):
    T, D = x.shape
    TT = 2 * T
    w0, wo, w1, w2, w3 = kept[:5]
    wide, hidden = wo.shape[1], w1.shape[1]
    shapes = [(D, 2 * wide), (D, 2 * wide)] + [w.shape[1:] for w in (wo, w1, w2, w3)]
    q = [s[0] // 4 for s in shapes]
    h = [half_of(n) for n in q]
    cols = [s[1] for s in shapes]
    n = range(6)
    lands = [2] * 6
    extra = max(spare, 1)
    vmem = (
        [pltpu.VMEM((2,) + s, BF16) for s in shapes]
        + [pltpu.VMEM((lands[i], 2, h[i], cols[i]), BF16) for i in n]
        + [pltpu.VMEM((lands[i], 2, q[i] - h[i], cols[i]), BF16) for i in n]
        + [pltpu.VMEM((lands[i], h[i], cols[i]), BF16) for i in n]
        + [pltpu.VMEM((lands[i], q[i] - h[i], cols[i]), BF16) for i in n]
        + [pltpu.VMEM((3, q[i] if i < 5 else 4 * q[i], cols[i]), BF16) for i in n]
        + [
            pltpu.VMEM((T, D), F32),
            pltpu.VMEM((T, D), F32),
            pltpu.VMEM((T, D), BF16),
            pltpu.VMEM((T, D), BF16),
            pltpu.VMEM((T, D), BF16),
            pltpu.VMEM((T, D), F32),
            pltpu.VMEM((TT, D), BF16),
            pltpu.VMEM((2, 8, wide), F32),
            pltpu.VMEM((2, 8, wide), F32),
            pltpu.VMEM((2, 8, wide), F32),
            pltpu.VMEM((3, 8, wide), F32),
            pltpu.VMEM((extra, 8, wide), F32),
            pltpu.VMEM((1, wide), F32),
        ]
    )
    dma = pltpu.SemaphoreType.DMA
    sems = [
        dma((6, 2, 4)), dma((6, 2, 4)), dma((6, 2, 2)), dma((6, 2, 2)), dma((6, 2)), dma((6, 3)),
        dma((6,)), dma((6,)), dma((6,)), dma((6,)), dma((6, 2)), dma((6, 2)), dma((6, 5)), dma((6, 5)),
        dma((6, 2 + extra)), dma((6, extra)), dma((40,)), dma((8,)), dma((8,)), dma((8 + extra,)), dma((8 + extra,)),
    ]
    outs = [((T, D), F32), ((T, D), F32)] + [(s, BF16) for s in shapes] + [((1, wide), F32)]
    if spare:
        outs += [((spare, q[i], cols[i]), BF16) for i in n]
    return pl.pallas_call(
        functools.partial(backward_kernel, shapes, spare),
        out_shape=[jax.ShapeDtypeStruct(s, t) for s, t in outs],
        in_specs=any_spec(1 + len(kept)),
        out_specs=any_spec(len(outs)),
        scratch_shapes=vmem + sems,
        compiler_params=pltpu.CompilerParams(collective_id=1, has_side_effects=True, vmem_limit_bytes=VMEM_LIMIT),
        cost_estimate=pl.CostEstimate(flops=30 * 10**9, bytes_accessed=80 * 10**6, transcendentals=10**6),
        name="backward",
    )(x, *kept)


def shards(
    inputs, w_query, w_key, w_value, w_gate, head_gain, w_out, w_first, w_second, w_third, cotangent
):
    wide = w_query.shape[1]
    weights = [w_query, w_key, w_value, w_gate, w_out, w_first.T, w_second.T, w_third]
    gain = head_gain.reshape(1, wide)
    kept = run_forward(inputs, cotangent, gain, weights)
    spare = (lax.axis_size("dp") // 8).bit_length() - 1
    output, grad_inputs, g_qk, g_vu, g_out, g_first, g_second, g_third, g_gain = run_backward(inputs, kept, spare)[:9]
    return (
        output,
        grad_inputs,
        *(g[:, i * wide : (i + 1) * wide].astype(F32) for g in (g_qk, g_vu) for i in range(2)),
        g_gain.reshape(wide),
        *(g.astype(F32) for g in (g_out, g_first.T, g_second.T, g_third)),
    )


def solution(mesh):
    rows, columns = P(("dp", "mp"), None), P(None, "mp")
    heads = P("mp", None)
    return jax.shard_map(
        shards,
        mesh=mesh,
        in_specs=(rows, columns, columns, columns, columns, P("mp"), heads, columns, columns, heads, rows),
        out_specs=(rows, rows, columns, columns, columns, columns, P("mp"), heads, columns, columns, heads),
        check_vma=False,
    )
```

```python
import functools

import jax
import jax.numpy as jnp
from jax import lax
from jax.experimental import pallas as pl
from jax.experimental.pallas import tpu as pltpu
from jax.sharding import PartitionSpec as P

DH = 64
BLK = 64
EPSILON = 1e-06
MESH = pl.DeviceIdType.MESH
F32 = jnp.float32
BF16 = jnp.bfloat16
UNIT = 128
VMEM_LIMIT = 61 * 2**20


GATHER = (
    (0, 1, 2, 3, 16, 18, 19, 17,),
    (32, 6, 35,),
    (),
    (),
    (33, 34,),
    (4,),
    (),
    (9,),
    (),
    (22, 5,),
    (),
    (),
    (8,),
    (7,),
    (),
    (),
    (),
    (),
    (),
    (21,),
    (24,),
    (),
    (23,),
    (38, 10, 37,),
    (25, 40,),
    (39,),
    (26,),
    (41,),
    (),
    (),
    (),
    (),
    (),
    (),
    (42,),
)
LEAD = 3


def rms_factor(values):
    return lax.rsqrt(jnp.mean(values * values, axis=-1, keepdims=True) + EPSILON)


def dot(left, right):
    return jnp.dot(left, right, preferred_element_type=F32)


def dot_tn(left, right):
    return lax.dot_general(left, right, (((0,), (0,)), ((), ())), preferred_element_type=F32)


def dot_nt(left, right):
    return lax.dot_general(left, right, (((1,), (1,)), ((), ())), preferred_element_type=F32)


def remote(src, dst, send, recv, device):
    return pltpu.make_async_remote_copy(src, dst, send, recv, device_id=device, device_id_type=MESH)


def rows_of(start, count):
    return pl.ds(pl.multiple_of(start, 16), count)


class Place:
    def __init__(self):
        dp, self.z = lax.axis_index("dp"), lax.axis_index("mp")
        self.dp = dp
        self.c = dp % 2
        self.bx, self.by = (dp // 2) % 2, (dp // 4) % 2
        self.p = self.by * 2 + self.bx
        self.px, self.py = self.by * 2 + 1 - self.bx, (1 - self.by) * 2 + self.bx
        self.pd = (1 - self.by) * 2 + 1 - self.bx
        self.sib = (dp + 1 - 2 * self.c, self.z)
        self.xn = (dp + 2 - 4 * self.bx, self.z)
        self.yn = (dp + 4 - 8 * self.by, self.z)
        self.own = self.z % 2
        self.innet = self.z // 2 == self.c

    def up(self):
        return (self.dp, self.z + 1)

    def down(self):
        return (self.dp, self.z - 1)


def half_of(count):
    return (count // 2 + 15) // 16 * 16


def gather_plan(shapes):
    plan = []
    for i, (rows, _) in enumerate(shapes):
        quarter = rows // 4
        if i < 4:
            parts = [quarter]
        elif i == 4:
            parts = [rows]
        else:
            first = half_of(quarter)
            parts = [first, quarter - first]
        start = 0
        for count in parts:
            plan.append((i, max(i - 3, 0), i * shapes[0][1] if i < 4 else 0, start, count))
            start += count
    return plan


def forward_kernel(plan, shapes, *refs):
    nw = 8
    x_in, cot_in, gain_in = refs[:3]
    w_in = refs[3 : 3 + nw]
    outs = refs[3 + nw : 3 + nw + 19]
    (w_out, a_out, qkv_out, u_out, o_out, p_out, z_out, h_out, b_out, m_out, d1_out, d2_out, cot_out, gain_out, g3_out) = (
        outs[:5], *outs[5:]
    )
    scratch = refs[3 + nw + 19 :]
    bufs = scratch[:5]
    (x_ref, cot, a_ref, qkv, u_ref, o_ref, p_ref, z_ref, hs, hr, h_ref, b_ref, m_ref, d1, d2, gain, g3) = scratch[5:22]
    (zs, zr, fzs, xs, xr, ys, yr, fs, fr, loc, gs, gr, es, er, sv) = scratch[22:]
    me = Place()
    z, c, own, innet = me.z, me.c, me.own, me.innet
    T = x_in.shape[0]
    TT = 2 * T
    count = len(plan)
    wide = shapes[0][1]

    bar = pltpu.get_barrier_semaphore()
    for d in (me.sib, me.xn, me.yn):
        pl.semaphore_signal(bar, inc=1, device_id=d, device_id_type=MESH)

    @pl.when(z < 3)
    def _():
        pl.semaphore_signal(bar, inc=1, device_id=me.up(), device_id_type=MESH)

    @pl.when(z > 0)
    def _():
        pl.semaphore_signal(bar, inc=1, device_id=me.down(), device_id_type=MESH)

    pl.semaphore_wait(bar, 3 + jnp.where(z < 3, 1, 0) + jnp.where(z > 0, 1, 0))

    def z_only(k):
        return plan[k][4] == shapes[plan[k][0]][0]

    def piece(k, who):
        i, _, _, start, rows = plan[k]
        return (0 if z_only(k) else who * (shapes[i][0] // 4) + start), rows

    def part(j, k, row, rows):
        _, buf, col, _, _ = plan[k]
        ref = bufs[buf]
        if buf:
            return ref.at[j, rows_of(row, rows), :]
        return ref.at[j, rows_of(row, rows), pl.ds(col, wide)]

    def z_first(k, d):
        row, rows = piece(k, me.p)
        src = w_in[plan[k][0]].at[rows_of(row, rows), :]
        return remote(src, part(own, k, row, rows), zs.at[k, d], zr.at[k, own], (me.dp, z + 1 - 2 * d))

    def z_next(k, j, d):
        row, rows = piece(k, me.p)
        r = part(j, k, row, rows)
        return remote(r, r, fzs.at[k, j], zr.at[k, j], (me.dp, z + 1 - 2 * d))

    def to_x(k, j):
        row, rows = piece(k, me.p)
        r = part(j, k, row, rows)
        return remote(r, r, xs.at[k, j], xr.at[k, j], me.xn)

    def to_y(k, j):
        row, rows = piece(k, me.p)
        r = part(j, k, row, rows)
        return remote(r, r, ys.at[k, j], yr.at[k, j], me.yn)

    def x_then_y(k, j):
        row, rows = piece(k, me.px)
        r = part(j, k, row, half_of(rows))
        return remote(r, r, fs.at[0, k, j], fr.at[0, k, j], me.yn)

    def y_then_x(k, j):
        row, rows = piece(k, me.py)
        h = half_of(rows)
        r = part(j, k, row + h, rows - h)
        return remote(r, r, fs.at[1, k, j], fr.at[1, k, j], me.xn)

    def gain_copy(j, d, src):
        return remote(src, gain.at[j], gs.at[j, d], gr.at[j], (me.dp, z + 1 - 2 * d))

    def own_copies():
        copies = []
        for i in range(nw):
            dst = bufs[i - 3].at[own] if i > 3 else bufs[0].at[own, :, pl.ds(i * wide, wide)]
            copies.append(pltpu.make_async_copy(w_in[i], dst, loc.at[i]))
        copies.append(pltpu.make_async_copy(gain_in, gain.at[own], loc.at[nw]))
        return copies

    both = [
        remote(x_in, x_ref.at[pl.ds(T, T), :], es.at[0], er.at[0], me.sib),
        remote(cot_in, cot.at[pl.ds(T, T), :], es.at[1], er.at[1], me.sib),
    ]
    mine = [
        pltpu.make_async_copy(x_in, x_ref.at[pl.ds(0, T), :], loc.at[nw + 1]),
        pltpu.make_async_copy(cot_in, cot.at[pl.ds(0, T), :], loc.at[nw + 2]),
    ]
    mine[0].start()
    both[0].start()

    order = [code for codes in GATHER for code in codes if code < 16]

    def z_starts(k):
        @pl.when(z < 3)
        def _():
            z_first(k, 0).start()

        @pl.when(z > 0)
        def _():
            z_first(k, 1).start()

    @pl.when(innet)
    def _():
        @pl.when(z < 3)
        def _():
            gain_copy(own, 0, gain_in).start()

        @pl.when(z > 0)
        def _():
            gain_copy(own, 1, gain_in).start()

        for k in order[:LEAD]:
            z_starts(k)
        for copy in own_copies():
            copy.start()

    mine[1].start()
    both[1].start()

    def upward(j):
        return (z > 2 * c + j) & (z < 3)

    def downward(j):
        return (z < 2 * c + j) & (z > 0)

    def others(step, *args):
        for j in (0, 1):
            @pl.when(z != 2 * c + j)
            def _():
                step(*args, j)

    def step_gain(j):
        gain_copy(j, 0, gain.at[j]).wait_recv()

        @pl.when(upward(j))
        def _():
            gain_copy(j, 0, gain.at[j]).start()

        @pl.when(downward(j))
        def _():
            gain_copy(j, 1, gain.at[j]).start()

    def step_a(k, j):
        z_next(k, j, 0).wait_recv()

        @pl.when(upward(j))
        def _():
            z_next(k, j, 0).start()

        @pl.when(downward(j))
        def _():
            z_next(k, j, 1).start()

        if not z_only(k):
            to_x(k, j).start()
            to_y(k, j).start()

    def step_b(k, j):
        to_x(k, j).wait_recv()
        x_then_y(k, j).start()
        to_y(k, j).wait_recv()
        y_then_x(k, j).start()

    def step_c(k, j):
        x_then_y(k, j).wait_recv()
        y_then_x(k, j).wait_recv()

    mark = [0]

    def checkpoint():
        for code in GATHER[mark[0]]:
            others((step_a, step_b, step_c)[code // 16], code % 16)
            after = order.index(code) + LEAD if code < 16 else count
            if after < count:
                pl.when(innet)(functools.partial(z_starts, order[after]))
        mark[0] += 1

    saves = []

    def save(src, dst):
        copy = pltpu.make_async_copy(src, dst, sv.at[len(saves)])
        copy.start()
        saves.append(copy)

    checkpoint()
    mine[0].wait()
    both[0].wait_recv()
    checkpoint()

    def norm_rows(t, carry):
        rows = rows_of(t * UNIT, UNIT)
        values = x_ref[rows, :].astype(F32)
        a_ref[rows, :] = (values * rms_factor(values)).astype(BF16)
        return carry

    for n in range(2):
        lax.fori_loop(n * TT // UNIT // 2, (n + 1) * TT // UNIT // 2, norm_rows, 0)
        checkpoint()
    save(a_ref, a_out)

    @pl.when(innet)
    def _():
        for copy in own_copies():
            copy.wait()

    others(step_gain)

    lane = lax.broadcasted_iota(jnp.int32, (UNIT, UNIT), 1)
    low_half = lane < DH
    keep = [low_half.astype(F32).astype(BF16), (lane >= DH).astype(F32).astype(BF16)]
    row2 = lax.broadcasted_iota(jnp.int32, (2 * UNIT, UNIT), 0) % UNIT
    col2 = lax.broadcasted_iota(jnp.int32, (2 * UNIT, UNIT), 1)
    seen = (row2 // BLK == col2 // BLK) & (col2 <= row2)

    def attend(j):
        def project(r, carry):
            rows = rows_of(r * 256, 256)
            acc = dot(a_ref[rows, :], bufs[0][j])
            qkv[j, rows, :] = acc[:, : 3 * wide].astype(BF16)
            u_ref[j, rows, :] = acc[:, 3 * wide :]
            return carry

        lax.fori_loop(0, TT // 256, project, 0)
        checkpoint()

        def unit(t, carry):
            rows = rows_of(t * UNIT, UNIT)
            for pair in range(wide // UNIT):
                q, k, v = (qkv[j, rows, pl.ds(f * wide + pair * UNIT, UNIT)] for f in range(3))
                cols = pl.ds(pair * UNIT, UNIT)
                scores = dot_nt(jnp.concatenate([q * keep[0], q * keep[1]], axis=0), k) * DH ** (-0.5)
                scores = jnp.where(seen, scores, -1e30)
                shifted = jnp.exp(scores - jnp.max(scores, axis=-1, keepdims=True))
                soft = (shifted / jnp.sum(shifted, axis=-1, keepdims=True)).astype(BF16)
                p_ref[j, pair, t] = soft
                attended = dot(
                    jnp.concatenate([soft[:UNIT], soft[UNIT:]], axis=1),
                    jnp.concatenate([v * keep[0], v * keep[1]], axis=0),
                )
                o_ref[j, rows, cols] = attended
                square = attended * attended
                mean0 = jnp.sum(jnp.where(low_half, square, 0.0), axis=-1, keepdims=True) / DH
                mean1 = jnp.sum(jnp.where(low_half, 0.0, square), axis=-1, keepdims=True) / DH
                normed = attended * lax.rsqrt(jnp.where(low_half, mean0, mean1) + EPSILON)
                u = u_ref[j, rows, cols]
                g = gain[j, :, cols]
                z_ref[j, rows, cols] = (normed * g * (u * jax.nn.sigmoid(u))).astype(BF16)
            return carry

        span = TT // UNIT // 4
        for n in range(4):
            lax.fori_loop(n * span, n * span + span, unit, 0)
            checkpoint()

    checkpoint()
    attend(0)
    attend(1)
    checkpoint()
    for src, dst in ((qkv, qkv_out), (u_ref, u_out), (o_ref, o_out), (p_ref, p_out), (z_ref, z_out), (gain, gain_out)):
        save(src, dst)
    save(bufs[0], w_out[0])
    save(bufs[1], w_out[1])

    def out_rows(row):
        rows = rows_of(row, 256)
        return dot(z_ref[0, rows, :], bufs[1][0]) + dot(z_ref[1, rows, :], bufs[1][1])

    swaps = []
    for i in range(T // 256):
        hs[pl.ds(i * 256, 256), :] = out_rows(T + i * 256)
        part_rows = pl.ds(i * 256, 256)
        swaps.append(remote(hs.at[part_rows, :], hr.at[part_rows, :], es.at[2 + i], er.at[2 + i], me.sib))
        swaps[-1].start()
        checkpoint()
    for i in range(T // 256):
        h_ref[pl.ds(i * 256, 256), :] = x_ref[pl.ds(i * 256, 256), :].astype(F32) + out_rows(i * 256)
        checkpoint()
    checkpoint()
    for i, swap in enumerate(list(swaps)):
        swap.wait_recv()

        def add_rows(t, carry):
            rows = rows_of(i * 256 + t * UNIT, UNIT)
            values = h_ref[rows, :] + hr[rows, :]
            h_ref[rows, :] = values
            b_ref[rows, :] = (values * rms_factor(values)).astype(BF16)
            return carry

        lax.fori_loop(0, 256 // UNIT, add_rows, 0)
        b_rows = pl.ds(i * 256, 256)
        swaps.append(remote(b_ref.at[b_rows, :], b_ref.at[pl.ds(T + i * 256, 256), :], es.at[4 + i], er.at[4 + i], me.sib))
        swaps[-1].start()
        checkpoint()
    save(h_ref, h_out)
    for swap in swaps[len(swaps) // 2 :]:
        swap.wait_recv()
    save(b_ref, b_out)

    def rows_loop(body):
        lax.fori_loop(0, TT // 256, lambda r, carry: (body(rows_of(r * 256, 256)), carry)[1], 0)

    checkpoint()
    save(bufs[2], w_out[2])
    for j in (0, 1):
        def first(rows):
            d2[j, rows, :] = dot_nt(b_ref[rows, :], bufs[2][j]).astype(BF16)

        rows_loop(first)
        checkpoint()
    save(bufs[3], w_out[3])
    for j in (0, 1):
        def second(rows):
            g2 = dot_nt(b_ref[rows, :], bufs[3][j])
            d1[j, rows, :] = g2.astype(BF16)
            m_ref[j, rows, :] = (d2[j, rows, :].astype(F32) * g2).astype(BF16)

        rows_loop(second)
        checkpoint()
    for src, dst in ((m_ref, m_out), (d1, d1_out), (d2, d2_out)):
        save(src, dst)
    mine[1].wait()
    both[1].wait_recv()
    save(cot, cot_out)
    hidden = m_ref.shape[2]
    for j in (0, 1):
        for start in range(0, hidden, 256):
            size = min(256, hidden - start)
            g3[j, pl.ds(start, size), :] = dot_tn(m_ref[j, :, pl.ds(start, size)], cot[...]).astype(BF16)
            checkpoint()
    save(g3, g3_out)
    checkpoint()
    save(bufs[4], w_out[4])

    @pl.when(innet)
    def _():
        for d, inside in ((0, z < 3), (1, z > 0)):
            @pl.when(inside)
            def _():
                gain_copy(own, d, gain_in).wait_send()
                for k in range(count):
                    z_first(k, d).wait_send()

    def ends(j):
        @pl.when(upward(j) | downward(j))
        def _():
            for k in range(count):
                z_next(k, j, 0).wait_send()

        @pl.when(upward(j))
        def _():
            gain_copy(j, 0, gain.at[j]).wait_send()

        @pl.when(downward(j))
        def _():
            gain_copy(j, 1, gain.at[j]).wait_send()

        for k in range(count):
            if not z_only(k):
                for copy in (to_x, to_y, x_then_y, y_then_x):
                    copy(k, j).wait_send()

    others(ends)
    for copy in both + swaps:
        copy.wait_send()
    for copy in saves:
        copy.wait()


def any_spec(count):
    return [pl.BlockSpec(memory_space=pl.ANY)] * count


def run_forward(x, cot, gain, weights):
    T, D = x.shape
    TT = 2 * T
    shapes = [w.shape for w in weights]
    plan = gather_plan(shapes)
    wide, hidden = shapes[0][1], shapes[5][0]
    units, pairs = TT // UNIT, wide // UNIT
    buffers = [(2, D, 4 * wide), (2, wide, D), (2, hidden, D), (2, hidden, D), (2, hidden, D)]
    kept = [
        ((TT, D), BF16),
        ((2, TT, 3 * wide), BF16),
        ((2, TT, wide), F32),
        ((2, TT, wide), F32),
        ((2, pairs, units, 2 * UNIT, UNIT), BF16),
        ((2, TT, wide), BF16),
        ((T, D), F32),
        ((TT, D), BF16),
        ((2, TT, hidden), BF16),
        ((2, TT, hidden), BF16),
        ((2, TT, hidden), BF16),
        ((TT, D), BF16),
        ((2, 1, wide), F32),
        ((2, hidden, D), BF16),
    ]
    vmem = [pltpu.VMEM(s, BF16) for s in buffers] + [
        pltpu.VMEM((TT, D), BF16),
        pltpu.VMEM((TT, D), BF16),
        pltpu.VMEM((TT, D), BF16),
        pltpu.VMEM((2, TT, 3 * wide), BF16),
        pltpu.VMEM((2, TT, wide), F32),
        pltpu.VMEM((2, TT, wide), F32),
        pltpu.VMEM((2, pairs, units, 2 * UNIT, UNIT), BF16),
        pltpu.VMEM((2, TT, wide), BF16),
        pltpu.VMEM((T, D), F32),
        pltpu.VMEM((T, D), F32),
        pltpu.VMEM((T, D), F32),
        pltpu.VMEM((TT, D), BF16),
        pltpu.VMEM((2, TT, hidden), BF16),
        pltpu.VMEM((2, TT, hidden), BF16),
        pltpu.VMEM((2, TT, hidden), BF16),
        pltpu.VMEM((2, 1, wide), F32),
        pltpu.VMEM((2, hidden, D), BF16),
    ]
    n = len(plan)
    dma = pltpu.SemaphoreType.DMA
    sems = [dma((n, 2))] * 7 + [dma((2, n, 2))] * 2 + [dma((11,)), dma((2, 2)), dma((2,)), dma((6,)), dma((6,)), dma((24,))]
    return pl.pallas_call(
        functools.partial(forward_kernel, plan, shapes),
        out_shape=[jax.ShapeDtypeStruct(s, BF16) for s in buffers] + [jax.ShapeDtypeStruct(s, t) for s, t in kept],
        in_specs=any_spec(3 + len(weights)),
        out_specs=any_spec(len(buffers) + len(kept)),
        scratch_shapes=vmem + sems,
        compiler_params=pltpu.CompilerParams(collective_id=0, has_side_effects=True, vmem_limit_bytes=VMEM_LIMIT),
        cost_estimate=pl.CostEstimate(flops=16 * 10**9, bytes_accessed=80 * 10**6, transcendentals=10**6),
        name="forward",
    )(x, cot, gain, *weights)


SCHEDULE = (
    (),
    (),
    (),
    (),
    (),
    (),
    (),
    (),
    (16,),
    (18,),
    (),
    (),
    (20,),
    (),
    (19, 21,),
    (32,),
    (34,),
    (36,),
    (24,),
    (),
    (),
    (),
    (),
    (),
    (),
    (35,),
    (37,),
    (),
    (22,),
    (),
    (),
    (1, 25, 40, 26, 38, 52, 53, 23, 27, 42, 17, 50, 69, 39, 51, 41, 68, 54, 58, 48, 85, 33, 56, 55, 67, 43, 66, 57, 59, 72, 84, 74, 65, 70, 71, 73, 83, 86, 75, 81, 90, 64, 89, 88, 87, 91, 80, 82,),
)
Z_FIRST = 1


def backward_kernel(shapes, spare, *refs):
    (x_in, w0_in, wo_in, w1_in, w2_in, w3_in, a_in, qkv_in, u_in, o_in, p_in, z_in, h_in, b_in, m_in, d1_in, d2_in) = refs[:17]
    cot_in, gain_in, g3_in = refs[17:20]
    out_out, dx_out = refs[20:22]
    final = refs[22:28]
    gain_out = refs[28]
    scratch = refs[29:]
    if spare:
        rq, scratch = scratch[:6], scratch[6:]
    gb, ra1, rb1, ra2, rb2, rz = (scratch[6 * i : 6 * i + 6] for i in range(6))
    (hs, hr, es_da, er_da, er_out, dh, dhl, gacc, gx, gy, gz, gq, gain_sent) = scratch[36:49]
    (s1, r1, s2, r2, sz, rzs, sx, rx, sy, ry, sf, rf, ss, rs, sq, rqs, ld, es, er, gss, grs) = scratch[49:]
    me = Place()
    z, c, own, innet, p = me.z, me.c, me.own, me.innet, me.p
    bx, by = me.bx, me.by
    T, D = x_in.shape
    TT = 2 * T
    wide = wo_in.shape[1]
    hidden = w1_in.shape[1]
    arrays = range(6)
    third = 5

    def other_quad(e):
        bit = 8 << e
        return (me.dp + bit - 2 * bit * ((me.dp // bit) % 2), z)

    def other_z(t):
        return (me.dp, lax.rem(z + t, 4))

    bar = pltpu.get_barrier_semaphore()
    greeted = [me.sib, me.xn, me.yn] + [other_z(t) for t in (1, 2, 3)] + [other_quad(e) for e in range(spare)]
    for d in greeted:
        pl.semaphore_signal(bar, inc=1, device_id=d, device_id_type=MESH)
    pl.semaphore_wait(bar, len(greeted))

    quarters = [s[0] // 4 for s in shapes]
    halves = [half_of(q) for q in quarters]

    def add_rows(dst, sources, rows):
        def body(t, carry):
            r = rows_of(t * 16, 16)
            total = dst[r, :].astype(F32)
            for src in sources:
                total = total + src[r, :].astype(F32)
            dst[r, :] = total.astype(BF16)
            return carry

        lax.fori_loop(0, rows // 16, body, 0)

    def z_first(i, j):
        return i == third and j == Z_FIRST

    def first_half(i, j, who):
        return gb[i].at[j, rows_of(who * quarters[i], halves[i]), :]

    def second_half(i, j, who):
        return gb[i].at[j, rows_of(who * quarters[i] + halves[i], quarters[i] - halves[i]), :]

    def whole(i, j, who):
        return gb[i].at[j, rows_of(who * quarters[i], quarters[i]), :]

    def round1(i, j):
        copies = []
        for b in (0, 1):
            copies.append(
                remote(first_half(i, j, b * 2 + 1 - bx), ra1[i].at[j, b], s1.at[i, j, b], r1.at[i, j, b], me.xn)
            )
            copies.append(
                remote(second_half(i, j, (1 - by) * 2 + b), rb1[i].at[j, b], s1.at[i, j, 2 + b], r1.at[i, j, 2 + b], me.yn)
            )
        return copies

    def round2(i, j):
        return [
            remote(first_half(i, j, (1 - by) * 2 + bx), ra2[i].at[j], s2.at[i, j, 0], r2.at[i, j, 0], me.yn),
            remote(second_half(i, j, by * 2 + 1 - bx), rb2[i].at[j], s2.at[i, j, 1], r2.at[i, j, 1], me.xn),
        ]

    def round_z(i, j):
        slot = lax.rem(z - (2 * c + j) + 3 + 4, 4)
        src = gb[i].at[j] if z_first(i, j) else whole(i, j, p)
        return remote(src, landing(i, j, slot), sz.at[i, j], rzs.at[i, slot], (me.dp, 2 * c + j))

    def landing(i, j, slot):
        if i == third and not z_first(i, j):
            return rz[i].at[slot, pl.ds(0, quarters[i]), :]
        return rz[i].at[slot]

    def landed_z(i, j, slot):
        return remote(landing(i, j, slot), landing(i, j, slot), sz.at[i, j], rzs.at[i, slot], me.sib)

    def spread(i, j):
        src = whole(i, j, p)
        dst = final[i].at[rows_of(p * quarters[i], quarters[i]), :]
        return [
            remote(src, dst, sx.at[i], rx.at[i], me.xn),
            remote(src, dst, sy.at[i], ry.at[i], me.yn),
            remote(src, dst, ss.at[i, 0], rs.at[i, 0], me.sib),
        ], pltpu.make_async_copy(src, dst, ld.at[33 + i])

    def quarter_rows(i, who, second=None):
        q, h = quarters[i], halves[i]
        if second is None:
            return final[i].at[rows_of(who * q, q), :]
        if second:
            return final[i].at[rows_of(who * q + h, q - h), :]
        return final[i].at[rows_of(who * q, h), :]

    def hand_on(i, slot, ref):
        return remote(ref, ref, ss.at[i, slot], rs.at[i, slot], me.sib)

    def pass_x(i):
        r = quarter_rows(i, me.px, False)
        return remote(r, r, sf.at[i, 0], rf.at[i, 0], me.yn), hand_on(i, 1, quarter_rows(i, me.px))

    def pass_y(i):
        r = quarter_rows(i, me.py, True)
        return remote(r, r, sf.at[i, 1], rf.at[i, 1], me.xn), hand_on(i, 2, quarter_rows(i, me.py))

    def pass_last(i):
        return hand_on(i, 3, quarter_rows(i, me.pd, False)), hand_on(i, 4, quarter_rows(i, me.pd, True))

    def step_1(i, j):
        for copy in round1(i, j):
            copy.start()

    def step_2(i, j):
        for copy in round1(i, j):
            copy.wait_recv()
        add_rows(first_half(i, j, (1 - by) * 2 + bx), [ra1[i].at[j, 1 - by]], halves[i])
        add_rows(second_half(i, j, by * 2 + 1 - bx), [rb1[i].at[j, 1 - bx]], quarters[i] - halves[i])
        for copy in round2(i, j):
            copy.start()

    def step_3(i, j):
        for copy in round2(i, j):
            copy.wait_recv()
        add_rows(first_half(i, j, p), [ra1[i].at[j, by], ra2[i].at[j]], halves[i])
        add_rows(
            second_half(i, j, p), [rb1[i].at[j, bx], rb2[i].at[j]], quarters[i] - halves[i]
        )

    def step_z(i, j):
        for slot in range(3):
            landed_z(i, j, slot).wait_recv()
        sources = [landing(i, j, slot) for slot in range(3)]
        if z_first(i, j):
            add_rows(gb[i].at[j], sources, 4 * quarters[i])
        else:
            add_rows(whole(i, j, p), sources, quarters[i])

    def step_spread(i, j):
        for e in range(spare):
            copy = remote(whole(i, j, p), rq[i].at[e], sq.at[i, e], rqs.at[i, e], other_quad(e))
            copy.start()
            copy.wait()
            h = halves[i]
            for k, (part, src) in enumerate(
                (
                    (ra2[i].at[j], rq[i].at[e, pl.ds(0, h), :]),
                    (rb2[i].at[j], rq[i].at[e, pl.ds(h, quarters[i] - h), :]),
                )
            ):
                local = pltpu.make_async_copy(src, part, sq.at[i, spare + k])
                local.start()
                local.wait()
            add_rows(first_half(i, j, p), [ra2[i].at[j]], h)
            add_rows(second_half(i, j, p), [rb2[i].at[j]], quarters[i] - h)
        copies, local = spread(i, j)
        for copy in copies:
            copy.start()
        local.start()

    def step_5(i, j):
        copies, _ = spread(i, j)
        copies[0].wait_recv()
        for copy in pass_x(i):
            copy.start()
        copies[1].wait_recv()
        for copy in pass_y(i):
            copy.start()

    def step_6(i, j):
        pass_x(i)[0].wait_recv()
        pass_y(i)[0].wait_recv()
        for copy in pass_last(i):
            copy.start()

    items = [
        (5, 0), (5, 1), (3, 0), (4, 0), (3, 1), (4, 1), (2, 0), (2, 1), (0, 0), (1, 0), (0, 1), (1, 1)
    ]

    def send(i, j):
        if z_first(i, j):
            @pl.when(z != 2 * c + j)
            def _():
                round_z(i, j).start()
        else:
            step_1(i, j)

    def step(code):
        stage, (i, j) = code // 16, items[code % 16]
        mine = z == 2 * c + j
        if not z_first(i, j) and stage == 1:
            step_2(i, j)
        elif not z_first(i, j) and stage == 2:
            step_3(i, j)

            @pl.when(jnp.logical_not(mine))
            def _():
                round_z(i, j).start()
        else:
            order = {0: (step_z, step_1), 1: (step_2,), 2: (step_3, step_spread), 3: (step_z, step_spread)}

            @pl.when(mine)
            def _():
                for part in order.get(stage, (step_5,) if stage == 4 else (step_6,)):
                    part(i, j)

    mark = [0]

    def checkpoint():
        for code in SCHEDULE[mark[0]]:
            step(code)
        mark[0] += 1

    loads = [0]

    def load(src, dst):
        copy = pltpu.make_async_copy(src, dst, ld.at[loads[0]])
        copy.start()
        loads[0] += 1
        return copy

    g3_load = load(g3_in, gb[5])

    def loop(count, body):
        lax.fori_loop(0, count, lambda t, carry: (body(t), carry)[1], 0)

    def feed_forward(b_ref, d1, d2):
        b_load, d1_load, d2_load = load(b_in, b_ref), load(d1_in, d1), load(d2_in, d2)

        def grads(w3, cot):
            copies = [load(w3_in, w3), load(cot_in, cot), b_load, d1_load, d2_load]
            g3_load.wait()
            for j in (0, 1):
                send(5, j)
            for copy in copies:
                copy.wait()
            for j in (0, 1):
                def rows_body(t):
                    rows = rows_of(t * 256, 256)
                    dm = dot_nt(cot[rows, :], w3[j])
                    d1[j, rows, :] = (dm * d1[j, rows, :].astype(F32)).astype(BF16)
                    d2[j, rows, :] = (dm * d2[j, rows, :].astype(F32)).astype(BF16)

                loop(TT // 256, rows_body)
                for i, d in ((3, d1), (4, d2)):
                    for start in range(0, hidden, 256):
                        size = min(256, hidden - start)
                        gb[i][j, pl.ds(start, size), :] = dot_tn(d[j, :, pl.ds(start, size)], b_ref[...]).astype(BF16)
                    send(i, j)
                    checkpoint()

        pl.run_scoped(grads, pltpu.VMEM((2, hidden, D), BF16), pltpu.VMEM((TT, D), BF16))

        def first_two(w1, w2):
            for copy in (load(w1_in, w1), load(w2_in, w2)):
                copy.wait()

            def db_rows(row):
                rows = rows_of(row, 256)
                total = dot(d1[0, rows, :], w1[0]) + dot(d2[0, rows, :], w2[0])
                return total + dot(d1[1, rows, :], w1[1]) + dot(d2[1, rows, :], w2[1])

            for t in range(T // 256):
                part = pl.ds(t * 256, 256)
                hs[part, :] = db_rows(T + t * 256)
                swap(t).start()
                checkpoint()
            for t in range(T // 256):
                dh[pl.ds(t * 256, 256), :] = db_rows(t * 256)
                checkpoint()

        pl.run_scoped(first_two, pltpu.VMEM((2, hidden, D), BF16), pltpu.VMEM((2, hidden, D), BF16))

    def swap(t):
        part = pl.ds(t * 256, 256)
        return remote(hs.at[part, :], hr.at[part, :], es.at[t], er.at[t], me.sib)

    def swap_low(t):
        part = pl.ds(t * 256, 256)
        return remote(dhl.at[part, :], dhl.at[pl.ds(T + t * 256, 256), :], es.at[2 + t], er.at[2 + t], me.sib)

    def swap_da(t):
        part = pl.ds(t * 256, 256)
        return remote(es_da.at[part, :], er_da.at[part, :], es.at[4 + t], er.at[4 + t], me.sib)

    def swap_out(t):
        part = pl.ds(t * 256, 256)
        return remote(es_da.at[part, :], er_out.at[part, :], es.at[6 + t], er.at[6 + t], me.sib)

    pl.run_scoped(
        feed_forward, pltpu.VMEM((TT, D), BF16), pltpu.VMEM((2, TT, hidden), BF16), pltpu.VMEM((2, TT, hidden), BF16)
    )

    lane = lax.broadcasted_iota(jnp.int32, (UNIT, UNIT), 1)
    low_half = lane < DH
    keep = [low_half.astype(F32).astype(BF16), (lane >= DH).astype(F32).astype(BF16)]

    def stacked(values):
        return jnp.concatenate([values * keep[0], values * keep[1]], axis=0)

    def head_mean(values):
        mean0 = jnp.sum(jnp.where(low_half, values, 0.0), axis=-1, keepdims=True) / DH
        mean1 = jnp.sum(jnp.where(low_half, 0.0, values), axis=-1, keepdims=True) / DH
        return jnp.where(low_half, mean0, mean1)

    def attention(dproj, a_ref):
        a_load = load(a_in, a_ref)

        def inner(qkv, u_ref, o_ref, p_ref, wo, gain):
            copies = [
                load(src, dst)
                for src, dst in (
                    (wo_in, wo), (u_in, u_ref), (o_in, o_ref), (p_in, p_ref), (qkv_in, qkv), (gain_in, gain)
                )
            ]
            pl.run_scoped(hidden_grads, pltpu.VMEM((T, D), F32))
            for copy in copies:
                copy.wait()
            gacc[...] = jnp.zeros_like(gacc)
            pl.run_scoped(out_grads, pltpu.VMEM((2, TT, wide), BF16))
            pl.run_scoped(functools.partial(heads, qkv, u_ref, o_ref, p_ref, wo, gain), pltpu.VMEM((TT, wide), F32))

        def hidden_grads(h_ref):
            for copy in (load(h_in, h_ref), load(cot_in.at[pl.ds(0, T), :], es_da)):
                copy.wait()
            for t in range(T // 256):
                swap(t).wait_recv()

                def rows_body(r):
                    rows = rows_of(t * 256 + r * 64, 64)
                    db = dh[rows, :] + hr[rows, :]
                    h = h_ref[rows, :]
                    factor = rms_factor(h)
                    normed = h * factor
                    grad = es_da[rows, :].astype(F32) + factor * (
                        db - normed * jnp.mean(db * normed, axis=-1, keepdims=True)
                    )
                    dh[rows, :] = grad
                    dhl[rows, :] = grad.astype(BF16)

                loop(4, rows_body)
                swap_low(t).start()
                checkpoint()
        def out_grads(z_ref):
            z_load = load(z_in, z_ref)
            for t in range(T // 256):
                swap_low(t).wait_recv()
            z_load.wait()
            for j in (0, 1):
                gb[2][j] = dot_tn(z_ref[j], dhl[...]).astype(BF16)
                send(2, j)
                checkpoint()

        def heads(qkv, u_ref, o_ref, p_ref, wo, gain, dz_ref):
            for j in (0, 1):
                def dz_rows(t):
                    rows = rows_of(t * 256, 256)
                    dz_ref[rows, :] = dot_nt(dhl[rows, :], wo[j])

                loop(TT // 256, dz_rows)

                def unit(t):
                    rows = rows_of(t * UNIT, UNIT)
                    for pair in range(wide // UNIT):
                        cols = pl.ds(pair * UNIT, UNIT)
                        q, k, v = (qkv[j, rows, pl.ds(f * wide + pair * UNIT, UNIT)] for f in range(3))
                        o, u, dz = o_ref[j, rows, cols], u_ref[j, rows, cols], dz_ref[rows, cols]
                        gain_row = gain[j, :, cols]
                        factor = lax.rsqrt(head_mean(o * o) + EPSILON)
                        normed = o * factor
                        s = jax.nn.sigmoid(u)
                        act = u * s
                        dzn = dz * normed
                        gacc[j, :, cols] += jnp.sum((dzn * act).reshape(UNIT // 8, 8, UNIT), axis=0)
                        du = (dzn * gain_row * s * (1.0 + u * (1.0 - s))).astype(BF16)
                        dn = dz * act * gain_row
                        do = stacked((factor * (dn - normed * head_mean(dn * normed))).astype(BF16))
                        soft_low = p_ref[j, pair, t]
                        soft = soft_low.astype(F32)
                        dv = dot_tn(soft_low, do)
                        dp = dot_nt(do, v)
                        ds = (soft * (dp - jnp.sum(dp * soft, axis=-1, keepdims=True))).astype(BF16)
                        dq = dot(jnp.concatenate([ds[:UNIT], ds[UNIT:]], axis=1), stacked(k)) * DH ** (-0.5)
                        dk = dot_tn(ds, stacked(q)) * DH ** (-0.5)
                        for f, value in enumerate((dq, dk, dv)):
                            dproj[j, rows, pl.ds(f * wide + pair * UNIT, UNIT)] = value.astype(BF16)
                        dproj[j, rows, pl.ds(3 * wide + pair * UNIT, UNIT)] = du

                for part in range(2):
                    loop(TT // UNIT // 2, lambda t: unit(t + part * (TT // UNIT // 2)))
                    checkpoint()
                if j == 0:
                    a_load.wait()
                for i in (0, 1):
                    def block(t):
                        rows = pl.ds(pl.multiple_of(t * 256, 256), 256)
                        cols = pl.ds(i * 2 * wide, 2 * wide)
                        gb[i][j, rows, :] = dot_tn(a_ref[:, rows], dproj[j, :, cols]).astype(BF16)

                    loop(D // 256, block)
                    send(i, j)
                    checkpoint()

        pl.run_scoped(
            inner,
            pltpu.VMEM((2, TT, 3 * wide), BF16),
            pltpu.VMEM((2, TT, wide), F32),
            pltpu.VMEM((2, TT, wide), F32),
            pltpu.VMEM((2, wide // UNIT, TT // UNIT, 2 * UNIT, UNIT), BF16),
            pltpu.VMEM((2, wide, D), BF16),
            pltpu.VMEM((2, 1, wide), F32),
        )

        def inputs_part(w0, x_ref):
            for copy in (load(w0_in, w0), load(x_in, x_ref)):
                copy.wait()

            def da_rows(row):
                rows = rows_of(row, 256)
                return dot_nt(dproj[0, rows, :], w0[0]) + dot_nt(dproj[1, rows, :], w0[1])

            for t in range(T // 256):
                es_da[pl.ds(t * 256, 256), :] = da_rows(T + t * 256).astype(BF16)
                swap_da(t).start()
                checkpoint()
            for t in range(T // 256):
                hs[pl.ds(t * 256, 256), :] = da_rows(t * 256)
                checkpoint()
            for t in range(T // 256):
                swap_da(t).wait_recv()

                def rows_body(r):
                    rows = rows_of(t * 256 + r * 64, 64)
                    da = hs[rows, :] + er_da[rows, :].astype(F32)
                    x = x_ref[rows, :].astype(F32)
                    factor = rms_factor(x)
                    normed = x * factor
                    dh[rows, :] = dh[rows, :] + factor * (
                        da - normed * jnp.mean(da * normed, axis=-1, keepdims=True)
                    )

                loop(4, rows_body)
                checkpoint()

        for t in range(T // 256):
            swap(t).wait_send()
        pl.run_scoped(inputs_part, pltpu.VMEM((2, D, 4 * wide), BF16), pltpu.VMEM((T, D), BF16))

    pl.run_scoped(attention, pltpu.VMEM((2, TT, 4 * wide), BF16), pltpu.VMEM((TT, D), BF16))
    dx_save = load(dh, dx_out)

    def gain_sum(k, src, dst, device, total):
        copy = remote(src, dst, gss.at[k], grs.at[k], device)
        copy.start()
        copy.wait()
        total[...] += dst[...]

    gain_sum(0, gacc, gx, me.xn, gacc)
    checkpoint()
    gain_sum(1, gacc, gy, me.yn, gacc)

    def gain_z(j):
        slot = lax.rem(z - (2 * c + j) + 3 + 4, 4)
        return remote(gacc.at[j], gz.at[slot], gss.at[2 + j], grs.at[4 + slot], (me.dp, 2 * c + j))

    for j in (0, 1):
        @pl.when(z != 2 * c + j)
        def _():
            gain_z(j).start()

    def output_part(m_ref, w3, stage):
        for copy in (load(m_in, m_ref), load(w3_in, w3), load(h_in, stage)):
            copy.wait()
        for t in range(T // 256):
            swap_da(t).wait_send()

        def out_rows(row):
            rows = rows_of(row, 256)
            return dot(m_ref[0, rows, :], w3[0]) + dot(m_ref[1, rows, :], w3[1])

        for t in range(T // 256):
            es_da[pl.ds(t * 256, 256), :] = out_rows(T + t * 256).astype(BF16)
            swap_out(t).start()
            checkpoint()
        for t in range(T // 256):
            rows = pl.ds(t * 256, 256)
            stage[rows, :] = stage[rows, :] + out_rows(t * 256)
            checkpoint()
        for t in range(T // 256):
            swap_out(t).wait_recv()
            rows = pl.ds(t * 256, 256)
            stage[rows, :] = stage[rows, :] + er_out[rows, :].astype(F32)

        load(stage, out_out).wait()

    pl.run_scoped(
        output_part, pltpu.VMEM((2, TT, hidden), BF16), pltpu.VMEM((2, hidden, D), BF16), pltpu.VMEM((T, D), F32)
    )

    def gain_final():
        return remote(gain_sent, gain_out, gss.at[7], grs.at[7], me.sib)

    @pl.when(innet)
    def _():
        for slot in range(3):
            remote(gz.at[slot], gz.at[slot], gss.at[2], grs.at[4 + slot], me.sib).wait_recv()
            gacc[own] += gz[slot]
        for e in range(spare):
            copy = remote(gacc.at[own], gq.at[e], gss.at[8 + e], grs.at[8 + e], other_quad(e))
            copy.start()
            copy.wait()
            gacc[own] += gq[e]
        gain_sent[...] = jnp.sum(gacc[own], axis=0, keepdims=True)
        local = pltpu.make_async_copy(gain_sent, gain_out, ld.at[39])
        local.start()
        gain_final().start()
        local.wait()
        gain_final().wait_send()

    checkpoint()

    @pl.when(jnp.logical_not(innet))
    def _():
        gain_final().wait_recv()
        for i in arrays:
            spread(i, 0)[0][2].wait_recv()
            pass_x(i)[1].wait_recv()
            pass_y(i)[1].wait_recv()
            for copy in pass_last(i):
                copy.wait_recv()

    @pl.when(innet)
    def _():
        for i in arrays:
            copies, local = spread(i, own)
            for copy in copies:
                copy.wait_send()
            local.wait()
            for copies in (pass_x(i), pass_y(i), pass_last(i)):
                for copy in copies:
                    copy.wait_send()

    for i, j in items:
        def ends():
            for copy in round1(i, j) + round2(i, j):
                copy.wait_send()

        if z_first(i, j):
            pl.when(z == 2 * c + j)(ends)
        else:
            ends()

        @pl.when(z != 2 * c + j)
        def _():
            round_z(i, j).wait_send()

    for j in (0, 1):
        @pl.when(z != 2 * c + j)
        def _():
            gain_z(j).wait_send()

    for t in range(T // 256):
        swap_low(t).wait_send()
        swap_out(t).wait_send()
    dx_save.wait()


def run_backward(x, kept, spare):
    T, D = x.shape
    TT = 2 * T
    w0, wo, w1, w2, w3 = kept[:5]
    wide, hidden = wo.shape[1], w1.shape[1]
    shapes = [(D, 2 * wide), (D, 2 * wide)] + [w.shape[1:] for w in (wo, w1, w2, w3)]
    q = [s[0] // 4 for s in shapes]
    h = [half_of(n) for n in q]
    cols = [s[1] for s in shapes]
    n = range(6)
    lands = [2] * 6
    extra = max(spare, 1)
    vmem = (
        [pltpu.VMEM((2,) + s, BF16) for s in shapes]
        + [pltpu.VMEM((lands[i], 2, h[i], cols[i]), BF16) for i in n]
        + [pltpu.VMEM((lands[i], 2, q[i] - h[i], cols[i]), BF16) for i in n]
        + [pltpu.VMEM((lands[i], h[i], cols[i]), BF16) for i in n]
        + [pltpu.VMEM((lands[i], q[i] - h[i], cols[i]), BF16) for i in n]
        + [pltpu.VMEM((3, q[i] if i < 5 else 4 * q[i], cols[i]), BF16) for i in n]
        + [
            pltpu.VMEM((T, D), F32),
            pltpu.VMEM((T, D), F32),
            pltpu.VMEM((T, D), BF16),
            pltpu.VMEM((T, D), BF16),
            pltpu.VMEM((T, D), BF16),
            pltpu.VMEM((T, D), F32),
            pltpu.VMEM((TT, D), BF16),
            pltpu.VMEM((2, 8, wide), F32),
            pltpu.VMEM((2, 8, wide), F32),
            pltpu.VMEM((2, 8, wide), F32),
            pltpu.VMEM((3, 8, wide), F32),
            pltpu.VMEM((extra, 8, wide), F32),
            pltpu.VMEM((1, wide), F32),
        ]
    )
    dma = pltpu.SemaphoreType.DMA
    sems = [
        dma((6, 2, 4)), dma((6, 2, 4)), dma((6, 2, 2)), dma((6, 2, 2)), dma((6, 2)), dma((6, 3)),
        dma((6,)), dma((6,)), dma((6,)), dma((6,)), dma((6, 2)), dma((6, 2)), dma((6, 5)), dma((6, 5)),
        dma((6, 2 + extra)), dma((6, extra)), dma((40,)), dma((8,)), dma((8,)), dma((8 + extra,)), dma((8 + extra,)),
    ]
    outs = [((T, D), F32), ((T, D), F32)] + [(s, BF16) for s in shapes] + [((1, wide), F32)]
    if spare:
        outs += [((spare, q[i], cols[i]), BF16) for i in n]
    return pl.pallas_call(
        functools.partial(backward_kernel, shapes, spare),
        out_shape=[jax.ShapeDtypeStruct(s, t) for s, t in outs],
        in_specs=any_spec(1 + len(kept)),
        out_specs=any_spec(len(outs)),
        scratch_shapes=vmem + sems,
        compiler_params=pltpu.CompilerParams(collective_id=1, has_side_effects=True, vmem_limit_bytes=VMEM_LIMIT),
        cost_estimate=pl.CostEstimate(flops=30 * 10**9, bytes_accessed=80 * 10**6, transcendentals=10**6),
        name="backward",
    )(x, *kept)


def finish_kernel(wide, *refs):
    ready, grads = refs[:2], refs[2:8]
    ready_out, outs = refs[8:10], refs[10:18]
    low, full = refs[18:24], refs[24:30]
    held = refs[30:32]
    sems, done = refs[32:]
    loads = [pltpu.make_async_copy(src, dst, sems.at[i]) for i, (src, dst) in enumerate(zip(grads, low))]
    for copy in loads:
        copy.start()
    moves = [pltpu.make_async_copy(src, dst, sems.at[6 + i]) for i, (src, dst) in enumerate(zip(ready, held))]
    for copy in moves:
        copy.start()
    saves = []
    for i in range(6):
        loads[i].wait()

        def widen(t, carry):
            rows = rows_of(t * 64, 64)
            full[i][rows, :] = low[i][rows, :].astype(F32)
            return carry

        lax.fori_loop(0, low[i].shape[0] // 64, widen, 0)
        if i < 2:
            parts = [(full[i].at[:, pl.ds(n * wide, wide)], outs[2 * i + n], done.at[2 * i + n]) for n in range(2)]
        else:
            parts = [(full[i], outs[2 + i], done.at[2 + i])]
        for part in parts:
            copy = pltpu.make_async_copy(*part)
            copy.start()
            saves.append(copy)
    for i in range(2):
        moves[i].wait()
        copy = pltpu.make_async_copy(held[i], ready_out[i], done.at[8 + i])
        copy.start()
        saves.append(copy)
    for copy in saves:
        copy.wait()


def run_finish(ready, grads, wide):
    shapes = [g.shape for g in grads]
    outs = [r.shape for r in ready] + [(shapes[0][0], wide)] * 4 + shapes[2:]
    return pl.pallas_call(
        functools.partial(finish_kernel, wide),
        out_shape=[jax.ShapeDtypeStruct(s, F32) for s in outs],
        in_specs=any_spec(8),
        out_specs=any_spec(len(outs)),
        scratch_shapes=[pltpu.VMEM(s, BF16) for s in shapes]
        + [pltpu.VMEM(s, F32) for s in shapes]
        + [pltpu.VMEM(r.shape, F32) for r in ready]
        + [pltpu.SemaphoreType.DMA((8,)), pltpu.SemaphoreType.DMA((10,))],
        compiler_params=pltpu.CompilerParams(vmem_limit_bytes=VMEM_LIMIT),
        cost_estimate=pl.CostEstimate(flops=0, bytes_accessed=30 * 10**6, transcendentals=0),
        name="finish",
    )(*ready, *grads)


def shards(
    inputs, w_query, w_key, w_value, w_gate, head_gain, w_out, w_first, w_second, w_third, cotangent
):
    wide = w_query.shape[1]
    weights = [w_query, w_key, w_value, w_gate, w_out, w_first.T, w_second.T, w_third]
    gain = head_gain.reshape(1, wide)
    kept = run_forward(inputs, cotangent, gain, weights)
    spare = (lax.axis_size("dp") // 8).bit_length() - 1
    results = run_backward(inputs, kept, spare)
    output, grad_inputs, *grads = run_finish(results[:2], results[2:8], wide)
    g_query, g_key, g_value, g_gate, g_out, g_first, g_second, g_third = grads
    g_gain = results[8].reshape(wide)
    return (
        output, grad_inputs, g_query, g_key, g_value, g_gate, g_gain, g_out, g_first.T, g_second.T, g_third
    )


def solution(mesh):
    rows, columns = P(("dp", "mp"), None), P(None, "mp")
    heads = P("mp", None)
    return jax.shard_map(
        shards,
        mesh=mesh,
        in_specs=(rows, columns, columns, columns, columns, P("mp"), heads, columns, columns, heads, rows),
        out_specs=(rows, rows, columns, columns, columns, columns, P("mp"), heads, columns, columns, heads),
        check_vma=False,
    )
```

```python
import functools

import jax
import jax.numpy as jnp
from jax import lax
from jax.experimental import pallas as pl
from jax.experimental.pallas import tpu as pltpu
from jax.sharding import PartitionSpec as P

DH = 64
BLK = 64
EPSILON = 1e-06
MESH = pl.DeviceIdType.MESH
F32 = jnp.float32
BF16 = jnp.bfloat16
UNIT = 128
VMEM_LIMIT = 61 * 2**20


GATHER = (
    (0, 1, 2, 3, 4, 16, 17, 18, 19,),
    (5, 33,),
    (32,),
    (),
    (34, 35,),
    (),
    (7,),
    (6,),
    (20,),
    (9,),
    (8,),
    (10,),
    (23, 22, 21,),
    (),
    (11,),
    (36,),
    (),
    (25,),
    (),
    (),
    (24, 26,),
    (),
    (),
    (38, 12, 37, 39,),
    (13, 27,),
    (42, 40, 41,),
    (28,),
    (29,),
    (),
    (),
    (),
    (),
    (43,),
    (44,),
    (45,),
)
LEAD = 3


def rms_factor(values):
    return lax.rsqrt(jnp.mean(values * values, axis=-1, keepdims=True) + EPSILON)


def dot(left, right):
    return jnp.dot(left, right, preferred_element_type=F32)


def dot_tn(left, right):
    return lax.dot_general(left, right, (((0,), (0,)), ((), ())), preferred_element_type=F32)


def dot_nt(left, right):
    return lax.dot_general(left, right, (((1,), (1,)), ((), ())), preferred_element_type=F32)


def remote(src, dst, send, recv, device):
    return pltpu.make_async_remote_copy(src, dst, send, recv, device_id=device, device_id_type=MESH)


def rows_of(start, count):
    return pl.ds(pl.multiple_of(start, 16), count)


class Place:
    def __init__(self):
        dp, self.z = lax.axis_index("dp"), lax.axis_index("mp")
        self.dp = dp
        self.c = dp % 2
        self.bx, self.by = (dp // 2) % 2, (dp // 4) % 2
        self.p = self.by * 2 + self.bx
        self.px, self.py = self.by * 2 + 1 - self.bx, (1 - self.by) * 2 + self.bx
        self.pd = (1 - self.by) * 2 + 1 - self.bx
        self.sib = (dp + 1 - 2 * self.c, self.z)
        self.xn = (dp + 2 - 4 * self.bx, self.z)
        self.yn = (dp + 4 - 8 * self.by, self.z)
        self.own = self.z % 2
        self.innet = self.z // 2 == self.c

    def up(self):
        return (self.dp, self.z + 1)

    def down(self):
        return (self.dp, self.z - 1)


def half_of(count):
    return (count // 2 + 15) // 16 * 16


def gather_plan(shapes):
    plan = []
    for i, (rows, _) in enumerate(shapes):
        quarter = rows // 4
        if i < 4:
            parts = [quarter]
        elif i == 4:
            parts = [quarter]
        else:
            third = (quarter // 3 + 15) // 16 * 16
            parts = [third, third, quarter - 2 * third]
        start = 0
        for count in parts:
            plan.append((i, max(i - 3, 0), i * shapes[0][1] if i < 4 else 0, start, count))
            start += count
    return plan


def forward_kernel(plan, shapes, *refs):
    nw = 8
    x_in, cot_in, gain_in = refs[:3]
    w_in = refs[3 : 3 + nw]
    outs = refs[3 + nw : 3 + nw + 19]
    (w_out, a_out, qkv_out, u_out, o_out, p_out, z_out, h_out, b_out, m_out, d1_out, d2_out, cot_out, gain_out, g3_out) = (
        outs[:5], *outs[5:]
    )
    scratch = refs[3 + nw + 19 :]
    bufs = scratch[:5]
    (x_ref, cot, a_ref, qkv, u_ref, o_ref, p_ref, z_ref, hs, hr, h_ref, b_ref, m_ref, d1, d2, gain, g3) = scratch[5:22]
    (zs, zr, fzs, xs, xr, ys, yr, fs, fr, loc, gs, gr, es, er, sv) = scratch[22:]
    me = Place()
    z, c, own, innet = me.z, me.c, me.own, me.innet
    T = x_in.shape[0]
    TT = 2 * T
    count = len(plan)
    wide = shapes[0][1]

    bar = pltpu.get_barrier_semaphore()
    for d in (me.sib, me.xn, me.yn):
        pl.semaphore_signal(bar, inc=1, device_id=d, device_id_type=MESH)

    @pl.when(z < 3)
    def _():
        pl.semaphore_signal(bar, inc=1, device_id=me.up(), device_id_type=MESH)

    @pl.when(z > 0)
    def _():
        pl.semaphore_signal(bar, inc=1, device_id=me.down(), device_id_type=MESH)

    pl.semaphore_wait(bar, 3 + jnp.where(z < 3, 1, 0) + jnp.where(z > 0, 1, 0))

    def z_only(k):
        return plan[k][4] == shapes[plan[k][0]][0]

    def piece(k, who):
        i, _, _, start, rows = plan[k]
        return (0 if z_only(k) else who * (shapes[i][0] // 4) + start), rows

    def part(j, k, row, rows):
        _, buf, col, _, _ = plan[k]
        ref = bufs[buf]
        if buf:
            return ref.at[j, rows_of(row, rows), :]
        return ref.at[j, rows_of(row, rows), pl.ds(col, wide)]

    def z_first(k, d):
        row, rows = piece(k, me.p)
        src = w_in[plan[k][0]].at[rows_of(row, rows), :]
        return remote(src, part(own, k, row, rows), zs.at[k, d], zr.at[k, own], (me.dp, z + 1 - 2 * d))

    def z_next(k, j, d):
        row, rows = piece(k, me.p)
        r = part(j, k, row, rows)
        return remote(r, r, fzs.at[k, j], zr.at[k, j], (me.dp, z + 1 - 2 * d))

    def to_x(k, j):
        row, rows = piece(k, me.p)
        r = part(j, k, row, rows)
        return remote(r, r, xs.at[k, j], xr.at[k, j], me.xn)

    def to_y(k, j):
        row, rows = piece(k, me.p)
        r = part(j, k, row, rows)
        return remote(r, r, ys.at[k, j], yr.at[k, j], me.yn)

    def x_then_y(k, j):
        row, rows = piece(k, me.px)
        r = part(j, k, row, half_of(rows))
        return remote(r, r, fs.at[0, k, j], fr.at[0, k, j], me.yn)

    def y_then_x(k, j):
        row, rows = piece(k, me.py)
        h = half_of(rows)
        r = part(j, k, row + h, rows - h)
        return remote(r, r, fs.at[1, k, j], fr.at[1, k, j], me.xn)

    def gain_copy(j, d, src):
        return remote(src, gain.at[j], gs.at[j, d], gr.at[j], (me.dp, z + 1 - 2 * d))

    def own_copies():
        copies = []
        for i in range(nw):
            dst = bufs[i - 3].at[own] if i > 3 else bufs[0].at[own, :, pl.ds(i * wide, wide)]
            copies.append(pltpu.make_async_copy(w_in[i], dst, loc.at[i]))
        copies.append(pltpu.make_async_copy(gain_in, gain.at[own], loc.at[nw]))
        return copies

    both = [
        remote(x_in, x_ref.at[pl.ds(T, T), :], es.at[0], er.at[0], me.sib),
        remote(cot_in, cot.at[pl.ds(T, T), :], es.at[1], er.at[1], me.sib),
    ]
    mine = [
        pltpu.make_async_copy(x_in, x_ref.at[pl.ds(0, T), :], loc.at[nw + 1]),
        pltpu.make_async_copy(cot_in, cot.at[pl.ds(0, T), :], loc.at[nw + 2]),
    ]
    mine[0].start()
    both[0].start()

    order = [code for codes in GATHER for code in codes if code < 16]

    def z_starts(k):
        @pl.when(z < 3)
        def _():
            z_first(k, 0).start()

        @pl.when(z > 0)
        def _():
            z_first(k, 1).start()

    @pl.when(innet)
    def _():
        @pl.when(z < 3)
        def _():
            gain_copy(own, 0, gain_in).start()

        @pl.when(z > 0)
        def _():
            gain_copy(own, 1, gain_in).start()

        for k in order[:LEAD]:
            z_starts(k)
        for copy in own_copies():
            copy.start()

    mine[1].start()
    both[1].start()

    def upward(j):
        return (z > 2 * c + j) & (z < 3)

    def downward(j):
        return (z < 2 * c + j) & (z > 0)

    def others(step, *args):
        for j in (0, 1):
            @pl.when(z != 2 * c + j)
            def _():
                step(*args, j)

    def step_gain(j):
        remote(gain.at[j], gain.at[j], gs.at[j, 0], gr.at[j], me.sib).wait_recv()

        @pl.when(upward(j))
        def _():
            gain_copy(j, 0, gain.at[j]).start()

        @pl.when(downward(j))
        def _():
            gain_copy(j, 1, gain.at[j]).start()

    def step_a(k, j):
        row, rows = piece(k, me.p)
        r = part(j, k, row, rows)
        remote(r, r, fzs.at[k, j], zr.at[k, j], me.sib).wait_recv()

        @pl.when(upward(j))
        def _():
            z_next(k, j, 0).start()

        @pl.when(downward(j))
        def _():
            z_next(k, j, 1).start()

        if not z_only(k):
            to_x(k, j).start()
            to_y(k, j).start()

    def step_b(k, j):
        to_x(k, j).wait_recv()
        x_then_y(k, j).start()
        to_y(k, j).wait_recv()
        y_then_x(k, j).start()

    def step_c(k, j):
        x_then_y(k, j).wait_recv()
        y_then_x(k, j).wait_recv()
        for copy in (to_x, to_y, x_then_y, y_then_x):
            copy(k, j).wait_send()

    mark = [0]

    def checkpoint():
        for code in GATHER[mark[0]]:
            others((step_a, step_b, step_c)[code // 16], code % 16)
            after = order.index(code) + LEAD if code < 16 else count
            if after < count:
                pl.when(innet)(functools.partial(z_starts, order[after]))
        mark[0] += 1

    saves = []

    def save(src, dst):
        copy = pltpu.make_async_copy(src, dst, sv.at[len(saves)])
        copy.start()
        saves.append(copy)

    checkpoint()
    mine[0].wait()
    both[0].wait_recv()
    checkpoint()

    def norm_rows(t, carry):
        rows = rows_of(t * UNIT, UNIT)
        values = x_ref[rows, :].astype(F32)
        a_ref[rows, :] = (values * rms_factor(values)).astype(BF16)
        return carry

    for n in range(2):
        lax.fori_loop(n * TT // UNIT // 2, (n + 1) * TT // UNIT // 2, norm_rows, 0)
        checkpoint()
    save(a_ref, a_out)

    @pl.when(innet)
    def _():
        for copy in own_copies():
            copy.wait()

    others(step_gain)

    lane = lax.broadcasted_iota(jnp.int32, (UNIT, UNIT), 1)
    low_half = lane < DH
    keep = [low_half.astype(F32).astype(BF16), (lane >= DH).astype(F32).astype(BF16)]
    row2 = lax.broadcasted_iota(jnp.int32, (2 * UNIT, UNIT), 0) % UNIT
    col2 = lax.broadcasted_iota(jnp.int32, (2 * UNIT, UNIT), 1)
    seen = (row2 // BLK == col2 // BLK) & (col2 <= row2)

    def attend(j):
        def project(r, carry):
            rows = rows_of(r * 256, 256)
            acc = dot(a_ref[rows, :], bufs[0][j])
            qkv[j, rows, :] = acc[:, : 3 * wide].astype(BF16)
            u_ref[j, rows, :] = acc[:, 3 * wide :]
            return carry

        lax.fori_loop(0, TT // 256, project, 0)
        checkpoint()

        def unit(t, carry):
            rows = rows_of(t * UNIT, UNIT)
            for pair in range(wide // UNIT):
                q, k, v = (qkv[j, rows, pl.ds(f * wide + pair * UNIT, UNIT)] for f in range(3))
                cols = pl.ds(pair * UNIT, UNIT)
                scores = dot_nt(jnp.concatenate([q * keep[0], q * keep[1]], axis=0), k) * DH ** (-0.5)
                scores = jnp.where(seen, scores, -1e30)
                shifted = jnp.exp(scores - jnp.max(scores, axis=-1, keepdims=True))
                soft = (shifted / jnp.sum(shifted, axis=-1, keepdims=True)).astype(BF16)
                p_ref[j, pair, t] = soft
                attended = dot(
                    jnp.concatenate([soft[:UNIT], soft[UNIT:]], axis=1),
                    jnp.concatenate([v * keep[0], v * keep[1]], axis=0),
                )
                o_ref[j, rows, cols] = attended
                square = attended * attended
                mean0 = jnp.sum(jnp.where(low_half, square, 0.0), axis=-1, keepdims=True) / DH
                mean1 = jnp.sum(jnp.where(low_half, 0.0, square), axis=-1, keepdims=True) / DH
                normed = attended * lax.rsqrt(jnp.where(low_half, mean0, mean1) + EPSILON)
                u = u_ref[j, rows, cols]
                g = gain[j, :, cols]
                z_ref[j, rows, cols] = (normed * g * (u * jax.nn.sigmoid(u))).astype(BF16)
            return carry

        span = TT // UNIT // 4
        for n in range(4):
            lax.fori_loop(n * span, n * span + span, unit, 0)
            checkpoint()

    checkpoint()
    attend(0)
    attend(1)
    checkpoint()
    for src, dst in ((qkv, qkv_out), (u_ref, u_out), (o_ref, o_out), (p_ref, p_out), (z_ref, z_out), (gain, gain_out)):
        save(src, dst)
    save(bufs[0], w_out[0])
    save(bufs[1], w_out[1])

    def out_rows(row):
        rows = rows_of(row, 256)
        return dot(z_ref[0, rows, :], bufs[1][0]) + dot(z_ref[1, rows, :], bufs[1][1])

    swaps = []
    for i in range(T // 256):
        hs[pl.ds(i * 256, 256), :] = out_rows(T + i * 256)
        part_rows = pl.ds(i * 256, 256)
        swaps.append(remote(hs.at[part_rows, :], hr.at[part_rows, :], es.at[2 + i], er.at[2 + i], me.sib))
        swaps[-1].start()
        checkpoint()
    for i in range(T // 256):
        h_ref[pl.ds(i * 256, 256), :] = x_ref[pl.ds(i * 256, 256), :].astype(F32) + out_rows(i * 256)
        checkpoint()
    checkpoint()
    for i, swap in enumerate(list(swaps)):
        swap.wait_recv()

        def add_rows(t, carry):
            rows = rows_of(i * 256 + t * UNIT, UNIT)
            values = h_ref[rows, :] + hr[rows, :]
            h_ref[rows, :] = values
            b_ref[rows, :] = (values * rms_factor(values)).astype(BF16)
            return carry

        lax.fori_loop(0, 256 // UNIT, add_rows, 0)
        b_rows = pl.ds(i * 256, 256)
        swaps.append(remote(b_ref.at[b_rows, :], b_ref.at[pl.ds(T + i * 256, 256), :], es.at[4 + i], er.at[4 + i], me.sib))
        swaps[-1].start()
        checkpoint()
    save(h_ref, h_out)
    for swap in swaps[len(swaps) // 2 :]:
        swap.wait_recv()
    save(b_ref, b_out)

    def rows_loop(body):
        lax.fori_loop(0, TT // 256, lambda r, carry: (body(rows_of(r * 256, 256)), carry)[1], 0)

    checkpoint()
    save(bufs[2], w_out[2])
    for j in (0, 1):
        def first(rows):
            d2[j, rows, :] = dot_nt(b_ref[rows, :], bufs[2][j]).astype(BF16)

        rows_loop(first)
        checkpoint()
    save(bufs[3], w_out[3])
    for j in (0, 1):
        def second(rows):
            g2 = dot_nt(b_ref[rows, :], bufs[3][j])
            d1[j, rows, :] = g2.astype(BF16)
            m_ref[j, rows, :] = (d2[j, rows, :].astype(F32) * g2).astype(BF16)

        rows_loop(second)
        checkpoint()
    for src, dst in ((m_ref, m_out), (d1, d1_out), (d2, d2_out)):
        save(src, dst)
    mine[1].wait()
    both[1].wait_recv()
    save(cot, cot_out)
    hidden = m_ref.shape[2]
    for j in (0, 1):
        for start in range(0, hidden, 256):
            size = min(256, hidden - start)
            g3[j, pl.ds(start, size), :] = dot_tn(m_ref[j, :, pl.ds(start, size)], cot[...]).astype(BF16)
            checkpoint()
    save(g3, g3_out)
    checkpoint()
    save(bufs[4], w_out[4])

    @pl.when(innet)
    def _():
        for d, inside in ((0, z < 3), (1, z > 0)):
            @pl.when(inside)
            def _():
                gain_copy(own, d, gain_in).wait_send()
                for k in range(count):
                    z_first(k, d).wait_send()

    def ends(j):
        @pl.when(upward(j) | downward(j))
        def _():
            for k in range(count):
                z_next(k, j, 0).wait_send()

        @pl.when(upward(j))
        def _():
            gain_copy(j, 0, gain.at[j]).wait_send()

        @pl.when(downward(j))
        def _():
            gain_copy(j, 1, gain.at[j]).wait_send()

    others(ends)
    for copy in both + swaps:
        copy.wait_send()
    for copy in saves:
        copy.wait()


def any_spec(count):
    return [pl.BlockSpec(memory_space=pl.ANY)] * count


def run_forward(x, cot, gain, weights):
    T, D = x.shape
    TT = 2 * T
    shapes = [w.shape for w in weights]
    plan = gather_plan(shapes)
    wide, hidden = shapes[0][1], shapes[5][0]
    units, pairs = TT // UNIT, wide // UNIT
    buffers = [(2, D, 4 * wide), (2, wide, D), (2, hidden, D), (2, hidden, D), (2, hidden, D)]
    kept = [
        ((TT, D), BF16),
        ((2, TT, 3 * wide), BF16),
        ((2, TT, wide), F32),
        ((2, TT, wide), F32),
        ((2, pairs, units, 2 * UNIT, UNIT), BF16),
        ((2, TT, wide), BF16),
        ((T, D), F32),
        ((TT, D), BF16),
        ((2, TT, hidden), BF16),
        ((2, TT, hidden), BF16),
        ((2, TT, hidden), BF16),
        ((TT, D), BF16),
        ((2, 1, wide), F32),
        ((2, hidden, D), BF16),
    ]
    vmem = [pltpu.VMEM(s, BF16) for s in buffers] + [
        pltpu.VMEM((TT, D), BF16),
        pltpu.VMEM((TT, D), BF16),
        pltpu.VMEM((TT, D), BF16),
        pltpu.VMEM((2, TT, 3 * wide), BF16),
        pltpu.VMEM((2, TT, wide), F32),
        pltpu.VMEM((2, TT, wide), F32),
        pltpu.VMEM((2, pairs, units, 2 * UNIT, UNIT), BF16),
        pltpu.VMEM((2, TT, wide), BF16),
        pltpu.VMEM((T, D), F32),
        pltpu.VMEM((T, D), F32),
        pltpu.VMEM((T, D), F32),
        pltpu.VMEM((TT, D), BF16),
        pltpu.VMEM((2, TT, hidden), BF16),
        pltpu.VMEM((2, TT, hidden), BF16),
        pltpu.VMEM((2, TT, hidden), BF16),
        pltpu.VMEM((2, 1, wide), F32),
        pltpu.VMEM((2, hidden, D), BF16),
    ]
    n = len(plan)
    dma = pltpu.SemaphoreType.DMA
    sems = [dma((n, 2))] * 7 + [dma((2, n, 2))] * 2 + [dma((11,)), dma((2, 2)), dma((2,)), dma((6,)), dma((6,)), dma((24,))]
    return pl.pallas_call(
        functools.partial(forward_kernel, plan, shapes),
        out_shape=[jax.ShapeDtypeStruct(s, BF16) for s in buffers] + [jax.ShapeDtypeStruct(s, t) for s, t in kept],
        in_specs=any_spec(3 + len(weights)),
        out_specs=any_spec(len(buffers) + len(kept)),
        scratch_shapes=vmem + sems,
        compiler_params=pltpu.CompilerParams(collective_id=0, has_side_effects=True, vmem_limit_bytes=VMEM_LIMIT),
        cost_estimate=pl.CostEstimate(flops=16 * 10**9, bytes_accessed=80 * 10**6, transcendentals=10**6),
        name="forward",
    )(x, cot, gain, *weights)


SCHEDULE = (
    (16,),
    (),
    (),
    (),
    (18,),
    (),
    (),
    (),
    (),
    (19,),
    (),
    (),
    (),
    (21,),
    (34,),
    (),
    (35, 32, 20,),
    (),
    (),
    (),
    (24,),
    (),
    (37,),
    (),
    (),
    (36,),
    (),
    (26,),
    (),
    (),
    (),
    (1, 22, 53, 40, 17, 27, 25, 48, 69, 23, 42, 38, 50, 33, 58, 51, 52, 43, 41, 64, 59, 39, 74, 66, 55, 56, 67, 68, 75, 65, 71, 80, 54, 57, 91, 85, 81, 84, 90, 87, 83, 72, 70, 73, 88, 82, 86, 89,),
)
Z_FIRST = 1


def backward_kernel(shapes, spare, *refs):
    (x_in, w0_in, wo_in, w1_in, w2_in, w3_in, a_in, qkv_in, u_in, o_in, p_in, z_in, h_in, b_in, m_in, d1_in, d2_in) = refs[:17]
    cot_in, gain_in, g3_in = refs[17:20]
    out_out, dx_out = refs[20:22]
    final = refs[22:28]
    gain_out = refs[28]
    scratch = refs[29:]
    if spare:
        rq, scratch = scratch[:6], scratch[6:]
    gb, ra1, rb1, ra2, rb2, rz = (scratch[6 * i : 6 * i + 6] for i in range(6))
    (hs, hr, es_da, er_da, er_out, dh, dhl, gacc, gx, gy, gz, gq, gain_sent) = scratch[36:49]
    (s1, r1, s2, r2, sz, rzs, sx, rx, sy, ry, sf, rf, ss, rs, sq, rqs, ld, es, er, gss, grs) = scratch[49:]
    me = Place()
    z, c, own, innet, p = me.z, me.c, me.own, me.innet, me.p
    bx, by = me.bx, me.by
    T, D = x_in.shape
    TT = 2 * T
    wide = wo_in.shape[1]
    hidden = w1_in.shape[1]
    arrays = range(6)
    third = 5

    def other_quad(e):
        bit = 8 << e
        return (me.dp + bit - 2 * bit * ((me.dp // bit) % 2), z)

    def other_z(t):
        return (me.dp, lax.rem(z + t, 4))

    bar = pltpu.get_barrier_semaphore()
    greeted = [me.sib, me.xn, me.yn] + [other_z(t) for t in (1, 2, 3)] + [other_quad(e) for e in range(spare)]
    for d in greeted:
        pl.semaphore_signal(bar, inc=1, device_id=d, device_id_type=MESH)
    pl.semaphore_wait(bar, len(greeted))

    quarters = [s[0] // 4 for s in shapes]
    halves = [half_of(q) for q in quarters]

    def add_rows(dst, sources, rows):
        def body(t, carry):
            r = rows_of(t * 16, 16)
            total = dst[r, :].astype(F32)
            for src in sources:
                total = total + src[r, :].astype(F32)
            dst[r, :] = total.astype(BF16)
            return carry

        lax.fori_loop(0, rows // 16, body, 0)

    def z_first(i, j):
        return i == third and j == Z_FIRST

    def first_half(i, j, who):
        return gb[i].at[j, rows_of(who * quarters[i], halves[i]), :]

    def second_half(i, j, who):
        return gb[i].at[j, rows_of(who * quarters[i] + halves[i], quarters[i] - halves[i]), :]

    def whole(i, j, who):
        return gb[i].at[j, rows_of(who * quarters[i], quarters[i]), :]

    def round1(i, j):
        copies = []
        for b in (0, 1):
            copies.append(
                remote(first_half(i, j, b * 2 + 1 - bx), ra1[i].at[j, b], s1.at[i, j, b], r1.at[i, j, b], me.xn)
            )
            copies.append(
                remote(second_half(i, j, (1 - by) * 2 + b), rb1[i].at[j, b], s1.at[i, j, 2 + b], r1.at[i, j, 2 + b], me.yn)
            )
        return copies

    def round2(i, j):
        return [
            remote(first_half(i, j, (1 - by) * 2 + bx), ra2[i].at[j], s2.at[i, j, 0], r2.at[i, j, 0], me.yn),
            remote(second_half(i, j, by * 2 + 1 - bx), rb2[i].at[j], s2.at[i, j, 1], r2.at[i, j, 1], me.xn),
        ]

    def round_z(i, j):
        slot = lax.rem(z - (2 * c + j) + 3 + 4, 4)
        src = gb[i].at[j] if z_first(i, j) else whole(i, j, p)
        return remote(src, landing(i, j, slot), sz.at[i, j], rzs.at[i, slot], (me.dp, 2 * c + j))

    def landing(i, j, slot):
        if i == third and not z_first(i, j):
            return rz[i].at[slot, pl.ds(0, quarters[i]), :]
        return rz[i].at[slot]

    def landed_z(i, j, slot):
        return remote(landing(i, j, slot), landing(i, j, slot), sz.at[i, j], rzs.at[i, slot], me.sib)

    def spread(i, j):
        src = whole(i, j, p)
        dst = final[i].at[rows_of(p * quarters[i], quarters[i]), :]
        return [
            remote(src, dst, sx.at[i], rx.at[i], me.xn),
            remote(src, dst, sy.at[i], ry.at[i], me.yn),
            remote(src, dst, ss.at[i, 0], rs.at[i, 0], me.sib),
        ], pltpu.make_async_copy(src, dst, ld.at[33 + i])

    def quarter_rows(i, who, second=None):
        q, h = quarters[i], halves[i]
        if second is None:
            return final[i].at[rows_of(who * q, q), :]
        if second:
            return final[i].at[rows_of(who * q + h, q - h), :]
        return final[i].at[rows_of(who * q, h), :]

    def hand_on(i, slot, ref):
        return remote(ref, ref, ss.at[i, slot], rs.at[i, slot], me.sib)

    def pass_x(i):
        r = quarter_rows(i, me.px, False)
        return remote(r, r, sf.at[i, 0], rf.at[i, 0], me.yn), hand_on(i, 1, quarter_rows(i, me.px))

    def pass_y(i):
        r = quarter_rows(i, me.py, True)
        return remote(r, r, sf.at[i, 1], rf.at[i, 1], me.xn), hand_on(i, 2, quarter_rows(i, me.py))

    def pass_last(i):
        return hand_on(i, 3, quarter_rows(i, me.pd, False)), hand_on(i, 4, quarter_rows(i, me.pd, True))

    def step_1(i, j):
        for copy in round1(i, j):
            copy.start()

    def step_2(i, j):
        for copy in round1(i, j):
            copy.wait_recv()
        add_rows(first_half(i, j, (1 - by) * 2 + bx), [ra1[i].at[j, 1 - by]], halves[i])
        add_rows(second_half(i, j, by * 2 + 1 - bx), [rb1[i].at[j, 1 - bx]], quarters[i] - halves[i])
        for copy in round2(i, j):
            copy.start()

    def step_3(i, j):
        for copy in round2(i, j):
            copy.wait_recv()
        for copy in round1(i, j):
            copy.wait_send()
        add_rows(first_half(i, j, p), [ra1[i].at[j, by], ra2[i].at[j]], halves[i])
        add_rows(
            second_half(i, j, p), [rb1[i].at[j, bx], rb2[i].at[j]], quarters[i] - halves[i]
        )

    def step_z(i, j):
        for slot in range(3):
            landed_z(i, j, slot).wait_recv()
        sources = [landing(i, j, slot) for slot in range(3)]
        if z_first(i, j):
            add_rows(gb[i].at[j], sources, 4 * quarters[i])
        else:
            add_rows(whole(i, j, p), sources, quarters[i])

    def step_spread(i, j):
        for e in range(spare):
            copy = remote(whole(i, j, p), rq[i].at[e], sq.at[i, e], rqs.at[i, e], other_quad(e))
            copy.start()
            copy.wait()
            h = halves[i]
            for k, (part, src) in enumerate(
                (
                    (ra2[i].at[j], rq[i].at[e, pl.ds(0, h), :]),
                    (rb2[i].at[j], rq[i].at[e, pl.ds(h, quarters[i] - h), :]),
                )
            ):
                local = pltpu.make_async_copy(src, part, sq.at[i, spare + k])
                local.start()
                local.wait()
            add_rows(first_half(i, j, p), [ra2[i].at[j]], h)
            add_rows(second_half(i, j, p), [rb2[i].at[j]], quarters[i] - h)
        copies, local = spread(i, j)
        for copy in copies:
            copy.start()
        local.start()

    def step_5(i, j):
        copies, _ = spread(i, j)
        copies[0].wait_recv()
        for copy in pass_x(i):
            copy.start()
        copies[1].wait_recv()
        for copy in pass_y(i):
            copy.start()

    def step_6(i, j):
        pass_x(i)[0].wait_recv()
        pass_y(i)[0].wait_recv()
        for copy in pass_last(i):
            copy.start()
        copies, local = spread(i, j)
        local.wait()
        for copy in copies + [pass_x(i)[0], pass_y(i)[0]] + round2(i, j):
            copy.wait_send()

    items = [
        (5, 0), (5, 1), (3, 0), (4, 0), (3, 1), (4, 1), (2, 0), (2, 1), (0, 0), (1, 0), (0, 1), (1, 1)
    ]

    def send(i, j):
        if z_first(i, j):
            @pl.when(z != 2 * c + j)
            def _():
                round_z(i, j).start()
        else:
            step_1(i, j)

    def step(code):
        stage, (i, j) = code // 16, items[code % 16]
        mine = z == 2 * c + j
        if not z_first(i, j) and stage == 1:
            step_2(i, j)
        elif not z_first(i, j) and stage == 2:
            step_3(i, j)

            @pl.when(jnp.logical_not(mine))
            def _():
                round_z(i, j).start()
        else:
            order = {0: (step_z, step_1), 1: (step_2,), 2: (step_3, step_spread), 3: (step_z, step_spread)}

            @pl.when(mine)
            def _():
                for part in order.get(stage, (step_5,) if stage == 4 else (step_6,)):
                    part(i, j)

            if stage == 5:
                @pl.when(jnp.logical_not(mine))
                def _():
                    round_z(i, j).wait_send()
                    if not z_first(i, j):
                        for copy in round2(i, j):
                            copy.wait_send()

    mark = [0]

    def checkpoint():
        for code in SCHEDULE[mark[0]]:
            step(code)
        mark[0] += 1

    loads = [0]

    def load(src, dst):
        copy = pltpu.make_async_copy(src, dst, ld.at[loads[0]])
        copy.start()
        loads[0] += 1
        return copy

    g3_load = load(g3_in, gb[5])

    def loop(count, body):
        lax.fori_loop(0, count, lambda t, carry: (body(t), carry)[1], 0)

    def feed_forward(b_ref, d1, d2):
        b_load, d1_load, d2_load = load(b_in, b_ref), load(d1_in, d1), load(d2_in, d2)

        def grads(w3, cot):
            copies = [load(w3_in, w3), load(cot_in, cot), b_load, d1_load, d2_load]
            g3_load.wait()
            for j in (0, 1):
                send(5, j)
            for copy in copies:
                copy.wait()
            for j in (0, 1):
                def rows_body(t):
                    rows = rows_of(t * 256, 256)
                    dm = dot_nt(cot[rows, :], w3[j])
                    d1[j, rows, :] = (dm * d1[j, rows, :].astype(F32)).astype(BF16)
                    d2[j, rows, :] = (dm * d2[j, rows, :].astype(F32)).astype(BF16)

                loop(TT // 256, rows_body)
                for i, d in ((3, d1), (4, d2)):
                    for start in range(0, hidden, 256):
                        size = min(256, hidden - start)
                        gb[i][j, pl.ds(start, size), :] = dot_tn(d[j, :, pl.ds(start, size)], b_ref[...]).astype(BF16)
                    send(i, j)
                    checkpoint()

        pl.run_scoped(grads, pltpu.VMEM((2, hidden, D), BF16), pltpu.VMEM((TT, D), BF16))

        def first_two(w1, w2):
            for copy in (load(w1_in, w1), load(w2_in, w2)):
                copy.wait()

            def db_rows(row):
                rows = rows_of(row, 256)
                total = dot(d1[0, rows, :], w1[0]) + dot(d2[0, rows, :], w2[0])
                return total + dot(d1[1, rows, :], w1[1]) + dot(d2[1, rows, :], w2[1])

            for t in range(T // 256):
                part = pl.ds(t * 256, 256)
                hs[part, :] = db_rows(T + t * 256)
                swap(t).start()
                checkpoint()
            for t in range(T // 256):
                dh[pl.ds(t * 256, 256), :] = db_rows(t * 256)
                checkpoint()

        pl.run_scoped(first_two, pltpu.VMEM((2, hidden, D), BF16), pltpu.VMEM((2, hidden, D), BF16))

    def swap(t):
        part = pl.ds(t * 256, 256)
        return remote(hs.at[part, :], hr.at[part, :], es.at[t], er.at[t], me.sib)

    def swap_low(t):
        part = pl.ds(t * 256, 256)
        return remote(dhl.at[part, :], dhl.at[pl.ds(T + t * 256, 256), :], es.at[2 + t], er.at[2 + t], me.sib)

    def swap_da(t):
        part = pl.ds(t * 256, 256)
        return remote(es_da.at[part, :], er_da.at[part, :], es.at[4 + t], er.at[4 + t], me.sib)

    def swap_out(t):
        part = pl.ds(t * 256, 256)
        return remote(es_da.at[part, :], er_out.at[part, :], es.at[6 + t], er.at[6 + t], me.sib)

    pl.run_scoped(
        feed_forward, pltpu.VMEM((TT, D), BF16), pltpu.VMEM((2, TT, hidden), BF16), pltpu.VMEM((2, TT, hidden), BF16)
    )

    lane = lax.broadcasted_iota(jnp.int32, (UNIT, UNIT), 1)
    low_half = lane < DH
    keep = [low_half.astype(F32).astype(BF16), (lane >= DH).astype(F32).astype(BF16)]

    def stacked(values):
        return jnp.concatenate([values * keep[0], values * keep[1]], axis=0)

    def head_mean(values):
        mean0 = jnp.sum(jnp.where(low_half, values, 0.0), axis=-1, keepdims=True) / DH
        mean1 = jnp.sum(jnp.where(low_half, 0.0, values), axis=-1, keepdims=True) / DH
        return jnp.where(low_half, mean0, mean1)

    def attention(dproj, a_ref):
        a_load = load(a_in, a_ref)

        def inner(qkv, u_ref, o_ref, p_ref, wo, gain):
            copies = [
                load(src, dst)
                for src, dst in (
                    (wo_in, wo), (u_in, u_ref), (o_in, o_ref), (p_in, p_ref), (qkv_in, qkv), (gain_in, gain)
                )
            ]
            pl.run_scoped(hidden_grads, pltpu.VMEM((T, D), F32))
            for copy in copies:
                copy.wait()
            gacc[...] = jnp.zeros_like(gacc)
            pl.run_scoped(out_grads, pltpu.VMEM((2, TT, wide), BF16))
            pl.run_scoped(functools.partial(heads, qkv, u_ref, o_ref, p_ref, wo, gain), pltpu.VMEM((TT, wide), F32))

        def hidden_grads(h_ref):
            for copy in (load(h_in, h_ref), load(cot_in.at[pl.ds(0, T), :], es_da)):
                copy.wait()
            for t in range(T // 256):
                swap(t).wait_recv()

                def rows_body(r):
                    rows = rows_of(t * 256 + r * 64, 64)
                    db = dh[rows, :] + hr[rows, :]
                    h = h_ref[rows, :]
                    factor = rms_factor(h)
                    normed = h * factor
                    grad = es_da[rows, :].astype(F32) + factor * (
                        db - normed * jnp.mean(db * normed, axis=-1, keepdims=True)
                    )
                    dh[rows, :] = grad
                    dhl[rows, :] = grad.astype(BF16)

                loop(4, rows_body)
                swap_low(t).start()
                checkpoint()
        def out_grads(z_ref):
            z_load = load(z_in, z_ref)
            for t in range(T // 256):
                swap_low(t).wait_recv()
            z_load.wait()
            for j in (0, 1):
                gb[2][j] = dot_tn(z_ref[j], dhl[...]).astype(BF16)
                send(2, j)
                checkpoint()

        def heads(qkv, u_ref, o_ref, p_ref, wo, gain, dz_ref):
            for j in (0, 1):
                def dz_rows(t):
                    rows = rows_of(t * 256, 256)
                    dz_ref[rows, :] = dot_nt(dhl[rows, :], wo[j])

                loop(TT // 256, dz_rows)

                def unit(t):
                    rows = rows_of(t * UNIT, UNIT)
                    for pair in range(wide // UNIT):
                        cols = pl.ds(pair * UNIT, UNIT)
                        q, k, v = (qkv[j, rows, pl.ds(f * wide + pair * UNIT, UNIT)] for f in range(3))
                        o, u, dz = o_ref[j, rows, cols], u_ref[j, rows, cols], dz_ref[rows, cols]
                        gain_row = gain[j, :, cols]
                        factor = lax.rsqrt(head_mean(o * o) + EPSILON)
                        normed = o * factor
                        s = jax.nn.sigmoid(u)
                        act = u * s
                        dzn = dz * normed
                        gacc[j, :, cols] += jnp.sum((dzn * act).reshape(UNIT // 8, 8, UNIT), axis=0)
                        du = (dzn * gain_row * s * (1.0 + u * (1.0 - s))).astype(BF16)
                        dn = dz * act * gain_row
                        do = stacked((factor * (dn - normed * head_mean(dn * normed))).astype(BF16))
                        soft_low = p_ref[j, pair, t]
                        soft = soft_low.astype(F32)
                        dv = dot_tn(soft_low, do)
                        dp = dot_nt(do, v)
                        ds = (soft * (dp - jnp.sum(dp * soft, axis=-1, keepdims=True))).astype(BF16)
                        dq = dot(jnp.concatenate([ds[:UNIT], ds[UNIT:]], axis=1), stacked(k)) * DH ** (-0.5)
                        dk = dot_tn(ds, stacked(q)) * DH ** (-0.5)
                        for f, value in enumerate((dq, dk, dv)):
                            dproj[j, rows, pl.ds(f * wide + pair * UNIT, UNIT)] = value.astype(BF16)
                        dproj[j, rows, pl.ds(3 * wide + pair * UNIT, UNIT)] = du

                for part in range(2):
                    loop(TT // UNIT // 2, lambda t: unit(t + part * (TT // UNIT // 2)))
                    checkpoint()
                if j == 0:
                    a_load.wait()
                for i in (0, 1):
                    def block(t):
                        rows = pl.ds(pl.multiple_of(t * 256, 256), 256)
                        cols = pl.ds(i * 2 * wide, 2 * wide)
                        gb[i][j, rows, :] = dot_tn(a_ref[:, rows], dproj[j, :, cols]).astype(BF16)

                    loop(D // 256, block)
                    send(i, j)
                    checkpoint()

        pl.run_scoped(
            inner,
            pltpu.VMEM((2, TT, 3 * wide), BF16),
            pltpu.VMEM((2, TT, wide), F32),
            pltpu.VMEM((2, TT, wide), F32),
            pltpu.VMEM((2, wide // UNIT, TT // UNIT, 2 * UNIT, UNIT), BF16),
            pltpu.VMEM((2, wide, D), BF16),
            pltpu.VMEM((2, 1, wide), F32),
        )

        def inputs_part(w0, x_ref):
            for copy in (load(w0_in, w0), load(x_in, x_ref)):
                copy.wait()

            def da_rows(row):
                rows = rows_of(row, 256)
                return dot_nt(dproj[0, rows, :], w0[0]) + dot_nt(dproj[1, rows, :], w0[1])

            for t in range(T // 256):
                es_da[pl.ds(t * 256, 256), :] = da_rows(T + t * 256).astype(BF16)
                swap_da(t).start()
                checkpoint()
            for t in range(T // 256):
                hs[pl.ds(t * 256, 256), :] = da_rows(t * 256)
                checkpoint()
            for t in range(T // 256):
                swap_da(t).wait_recv()

                def rows_body(r):
                    rows = rows_of(t * 256 + r * 64, 64)
                    da = hs[rows, :] + er_da[rows, :].astype(F32)
                    x = x_ref[rows, :].astype(F32)
                    factor = rms_factor(x)
                    normed = x * factor
                    dh[rows, :] = dh[rows, :] + factor * (
                        da - normed * jnp.mean(da * normed, axis=-1, keepdims=True)
                    )

                loop(4, rows_body)
                checkpoint()

        for t in range(T // 256):
            swap(t).wait_send()
        pl.run_scoped(inputs_part, pltpu.VMEM((2, D, 4 * wide), BF16), pltpu.VMEM((T, D), BF16))

    pl.run_scoped(attention, pltpu.VMEM((2, TT, 4 * wide), BF16), pltpu.VMEM((TT, D), BF16))
    dx_save = load(dh, dx_out)

    def gain_sum(k, src, dst, device, total):
        copy = remote(src, dst, gss.at[k], grs.at[k], device)
        copy.start()
        copy.wait()
        total[...] += dst[...]

    gain_sum(0, gacc, gx, me.xn, gacc)
    checkpoint()
    gain_sum(1, gacc, gy, me.yn, gacc)

    def gain_z(j):
        slot = lax.rem(z - (2 * c + j) + 3 + 4, 4)
        return remote(gacc.at[j], gz.at[slot], gss.at[2 + j], grs.at[4 + slot], (me.dp, 2 * c + j))

    for j in (0, 1):
        @pl.when(z != 2 * c + j)
        def _():
            gain_z(j).start()

    def output_part(m_ref, w3, stage):
        for copy in (load(m_in, m_ref), load(w3_in, w3), load(h_in, stage)):
            copy.wait()
        for t in range(T // 256):
            swap_da(t).wait_send()

        def out_rows(row):
            rows = rows_of(row, 256)
            return dot(m_ref[0, rows, :], w3[0]) + dot(m_ref[1, rows, :], w3[1])

        for t in range(T // 256):
            es_da[pl.ds(t * 256, 256), :] = out_rows(T + t * 256).astype(BF16)
            swap_out(t).start()
            checkpoint()
        for t in range(T // 256):
            rows = pl.ds(t * 256, 256)
            stage[rows, :] = stage[rows, :] + out_rows(t * 256)
            checkpoint()
        for t in range(T // 256):
            swap_out(t).wait_recv()
            rows = pl.ds(t * 256, 256)
            stage[rows, :] = stage[rows, :] + er_out[rows, :].astype(F32)

        load(stage, out_out).wait()

    pl.run_scoped(
        output_part, pltpu.VMEM((2, TT, hidden), BF16), pltpu.VMEM((2, hidden, D), BF16), pltpu.VMEM((T, D), F32)
    )

    def gain_final():
        return remote(gain_sent, gain_out, gss.at[7], grs.at[7], me.sib)

    @pl.when(innet)
    def _():
        for slot in range(3):
            remote(gz.at[slot], gz.at[slot], gss.at[2], grs.at[4 + slot], me.sib).wait_recv()
            gacc[own] += gz[slot]
        for e in range(spare):
            copy = remote(gacc.at[own], gq.at[e], gss.at[8 + e], grs.at[8 + e], other_quad(e))
            copy.start()
            copy.wait()
            gacc[own] += gq[e]
        gain_sent[...] = jnp.sum(gacc[own], axis=0, keepdims=True)
        local = pltpu.make_async_copy(gain_sent, gain_out, ld.at[39])
        local.start()
        gain_final().start()
        local.wait()
        gain_final().wait_send()

    checkpoint()

    @pl.when(jnp.logical_not(innet))
    def _():
        gain_final().wait_recv()
        for i in arrays:
            spread(i, 0)[0][2].wait_recv()
            pass_x(i)[1].wait_recv()
            pass_y(i)[1].wait_recv()
            for copy in pass_last(i):
                copy.wait_recv()

    @pl.when(innet)
    def _():
        for i in arrays:
            for copy in (pass_x(i)[1], pass_y(i)[1]) + pass_last(i):
                copy.wait_send()

    for j in (0, 1):
        @pl.when(z != 2 * c + j)
        def _():
            gain_z(j).wait_send()

    for t in range(T // 256):
        swap_low(t).wait_send()
        swap_out(t).wait_send()
    dx_save.wait()


def run_backward(x, kept, spare):
    T, D = x.shape
    TT = 2 * T
    w0, wo, w1, w2, w3 = kept[:5]
    wide, hidden = wo.shape[1], w1.shape[1]
    shapes = [(D, 2 * wide), (D, 2 * wide)] + [w.shape[1:] for w in (wo, w1, w2, w3)]
    q = [s[0] // 4 for s in shapes]
    h = [half_of(n) for n in q]
    cols = [s[1] for s in shapes]
    n = range(6)
    lands = [2] * 6
    extra = max(spare, 1)
    vmem = (
        [pltpu.VMEM((2,) + s, BF16) for s in shapes]
        + [pltpu.VMEM((lands[i], 2, h[i], cols[i]), BF16) for i in n]
        + [pltpu.VMEM((lands[i], 2, q[i] - h[i], cols[i]), BF16) for i in n]
        + [pltpu.VMEM((lands[i], h[i], cols[i]), BF16) for i in n]
        + [pltpu.VMEM((lands[i], q[i] - h[i], cols[i]), BF16) for i in n]
        + [pltpu.VMEM((3, q[i] if i < 5 else 4 * q[i], cols[i]), BF16) for i in n]
        + [
            pltpu.VMEM((T, D), F32),
            pltpu.VMEM((T, D), F32),
            pltpu.VMEM((T, D), BF16),
            pltpu.VMEM((T, D), BF16),
            pltpu.VMEM((T, D), BF16),
            pltpu.VMEM((T, D), F32),
            pltpu.VMEM((TT, D), BF16),
            pltpu.VMEM((2, 8, wide), F32),
            pltpu.VMEM((2, 8, wide), F32),
            pltpu.VMEM((2, 8, wide), F32),
            pltpu.VMEM((3, 8, wide), F32),
            pltpu.VMEM((extra, 8, wide), F32),
            pltpu.VMEM((1, wide), F32),
        ]
    )
    dma = pltpu.SemaphoreType.DMA
    sems = [
        dma((6, 2, 4)), dma((6, 2, 4)), dma((6, 2, 2)), dma((6, 2, 2)), dma((6, 2)), dma((6, 3)),
        dma((6,)), dma((6,)), dma((6,)), dma((6,)), dma((6, 2)), dma((6, 2)), dma((6, 5)), dma((6, 5)),
        dma((6, 2 + extra)), dma((6, extra)), dma((40,)), dma((8,)), dma((8,)), dma((8 + extra,)), dma((8 + extra,)),
    ]
    outs = [((T, D), F32), ((T, D), F32)] + [(s, BF16) for s in shapes] + [((1, wide), F32)]
    if spare:
        outs += [((spare, q[i], cols[i]), BF16) for i in n]
    return pl.pallas_call(
        functools.partial(backward_kernel, shapes, spare),
        out_shape=[jax.ShapeDtypeStruct(s, t) for s, t in outs],
        in_specs=any_spec(1 + len(kept)),
        out_specs=any_spec(len(outs)),
        scratch_shapes=vmem + sems,
        compiler_params=pltpu.CompilerParams(collective_id=1, has_side_effects=True, vmem_limit_bytes=VMEM_LIMIT),
        cost_estimate=pl.CostEstimate(flops=30 * 10**9, bytes_accessed=80 * 10**6, transcendentals=10**6),
        name="backward",
    )(x, *kept)


def finish_kernel(wide, *refs):
    ready, grads = refs[:2], refs[2:8]
    ready_out, outs = refs[8:10], refs[10:18]
    low, full = refs[18:24], refs[24:30]
    held = refs[30:32]
    sems, done = refs[32:]
    loads = [pltpu.make_async_copy(src, dst, sems.at[i]) for i, (src, dst) in enumerate(zip(grads, low))]
    for copy in loads:
        copy.start()
    moves = [pltpu.make_async_copy(src, dst, sems.at[6 + i]) for i, (src, dst) in enumerate(zip(ready, held))]
    for copy in moves:
        copy.start()
    saves = []
    for i in range(6):
        loads[i].wait()

        def widen(t, carry):
            rows = rows_of(t * 64, 64)
            full[i][rows, :] = low[i][rows, :].astype(F32)
            return carry

        lax.fori_loop(0, low[i].shape[0] // 64, widen, 0)
        if i < 2:
            parts = [(full[i].at[:, pl.ds(n * wide, wide)], outs[2 * i + n], done.at[2 * i + n]) for n in range(2)]
        else:
            parts = [(full[i], outs[2 + i], done.at[2 + i])]
        for part in parts:
            copy = pltpu.make_async_copy(*part)
            copy.start()
            saves.append(copy)
    for i in range(2):
        moves[i].wait()
        copy = pltpu.make_async_copy(held[i], ready_out[i], done.at[8 + i])
        copy.start()
        saves.append(copy)
    for copy in saves:
        copy.wait()


def run_finish(ready, grads, wide):
    shapes = [g.shape for g in grads]
    outs = [r.shape for r in ready] + [(shapes[0][0], wide)] * 4 + shapes[2:]
    return pl.pallas_call(
        functools.partial(finish_kernel, wide),
        out_shape=[jax.ShapeDtypeStruct(s, F32) for s in outs],
        in_specs=any_spec(8),
        out_specs=any_spec(len(outs)),
        scratch_shapes=[pltpu.VMEM(s, BF16) for s in shapes]
        + [pltpu.VMEM(s, F32) for s in shapes]
        + [pltpu.VMEM(r.shape, F32) for r in ready]
        + [pltpu.SemaphoreType.DMA((8,)), pltpu.SemaphoreType.DMA((10,))],
        compiler_params=pltpu.CompilerParams(vmem_limit_bytes=VMEM_LIMIT),
        cost_estimate=pl.CostEstimate(flops=0, bytes_accessed=30 * 10**6, transcendentals=0),
        name="finish",
    )(*ready, *grads)


def shards(
    inputs, w_query, w_key, w_value, w_gate, head_gain, w_out, w_first, w_second, w_third, cotangent
):
    wide = w_query.shape[1]
    weights = [w_query, w_key, w_value, w_gate, w_out, w_first.T, w_second.T, w_third]
    gain = head_gain.reshape(1, wide)
    kept = run_forward(inputs, cotangent, gain, weights)
    spare = (lax.axis_size("dp") // 8).bit_length() - 1
    results = run_backward(inputs, kept, spare)
    output, grad_inputs, *grads = run_finish(results[:2], results[2:8], wide)
    g_query, g_key, g_value, g_gate, g_out, g_first, g_second, g_third = grads
    g_gain = results[8].reshape(wide)
    return (
        output, grad_inputs, g_query, g_key, g_value, g_gate, g_gain, g_out, g_first.T, g_second.T, g_third
    )


def solution(mesh):
    rows, columns = P(("dp", "mp"), None), P(None, "mp")
    heads = P("mp", None)
    return jax.shard_map(
        shards,
        mesh=mesh,
        in_specs=(rows, columns, columns, columns, columns, P("mp"), heads, columns, columns, heads, rows),
        out_specs=(rows, rows, columns, columns, columns, columns, P("mp"), heads, columns, columns, heads),
        check_vma=False,
    )
```

```python
import functools

import jax
import jax.numpy as jnp
from jax import lax
from jax.experimental import pallas as pl
from jax.experimental.pallas import tpu as pltpu
from jax.sharding import PartitionSpec as P

DH = 64
BLK = 64
EPSILON = 1e-06
MESH = pl.DeviceIdType.MESH
F32 = jnp.float32
BF16 = jnp.bfloat16
UNIT = 128
VMEM_LIMIT = 61 * 2**20


GATHER = (
    (0, 1, 2, 3, 4, 16, 17, 18, 19,),
    (5, 33,),
    (32,),
    (),
    (34, 35,),
    (),
    (7,),
    (6,),
    (20,),
    (9,),
    (8,),
    (10,),
    (23, 22, 21,),
    (),
    (11,),
    (36,),
    (),
    (25,),
    (),
    (),
    (24, 26,),
    (),
    (),
    (38, 12, 37, 39,),
    (13, 27,),
    (42, 40, 41,),
    (28,),
    (29,),
    (),
    (),
    (),
    (),
    (43,),
    (44,),
    (45,),
)
LEAD = 3


def rms_factor(values):
    return lax.rsqrt(jnp.mean(values * values, axis=-1, keepdims=True) + EPSILON)


def dot(left, right):
    return jnp.dot(left, right, preferred_element_type=F32)


def dot_tn(left, right):
    return lax.dot_general(left, right, (((0,), (0,)), ((), ())), preferred_element_type=F32)


def dot_nt(left, right):
    return lax.dot_general(left, right, (((1,), (1,)), ((), ())), preferred_element_type=F32)


def remote(src, dst, send, recv, device):
    return pltpu.make_async_remote_copy(src, dst, send, recv, device_id=device, device_id_type=MESH)


def rows_of(start, count):
    return pl.ds(pl.multiple_of(start, 16), count)


class Place:
    def __init__(self):
        dp, self.z = lax.axis_index("dp"), lax.axis_index("mp")
        self.dp = dp
        self.c = dp % 2
        self.bx, self.by = (dp // 2) % 2, (dp // 4) % 2
        self.p = self.by * 2 + self.bx
        self.px, self.py = self.by * 2 + 1 - self.bx, (1 - self.by) * 2 + self.bx
        self.pd = (1 - self.by) * 2 + 1 - self.bx
        self.sib = (dp + 1 - 2 * self.c, self.z)
        self.xn = (dp + 2 - 4 * self.bx, self.z)
        self.yn = (dp + 4 - 8 * self.by, self.z)
        self.own = self.z % 2
        self.innet = self.z // 2 == self.c

    def up(self):
        return (self.dp, self.z + 1)

    def down(self):
        return (self.dp, self.z - 1)


def half_of(count):
    return (count // 2 + 15) // 16 * 16


def gather_plan(shapes):
    plan = []
    for i, (rows, _) in enumerate(shapes):
        quarter = rows // 4
        if i < 4:
            parts = [quarter]
        elif i == 4:
            parts = [quarter]
        else:
            third = (quarter // 3 + 15) // 16 * 16
            parts = [third, third, quarter - 2 * third]
        start = 0
        for count in parts:
            plan.append((i, max(i - 3, 0), i * shapes[0][1] if i < 4 else 0, start, count))
            start += count
    return plan


def forward_kernel(plan, shapes, *refs):
    nw = 8
    x_in, cot_in, gain_in = refs[:3]
    w_in = refs[3 : 3 + nw]
    outs = refs[3 + nw : 3 + nw + 19]
    (w_out, a_out, qkv_out, u_out, o_out, p_out, z_out, h_out, b_out, m_out, d1_out, d2_out, cot_out, gain_out, g3_out) = (
        outs[:5], *outs[5:]
    )
    scratch = refs[3 + nw + 19 :]
    bufs = scratch[:5]
    (x_ref, cot, a_ref, qkv, u_ref, o_ref, p_ref, z_ref, hs, hr, h_ref, b_ref, m_ref, d1, d2, gain, g3) = scratch[5:22]
    (zs, zr, fzs, xs, xr, ys, yr, fs, fr, loc, gs, gr, es, er, sv) = scratch[22:]
    me = Place()
    z, c, own, innet = me.z, me.c, me.own, me.innet
    T = x_in.shape[0]
    TT = 2 * T
    count = len(plan)
    wide = shapes[0][1]

    bar = pltpu.get_barrier_semaphore()
    for d in (me.sib, me.xn, me.yn):
        pl.semaphore_signal(bar, inc=1, device_id=d, device_id_type=MESH)

    @pl.when(z < 3)
    def _():
        pl.semaphore_signal(bar, inc=1, device_id=me.up(), device_id_type=MESH)

    @pl.when(z > 0)
    def _():
        pl.semaphore_signal(bar, inc=1, device_id=me.down(), device_id_type=MESH)

    pl.semaphore_wait(bar, 3 + jnp.where(z < 3, 1, 0) + jnp.where(z > 0, 1, 0))

    def z_only(k):
        return plan[k][4] == shapes[plan[k][0]][0]

    def piece(k, who):
        i, _, _, start, rows = plan[k]
        return (0 if z_only(k) else who * (shapes[i][0] // 4) + start), rows

    def part(j, k, row, rows):
        _, buf, col, _, _ = plan[k]
        ref = bufs[buf]
        if buf:
            return ref.at[j, rows_of(row, rows), :]
        return ref.at[j, rows_of(row, rows), pl.ds(col, wide)]

    def z_first(k, d):
        row, rows = piece(k, me.p)
        src = w_in[plan[k][0]].at[rows_of(row, rows), :]
        return remote(src, part(own, k, row, rows), zs.at[k, d], zr.at[k, own], (me.dp, z + 1 - 2 * d))

    def z_next(k, j, d):
        row, rows = piece(k, me.p)
        r = part(j, k, row, rows)
        return remote(r, r, fzs.at[k, j], zr.at[k, j], (me.dp, z + 1 - 2 * d))

    def to_x(k, j):
        row, rows = piece(k, me.p)
        r = part(j, k, row, rows)
        return remote(r, r, xs.at[k, j], xr.at[k, j], me.xn)

    def to_y(k, j):
        row, rows = piece(k, me.p)
        r = part(j, k, row, rows)
        return remote(r, r, ys.at[k, j], yr.at[k, j], me.yn)

    def x_then_y(k, j):
        row, rows = piece(k, me.px)
        r = part(j, k, row, half_of(rows))
        return remote(r, r, fs.at[0, k, j], fr.at[0, k, j], me.yn)

    def y_then_x(k, j):
        row, rows = piece(k, me.py)
        h = half_of(rows)
        r = part(j, k, row + h, rows - h)
        return remote(r, r, fs.at[1, k, j], fr.at[1, k, j], me.xn)

    def gain_copy(j, d, src):
        return remote(src, gain.at[j], gs.at[j, d], gr.at[j], (me.dp, z + 1 - 2 * d))

    def own_copies():
        copies = []
        for i in range(nw):
            dst = bufs[i - 3].at[own] if i > 3 else bufs[0].at[own, :, pl.ds(i * wide, wide)]
            copies.append(pltpu.make_async_copy(w_in[i], dst, loc.at[i]))
        copies.append(pltpu.make_async_copy(gain_in, gain.at[own], loc.at[nw]))
        return copies

    both = [
        remote(x_in, x_ref.at[pl.ds(T, T), :], es.at[0], er.at[0], me.sib),
        remote(cot_in, cot.at[pl.ds(T, T), :], es.at[1], er.at[1], me.sib),
    ]
    mine = [
        pltpu.make_async_copy(x_in, x_ref.at[pl.ds(0, T), :], loc.at[nw + 1]),
        pltpu.make_async_copy(cot_in, cot.at[pl.ds(0, T), :], loc.at[nw + 2]),
    ]
    mine[0].start()
    both[0].start()

    order = [code for codes in GATHER for code in codes if code < 16]

    def z_starts(k):
        @pl.when(z < 3)
        def _():
            z_first(k, 0).start()

        @pl.when(z > 0)
        def _():
            z_first(k, 1).start()

    @pl.when(innet)
    def _():
        @pl.when(z < 3)
        def _():
            gain_copy(own, 0, gain_in).start()

        @pl.when(z > 0)
        def _():
            gain_copy(own, 1, gain_in).start()

        for k in order[:LEAD]:
            z_starts(k)
        for copy in own_copies():
            copy.start()

    mine[1].start()
    both[1].start()

    def upward(j):
        return (z > 2 * c + j) & (z < 3)

    def downward(j):
        return (z < 2 * c + j) & (z > 0)

    def others(step, *args):
        for j in (0, 1):
            @pl.when(z != 2 * c + j)
            def _():
                step(*args, j)

    def step_gain(j):
        remote(gain.at[j], gain.at[j], gs.at[j, 0], gr.at[j], me.sib).wait_recv()

        @pl.when(upward(j))
        def _():
            gain_copy(j, 0, gain.at[j]).start()

        @pl.when(downward(j))
        def _():
            gain_copy(j, 1, gain.at[j]).start()

    def step_a(k, j):
        row, rows = piece(k, me.p)
        r = part(j, k, row, rows)
        remote(r, r, fzs.at[k, j], zr.at[k, j], me.sib).wait_recv()

        @pl.when(upward(j))
        def _():
            z_next(k, j, 0).start()

        @pl.when(downward(j))
        def _():
            z_next(k, j, 1).start()

        if not z_only(k):
            to_x(k, j).start()
            to_y(k, j).start()

    def step_b(k, j):
        to_x(k, j).wait_recv()
        x_then_y(k, j).start()
        to_y(k, j).wait_recv()
        y_then_x(k, j).start()

    def step_c(k, j):
        x_then_y(k, j).wait_recv()
        y_then_x(k, j).wait_recv()
        for copy in (to_x, to_y, x_then_y, y_then_x):
            copy(k, j).wait_send()

    mark = [0]

    def checkpoint():
        for code in GATHER[mark[0]]:
            others((step_a, step_b, step_c)[code // 16], code % 16)
            after = order.index(code) + LEAD if code < 16 else count
            if after < count:
                pl.when(innet)(functools.partial(z_starts, order[after]))
        mark[0] += 1

    saves = []

    def save(src, dst):
        copy = pltpu.make_async_copy(src, dst, sv.at[len(saves)])
        copy.start()
        saves.append(copy)

    checkpoint()
    mine[0].wait()
    both[0].wait_recv()
    checkpoint()

    def norm_rows(t, carry):
        rows = rows_of(t * UNIT, UNIT)
        values = x_ref[rows, :].astype(F32)
        a_ref[rows, :] = (values * rms_factor(values)).astype(BF16)
        return carry

    for n in range(2):
        lax.fori_loop(n * TT // UNIT // 2, (n + 1) * TT // UNIT // 2, norm_rows, 0)
        checkpoint()
    save(a_ref, a_out)

    @pl.when(innet)
    def _():
        for copy in own_copies():
            copy.wait()

    others(step_gain)

    lane = lax.broadcasted_iota(jnp.int32, (UNIT, UNIT), 1)
    low_half = lane < DH
    keep = [low_half.astype(F32).astype(BF16), (lane >= DH).astype(F32).astype(BF16)]
    row2 = lax.broadcasted_iota(jnp.int32, (2 * UNIT, UNIT), 0) % UNIT
    col2 = lax.broadcasted_iota(jnp.int32, (2 * UNIT, UNIT), 1)
    seen = (row2 // BLK == col2 // BLK) & (col2 <= row2)

    def attend(j):
        def project(r, carry):
            rows = rows_of(r * 256, 256)
            acc = dot(a_ref[rows, :], bufs[0][j])
            qkv[j, rows, :] = acc[:, : 3 * wide].astype(BF16)
            u_ref[j, rows, :] = acc[:, 3 * wide :]
            return carry

        lax.fori_loop(0, TT // 256, project, 0)
        checkpoint()

        def unit(t, carry):
            rows = rows_of(t * UNIT, UNIT)
            for pair in range(wide // UNIT):
                q, k, v = (qkv[j, rows, pl.ds(f * wide + pair * UNIT, UNIT)] for f in range(3))
                cols = pl.ds(pair * UNIT, UNIT)
                scores = dot_nt(jnp.concatenate([q * keep[0], q * keep[1]], axis=0), k) * DH ** (-0.5)
                scores = jnp.where(seen, scores, -1e30)
                shifted = jnp.exp(scores - jnp.max(scores, axis=-1, keepdims=True))
                soft = (shifted / jnp.sum(shifted, axis=-1, keepdims=True)).astype(BF16)
                p_ref[j, pair, t] = soft
                attended = dot(
                    jnp.concatenate([soft[:UNIT], soft[UNIT:]], axis=1),
                    jnp.concatenate([v * keep[0], v * keep[1]], axis=0),
                )
                o_ref[j, rows, cols] = attended
                square = attended * attended
                mean0 = jnp.sum(jnp.where(low_half, square, 0.0), axis=-1, keepdims=True) / DH
                mean1 = jnp.sum(jnp.where(low_half, 0.0, square), axis=-1, keepdims=True) / DH
                normed = attended * lax.rsqrt(jnp.where(low_half, mean0, mean1) + EPSILON)
                u = u_ref[j, rows, cols]
                g = gain[j, :, cols]
                z_ref[j, rows, cols] = (normed * g * (u * jax.nn.sigmoid(u))).astype(BF16)
            return carry

        span = TT // UNIT // 4
        for n in range(4):
            lax.fori_loop(n * span, n * span + span, unit, 0)
            checkpoint()

    checkpoint()
    attend(0)
    attend(1)
    checkpoint()
    for src, dst in ((qkv, qkv_out), (u_ref, u_out), (o_ref, o_out), (p_ref, p_out), (z_ref, z_out), (gain, gain_out)):
        save(src, dst)
    save(bufs[0], w_out[0])
    save(bufs[1], w_out[1])

    def out_rows(row):
        rows = rows_of(row, 256)
        return dot(z_ref[0, rows, :], bufs[1][0]) + dot(z_ref[1, rows, :], bufs[1][1])

    swaps = []
    for i in range(T // 256):
        hs[pl.ds(i * 256, 256), :] = out_rows(T + i * 256)
        part_rows = pl.ds(i * 256, 256)
        swaps.append(remote(hs.at[part_rows, :], hr.at[part_rows, :], es.at[2 + i], er.at[2 + i], me.sib))
        swaps[-1].start()
        checkpoint()
    for i in range(T // 256):
        h_ref[pl.ds(i * 256, 256), :] = x_ref[pl.ds(i * 256, 256), :].astype(F32) + out_rows(i * 256)
        checkpoint()
    checkpoint()
    for i, swap in enumerate(list(swaps)):
        swap.wait_recv()

        def add_rows(t, carry):
            rows = rows_of(i * 256 + t * UNIT, UNIT)
            values = h_ref[rows, :] + hr[rows, :]
            h_ref[rows, :] = values
            b_ref[rows, :] = (values * rms_factor(values)).astype(BF16)
            return carry

        lax.fori_loop(0, 256 // UNIT, add_rows, 0)
        b_rows = pl.ds(i * 256, 256)
        swaps.append(remote(b_ref.at[b_rows, :], b_ref.at[pl.ds(T + i * 256, 256), :], es.at[4 + i], er.at[4 + i], me.sib))
        swaps[-1].start()
        checkpoint()
    save(h_ref, h_out)
    for swap in swaps[len(swaps) // 2 :]:
        swap.wait_recv()
    save(b_ref, b_out)

    def rows_loop(body):
        lax.fori_loop(0, TT // 256, lambda r, carry: (body(rows_of(r * 256, 256)), carry)[1], 0)

    checkpoint()
    save(bufs[2], w_out[2])
    for j in (0, 1):
        def first(rows):
            d2[j, rows, :] = dot_nt(b_ref[rows, :], bufs[2][j]).astype(BF16)

        rows_loop(first)
        checkpoint()
    save(bufs[3], w_out[3])
    for j in (0, 1):
        def second(rows):
            g2 = dot_nt(b_ref[rows, :], bufs[3][j])
            d1[j, rows, :] = g2.astype(BF16)
            m_ref[j, rows, :] = (d2[j, rows, :].astype(F32) * g2).astype(BF16)

        rows_loop(second)
        checkpoint()
    for src, dst in ((m_ref, m_out), (d1, d1_out), (d2, d2_out)):
        save(src, dst)
    mine[1].wait()
    both[1].wait_recv()
    save(cot, cot_out)
    hidden = m_ref.shape[2]
    for j in (0, 1):
        for start in range(0, hidden, 256):
            size = min(256, hidden - start)
            g3[j, pl.ds(start, size), :] = dot_tn(m_ref[j, :, pl.ds(start, size)], cot[...]).astype(BF16)
            checkpoint()
    save(g3, g3_out)
    checkpoint()
    save(bufs[4], w_out[4])

    @pl.when(innet)
    def _():
        for d, inside in ((0, z < 3), (1, z > 0)):
            @pl.when(inside)
            def _():
                gain_copy(own, d, gain_in).wait_send()
                for k in range(count):
                    z_first(k, d).wait_send()

    def ends(j):
        @pl.when(upward(j) | downward(j))
        def _():
            for k in range(count):
                z_next(k, j, 0).wait_send()

        @pl.when(upward(j))
        def _():
            gain_copy(j, 0, gain.at[j]).wait_send()

        @pl.when(downward(j))
        def _():
            gain_copy(j, 1, gain.at[j]).wait_send()

    others(ends)
    for copy in both + swaps:
        copy.wait_send()
    for copy in saves:
        copy.wait()


def any_spec(count):
    return [pl.BlockSpec(memory_space=pl.ANY)] * count


def run_forward(x, cot, gain, weights):
    T, D = x.shape
    TT = 2 * T
    shapes = [w.shape for w in weights]
    plan = gather_plan(shapes)
    wide, hidden = shapes[0][1], shapes[5][0]
    units, pairs = TT // UNIT, wide // UNIT
    buffers = [(2, D, 4 * wide), (2, wide, D), (2, hidden, D), (2, hidden, D), (2, hidden, D)]
    kept = [
        ((TT, D), BF16),
        ((2, TT, 3 * wide), BF16),
        ((2, TT, wide), F32),
        ((2, TT, wide), F32),
        ((2, pairs, units, 2 * UNIT, UNIT), BF16),
        ((2, TT, wide), BF16),
        ((T, D), F32),
        ((TT, D), BF16),
        ((2, TT, hidden), BF16),
        ((2, TT, hidden), BF16),
        ((2, TT, hidden), BF16),
        ((TT, D), BF16),
        ((2, 1, wide), F32),
        ((2, hidden, D), BF16),
    ]
    vmem = [pltpu.VMEM(s, BF16) for s in buffers] + [
        pltpu.VMEM((TT, D), BF16),
        pltpu.VMEM((TT, D), BF16),
        pltpu.VMEM((TT, D), BF16),
        pltpu.VMEM((2, TT, 3 * wide), BF16),
        pltpu.VMEM((2, TT, wide), F32),
        pltpu.VMEM((2, TT, wide), F32),
        pltpu.VMEM((2, pairs, units, 2 * UNIT, UNIT), BF16),
        pltpu.VMEM((2, TT, wide), BF16),
        pltpu.VMEM((T, D), F32),
        pltpu.VMEM((T, D), F32),
        pltpu.VMEM((T, D), F32),
        pltpu.VMEM((TT, D), BF16),
        pltpu.VMEM((2, TT, hidden), BF16),
        pltpu.VMEM((2, TT, hidden), BF16),
        pltpu.VMEM((2, TT, hidden), BF16),
        pltpu.VMEM((2, 1, wide), F32),
        pltpu.VMEM((2, hidden, D), BF16),
    ]
    n = len(plan)
    dma = pltpu.SemaphoreType.DMA
    sems = [dma((n, 2))] * 7 + [dma((2, n, 2))] * 2 + [dma((11,)), dma((2, 2)), dma((2,)), dma((6,)), dma((6,)), dma((24,))]
    return pl.pallas_call(
        functools.partial(forward_kernel, plan, shapes),
        out_shape=[jax.ShapeDtypeStruct(s, BF16) for s in buffers] + [jax.ShapeDtypeStruct(s, t) for s, t in kept],
        in_specs=any_spec(3 + len(weights)),
        out_specs=any_spec(len(buffers) + len(kept)),
        scratch_shapes=vmem + sems,
        compiler_params=pltpu.CompilerParams(collective_id=0, has_side_effects=True, vmem_limit_bytes=VMEM_LIMIT),
        cost_estimate=pl.CostEstimate(flops=16 * 10**9, bytes_accessed=80 * 10**6, transcendentals=10**6),
        name="forward",
    )(x, cot, gain, *weights)


SCHEDULE = (
    (16,),
    (),
    (),
    (),
    (18,),
    (),
    (),
    (),
    (),
    (19,),
    (),
    (),
    (),
    (21,),
    (34,),
    (),
    (35, 32, 20,),
    (),
    (),
    (),
    (24,),
    (),
    (37,),
    (),
    (),
    (36,),
    (),
    (26,),
    (),
    (),
    (),
    (1, 22, 53, 40, 17, 27, 25, 48, 69, 23, 42, 38, 50, 33, 58, 51, 52, 43, 41, 64, 59, 39, 74, 66, 55, 56, 67, 68, 75, 65, 71, 80, 54, 57, 91, 85, 81, 84, 90, 87, 83, 72, 70, 73, 88, 82, 86, 89,),
)
Z_FIRST = 1


def backward_kernel(shapes, spare, *refs):
    (x_in, w0_in, wo_in, w1_in, w2_in, w3_in, a_in, qkv_in, u_in, o_in, p_in, z_in, h_in, b_in, m_in, d1_in, d2_in) = refs[:17]
    cot_in, gain_in, g3_in = refs[17:20]
    out_out, dx_out = refs[20:22]
    final = refs[22:28]
    gain_out = refs[28]
    scratch = refs[29:]
    if spare:
        rq, scratch = scratch[:6], scratch[6:]
    gb, ra1, rb1, ra2, rb2, rz = (scratch[6 * i : 6 * i + 6] for i in range(6))
    (hs, hr, es_da, er_da, er_out, dh, dhl, gacc, gx, gy, gz, gq, gain_sent) = scratch[36:49]
    (s1, r1, s2, r2, sz, rzs, sx, rx, sy, ry, sf, rf, ss, rs, sq, rqs, ld, es, er, gss, grs) = scratch[49:]
    me = Place()
    z, c, own, innet, p = me.z, me.c, me.own, me.innet, me.p
    bx, by = me.bx, me.by
    T, D = x_in.shape
    TT = 2 * T
    wide = wo_in.shape[1]
    hidden = w1_in.shape[1]
    arrays = range(6)
    third = 5

    def other_quad(e):
        bit = 8 << e
        return (me.dp + bit - 2 * bit * ((me.dp // bit) % 2), z)

    def other_z(t):
        return (me.dp, lax.rem(z + t, 4))

    g3_load = pltpu.make_async_copy(g3_in, gb[5], ld.at[32])
    g3_load.start()
    bar = pltpu.get_barrier_semaphore()
    greeted = [me.sib, me.xn, me.yn] + [other_z(t) for t in (1, 2, 3)] + [other_quad(e) for e in range(spare)]
    for d in greeted:
        pl.semaphore_signal(bar, inc=1, device_id=d, device_id_type=MESH)
    pl.semaphore_wait(bar, len(greeted))

    quarters = [s[0] // 4 for s in shapes]
    halves = [half_of(q) for q in quarters]

    def add_rows(dst, sources, rows):
        def body(t, carry):
            r = rows_of(t * 16, 16)
            total = dst[r, :].astype(F32)
            for src in sources:
                total = total + src[r, :].astype(F32)
            dst[r, :] = total.astype(BF16)
            return carry

        lax.fori_loop(0, rows // 16, body, 0)

    def z_first(i, j):
        return i == third and j == Z_FIRST

    def first_half(i, j, who):
        return gb[i].at[j, rows_of(who * quarters[i], halves[i]), :]

    def second_half(i, j, who):
        return gb[i].at[j, rows_of(who * quarters[i] + halves[i], quarters[i] - halves[i]), :]

    def whole(i, j, who):
        return gb[i].at[j, rows_of(who * quarters[i], quarters[i]), :]

    def round1(i, j):
        copies = []
        for b in (0, 1):
            copies.append(
                remote(first_half(i, j, b * 2 + 1 - bx), ra1[i].at[j, b], s1.at[i, j, b], r1.at[i, j, b], me.xn)
            )
            copies.append(
                remote(second_half(i, j, (1 - by) * 2 + b), rb1[i].at[j, b], s1.at[i, j, 2 + b], r1.at[i, j, 2 + b], me.yn)
            )
        return copies

    def round2(i, j):
        return [
            remote(first_half(i, j, (1 - by) * 2 + bx), ra2[i].at[j], s2.at[i, j, 0], r2.at[i, j, 0], me.yn),
            remote(second_half(i, j, by * 2 + 1 - bx), rb2[i].at[j], s2.at[i, j, 1], r2.at[i, j, 1], me.xn),
        ]

    def round_z(i, j):
        slot = lax.rem(z - (2 * c + j) + 3 + 4, 4)
        src = gb[i].at[j] if z_first(i, j) else whole(i, j, p)
        return remote(src, landing(i, j, slot), sz.at[i, j], rzs.at[i, slot], (me.dp, 2 * c + j))

    def landing(i, j, slot):
        if i == third and not z_first(i, j):
            return rz[i].at[slot, pl.ds(0, quarters[i]), :]
        return rz[i].at[slot]

    def landed_z(i, j, slot):
        return remote(landing(i, j, slot), landing(i, j, slot), sz.at[i, j], rzs.at[i, slot], me.sib)

    def spread(i, j):
        src = whole(i, j, p)
        dst = final[i].at[rows_of(p * quarters[i], quarters[i]), :]
        return [
            remote(src, dst, sx.at[i], rx.at[i], me.xn),
            remote(src, dst, sy.at[i], ry.at[i], me.yn),
            remote(src, dst, ss.at[i, 0], rs.at[i, 0], me.sib),
        ], pltpu.make_async_copy(src, dst, ld.at[33 + i])

    def quarter_rows(i, who, second=None):
        q, h = quarters[i], halves[i]
        if second is None:
            return final[i].at[rows_of(who * q, q), :]
        if second:
            return final[i].at[rows_of(who * q + h, q - h), :]
        return final[i].at[rows_of(who * q, h), :]

    def hand_on(i, slot, ref):
        return remote(ref, ref, ss.at[i, slot], rs.at[i, slot], me.sib)

    def pass_x(i):
        r = quarter_rows(i, me.px, False)
        return remote(r, r, sf.at[i, 0], rf.at[i, 0], me.yn), hand_on(i, 1, quarter_rows(i, me.px))

    def pass_y(i):
        r = quarter_rows(i, me.py, True)
        return remote(r, r, sf.at[i, 1], rf.at[i, 1], me.xn), hand_on(i, 2, quarter_rows(i, me.py))

    def pass_last(i):
        return hand_on(i, 3, quarter_rows(i, me.pd, False)), hand_on(i, 4, quarter_rows(i, me.pd, True))

    def step_1(i, j):
        for copy in round1(i, j):
            copy.start()

    def step_2(i, j):
        for copy in round1(i, j):
            copy.wait_recv()
        add_rows(first_half(i, j, (1 - by) * 2 + bx), [ra1[i].at[j, 1 - by]], halves[i])
        add_rows(second_half(i, j, by * 2 + 1 - bx), [rb1[i].at[j, 1 - bx]], quarters[i] - halves[i])
        for copy in round2(i, j):
            copy.start()

    def step_3(i, j):
        for copy in round2(i, j):
            copy.wait_recv()
        for copy in round1(i, j):
            copy.wait_send()
        add_rows(first_half(i, j, p), [ra1[i].at[j, by], ra2[i].at[j]], halves[i])
        add_rows(
            second_half(i, j, p), [rb1[i].at[j, bx], rb2[i].at[j]], quarters[i] - halves[i]
        )

    def step_z(i, j):
        for slot in range(3):
            landed_z(i, j, slot).wait_recv()
        sources = [landing(i, j, slot) for slot in range(3)]
        if z_first(i, j):
            add_rows(gb[i].at[j], sources, 4 * quarters[i])
        else:
            add_rows(whole(i, j, p), sources, quarters[i])

    def step_spread(i, j):
        for e in range(spare):
            copy = remote(whole(i, j, p), rq[i].at[e], sq.at[i, e], rqs.at[i, e], other_quad(e))
            copy.start()
            copy.wait()
            h = halves[i]
            for k, (part, src) in enumerate(
                (
                    (ra2[i].at[j], rq[i].at[e, pl.ds(0, h), :]),
                    (rb2[i].at[j], rq[i].at[e, pl.ds(h, quarters[i] - h), :]),
                )
            ):
                local = pltpu.make_async_copy(src, part, sq.at[i, spare + k])
                local.start()
                local.wait()
            add_rows(first_half(i, j, p), [ra2[i].at[j]], h)
            add_rows(second_half(i, j, p), [rb2[i].at[j]], quarters[i] - h)
        copies, local = spread(i, j)
        for copy in copies:
            copy.start()
        local.start()

    def step_5(i, j):
        copies, _ = spread(i, j)
        copies[0].wait_recv()
        for copy in pass_x(i):
            copy.start()
        copies[1].wait_recv()
        for copy in pass_y(i):
            copy.start()

    def step_6(i, j):
        pass_x(i)[0].wait_recv()
        pass_y(i)[0].wait_recv()
        for copy in pass_last(i):
            copy.start()
        copies, local = spread(i, j)
        local.wait()
        for copy in copies + [pass_x(i)[0], pass_y(i)[0]] + round2(i, j):
            copy.wait_send()

    items = [
        (5, 0), (5, 1), (3, 0), (4, 0), (3, 1), (4, 1), (2, 0), (2, 1), (0, 0), (1, 0), (0, 1), (1, 1)
    ]

    def send(i, j):
        if z_first(i, j):
            @pl.when(z != 2 * c + j)
            def _():
                round_z(i, j).start()
        else:
            step_1(i, j)

    def step(code):
        stage, (i, j) = code // 16, items[code % 16]
        mine = z == 2 * c + j
        if not z_first(i, j) and stage == 1:
            step_2(i, j)
        elif not z_first(i, j) and stage == 2:
            step_3(i, j)

            @pl.when(jnp.logical_not(mine))
            def _():
                round_z(i, j).start()
        else:
            order = {0: (step_z, step_1), 1: (step_2,), 2: (step_3, step_spread), 3: (step_z, step_spread)}

            @pl.when(mine)
            def _():
                for part in order.get(stage, (step_5,) if stage == 4 else (step_6,)):
                    part(i, j)

            if stage == 5:
                @pl.when(jnp.logical_not(mine))
                def _():
                    round_z(i, j).wait_send()
                    if not z_first(i, j):
                        for copy in round2(i, j):
                            copy.wait_send()

    mark = [0]

    def checkpoint():
        for code in SCHEDULE[mark[0]]:
            step(code)
        mark[0] += 1

    loads = [0]

    def load(src, dst):
        copy = pltpu.make_async_copy(src, dst, ld.at[loads[0]])
        copy.start()
        loads[0] += 1
        return copy


    def loop(count, body):
        lax.fori_loop(0, count, lambda t, carry: (body(t), carry)[1], 0)

    def feed_forward(b_ref, d1, d2):
        b_load, d1_load, d2_load = load(b_in, b_ref), load(d1_in, d1), load(d2_in, d2)

        def grads(w3, cot):
            copies = [load(w3_in, w3), load(cot_in, cot), b_load, d1_load, d2_load]
            g3_load.wait()
            for j in (0, 1):
                send(5, j)
            for copy in copies:
                copy.wait()
            for j in (0, 1):
                def rows_body(t):
                    rows = rows_of(t * 256, 256)
                    dm = dot_nt(cot[rows, :], w3[j])
                    d1[j, rows, :] = (dm * d1[j, rows, :].astype(F32)).astype(BF16)
                    d2[j, rows, :] = (dm * d2[j, rows, :].astype(F32)).astype(BF16)

                loop(TT // 256, rows_body)
                for i, d in ((3, d1), (4, d2)):
                    for start in range(0, hidden, 256):
                        size = min(256, hidden - start)
                        gb[i][j, pl.ds(start, size), :] = dot_tn(d[j, :, pl.ds(start, size)], b_ref[...]).astype(BF16)
                    send(i, j)
                    checkpoint()

        pl.run_scoped(grads, pltpu.VMEM((2, hidden, D), BF16), pltpu.VMEM((TT, D), BF16))

        def first_two(w1, w2):
            for copy in (load(w1_in, w1), load(w2_in, w2)):
                copy.wait()

            def db_rows(row):
                rows = rows_of(row, 256)
                total = dot(d1[0, rows, :], w1[0]) + dot(d2[0, rows, :], w2[0])
                return total + dot(d1[1, rows, :], w1[1]) + dot(d2[1, rows, :], w2[1])

            for t in range(T // 256):
                part = pl.ds(t * 256, 256)
                hs[part, :] = db_rows(T + t * 256)
                swap(t).start()
                checkpoint()
            for t in range(T // 256):
                dh[pl.ds(t * 256, 256), :] = db_rows(t * 256)
                checkpoint()

        pl.run_scoped(first_two, pltpu.VMEM((2, hidden, D), BF16), pltpu.VMEM((2, hidden, D), BF16))

    def swap(t):
        part = pl.ds(t * 256, 256)
        return remote(hs.at[part, :], hr.at[part, :], es.at[t], er.at[t], me.sib)

    def swap_low(t):
        part = pl.ds(t * 256, 256)
        return remote(dhl.at[part, :], dhl.at[pl.ds(T + t * 256, 256), :], es.at[2 + t], er.at[2 + t], me.sib)

    def swap_da(t):
        part = pl.ds(t * 256, 256)
        return remote(es_da.at[part, :], er_da.at[part, :], es.at[4 + t], er.at[4 + t], me.sib)

    def swap_out(t):
        part = pl.ds(t * 256, 256)
        return remote(es_da.at[part, :], er_out.at[part, :], es.at[6 + t], er.at[6 + t], me.sib)

    pl.run_scoped(
        feed_forward, pltpu.VMEM((TT, D), BF16), pltpu.VMEM((2, TT, hidden), BF16), pltpu.VMEM((2, TT, hidden), BF16)
    )

    lane = lax.broadcasted_iota(jnp.int32, (UNIT, UNIT), 1)
    low_half = lane < DH
    keep = [low_half.astype(F32).astype(BF16), (lane >= DH).astype(F32).astype(BF16)]

    def stacked(values):
        return jnp.concatenate([values * keep[0], values * keep[1]], axis=0)

    def head_mean(values):
        mean0 = jnp.sum(jnp.where(low_half, values, 0.0), axis=-1, keepdims=True) / DH
        mean1 = jnp.sum(jnp.where(low_half, 0.0, values), axis=-1, keepdims=True) / DH
        return jnp.where(low_half, mean0, mean1)

    def attention(dproj, a_ref):
        a_load = load(a_in, a_ref)

        def inner(qkv, u_ref, o_ref, p_ref, wo, gain):
            copies = [
                load(src, dst)
                for src, dst in (
                    (wo_in, wo), (u_in, u_ref), (o_in, o_ref), (p_in, p_ref), (qkv_in, qkv), (gain_in, gain)
                )
            ]
            pl.run_scoped(hidden_grads, pltpu.VMEM((T, D), F32))
            for copy in copies:
                copy.wait()
            gacc[...] = jnp.zeros_like(gacc)
            pl.run_scoped(out_grads, pltpu.VMEM((2, TT, wide), BF16))
            pl.run_scoped(functools.partial(heads, qkv, u_ref, o_ref, p_ref, wo, gain), pltpu.VMEM((TT, wide), F32))

        def hidden_grads(h_ref):
            for copy in (load(h_in, h_ref), load(cot_in.at[pl.ds(0, T), :], es_da)):
                copy.wait()
            for t in range(T // 256):
                swap(t).wait_recv()

                def rows_body(r):
                    rows = rows_of(t * 256 + r * 64, 64)
                    db = dh[rows, :] + hr[rows, :]
                    h = h_ref[rows, :]
                    factor = rms_factor(h)
                    normed = h * factor
                    grad = es_da[rows, :].astype(F32) + factor * (
                        db - normed * jnp.mean(db * normed, axis=-1, keepdims=True)
                    )
                    dh[rows, :] = grad
                    dhl[rows, :] = grad.astype(BF16)

                loop(4, rows_body)
                swap_low(t).start()
                checkpoint()
        def out_grads(z_ref):
            z_load = load(z_in, z_ref)
            for t in range(T // 256):
                swap_low(t).wait_recv()
            z_load.wait()
            for j in (0, 1):
                gb[2][j] = dot_tn(z_ref[j], dhl[...]).astype(BF16)
                send(2, j)
                checkpoint()

        def heads(qkv, u_ref, o_ref, p_ref, wo, gain, dz_ref):
            for j in (0, 1):
                def dz_rows(t):
                    rows = rows_of(t * 256, 256)
                    dz_ref[rows, :] = dot_nt(dhl[rows, :], wo[j])

                loop(TT // 256, dz_rows)

                def unit(t):
                    rows = rows_of(t * UNIT, UNIT)
                    for pair in range(wide // UNIT):
                        cols = pl.ds(pair * UNIT, UNIT)
                        q, k, v = (qkv[j, rows, pl.ds(f * wide + pair * UNIT, UNIT)] for f in range(3))
                        o, u, dz = o_ref[j, rows, cols], u_ref[j, rows, cols], dz_ref[rows, cols]
                        gain_row = gain[j, :, cols]
                        factor = lax.rsqrt(head_mean(o * o) + EPSILON)
                        normed = o * factor
                        s = jax.nn.sigmoid(u)
                        act = u * s
                        dzn = dz * normed
                        gacc[j, :, cols] += jnp.sum((dzn * act).reshape(UNIT // 8, 8, UNIT), axis=0)
                        du = (dzn * gain_row * s * (1.0 + u * (1.0 - s))).astype(BF16)
                        dn = dz * act * gain_row
                        do = stacked((factor * (dn - normed * head_mean(dn * normed))).astype(BF16))
                        soft_low = p_ref[j, pair, t]
                        soft = soft_low.astype(F32)
                        dv = dot_tn(soft_low, do)
                        dp = dot_nt(do, v)
                        ds = (soft * (dp - jnp.sum(dp * soft, axis=-1, keepdims=True))).astype(BF16)
                        dq = dot(jnp.concatenate([ds[:UNIT], ds[UNIT:]], axis=1), stacked(k)) * DH ** (-0.5)
                        dk = dot_tn(ds, stacked(q)) * DH ** (-0.5)
                        for f, value in enumerate((dq, dk, dv)):
                            dproj[j, rows, pl.ds(f * wide + pair * UNIT, UNIT)] = value.astype(BF16)
                        dproj[j, rows, pl.ds(3 * wide + pair * UNIT, UNIT)] = du

                for part in range(2):
                    loop(TT // UNIT // 2, lambda t: unit(t + part * (TT // UNIT // 2)))
                    checkpoint()
                if j == 0:
                    a_load.wait()
                for i in (0, 1):
                    def block(t):
                        rows = pl.ds(pl.multiple_of(t * 256, 256), 256)
                        cols = pl.ds(i * 2 * wide, 2 * wide)
                        gb[i][j, rows, :] = dot_tn(a_ref[:, rows], dproj[j, :, cols]).astype(BF16)

                    loop(D // 256, block)
                    send(i, j)
                    checkpoint()

        pl.run_scoped(
            inner,
            pltpu.VMEM((2, TT, 3 * wide), BF16),
            pltpu.VMEM((2, TT, wide), F32),
            pltpu.VMEM((2, TT, wide), F32),
            pltpu.VMEM((2, wide // UNIT, TT // UNIT, 2 * UNIT, UNIT), BF16),
            pltpu.VMEM((2, wide, D), BF16),
            pltpu.VMEM((2, 1, wide), F32),
        )

        def inputs_part(w0, x_ref):
            for copy in (load(w0_in, w0), load(x_in, x_ref)):
                copy.wait()

            def da_rows(row):
                rows = rows_of(row, 256)
                return dot_nt(dproj[0, rows, :], w0[0]) + dot_nt(dproj[1, rows, :], w0[1])

            for t in range(T // 256):
                es_da[pl.ds(t * 256, 256), :] = da_rows(T + t * 256).astype(BF16)
                swap_da(t).start()
                checkpoint()
            for t in range(T // 256):
                hs[pl.ds(t * 256, 256), :] = da_rows(t * 256)
                checkpoint()
            for t in range(T // 256):
                swap_da(t).wait_recv()

                def rows_body(r):
                    rows = rows_of(t * 256 + r * 64, 64)
                    da = hs[rows, :] + er_da[rows, :].astype(F32)
                    x = x_ref[rows, :].astype(F32)
                    factor = rms_factor(x)
                    normed = x * factor
                    dh[rows, :] = dh[rows, :] + factor * (
                        da - normed * jnp.mean(da * normed, axis=-1, keepdims=True)
                    )

                loop(4, rows_body)
                checkpoint()

        for t in range(T // 256):
            swap(t).wait_send()
        pl.run_scoped(inputs_part, pltpu.VMEM((2, D, 4 * wide), BF16), pltpu.VMEM((T, D), BF16))

    pl.run_scoped(attention, pltpu.VMEM((2, TT, 4 * wide), BF16), pltpu.VMEM((TT, D), BF16))
    dx_save = load(dh, dx_out)

    def gain_sum(k, src, dst, device, total):
        copy = remote(src, dst, gss.at[k], grs.at[k], device)
        copy.start()
        copy.wait()
        total[...] += dst[...]

    gain_sum(0, gacc, gx, me.xn, gacc)
    checkpoint()
    gain_sum(1, gacc, gy, me.yn, gacc)

    def gain_z(j):
        slot = lax.rem(z - (2 * c + j) + 3 + 4, 4)
        return remote(gacc.at[j], gz.at[slot], gss.at[2 + j], grs.at[4 + slot], (me.dp, 2 * c + j))

    for j in (0, 1):
        @pl.when(z != 2 * c + j)
        def _():
            gain_z(j).start()

    def output_part(m_ref, w3, stage):
        for copy in (load(m_in, m_ref), load(w3_in, w3), load(h_in, stage)):
            copy.wait()
        for t in range(T // 256):
            swap_da(t).wait_send()

        def out_rows(row):
            rows = rows_of(row, 256)
            return dot(m_ref[0, rows, :], w3[0]) + dot(m_ref[1, rows, :], w3[1])

        for t in range(T // 256):
            es_da[pl.ds(t * 256, 256), :] = out_rows(T + t * 256).astype(BF16)
            swap_out(t).start()
            checkpoint()
        for t in range(T // 256):
            rows = pl.ds(t * 256, 256)
            stage[rows, :] = stage[rows, :] + out_rows(t * 256)
            checkpoint()
        for t in range(T // 256):
            swap_out(t).wait_recv()
            rows = pl.ds(t * 256, 256)
            stage[rows, :] = stage[rows, :] + er_out[rows, :].astype(F32)

        load(stage, out_out).wait()

    pl.run_scoped(
        output_part, pltpu.VMEM((2, TT, hidden), BF16), pltpu.VMEM((2, hidden, D), BF16), pltpu.VMEM((T, D), F32)
    )

    def gain_final():
        return remote(gain_sent, gain_out, gss.at[7], grs.at[7], me.sib)

    @pl.when(innet)
    def _():
        for slot in range(3):
            remote(gz.at[slot], gz.at[slot], gss.at[2], grs.at[4 + slot], me.sib).wait_recv()
            gacc[own] += gz[slot]
        for e in range(spare):
            copy = remote(gacc.at[own], gq.at[e], gss.at[8 + e], grs.at[8 + e], other_quad(e))
            copy.start()
            copy.wait()
            gacc[own] += gq[e]
        gain_sent[...] = jnp.sum(gacc[own], axis=0, keepdims=True)
        local = pltpu.make_async_copy(gain_sent, gain_out, ld.at[39])
        local.start()
        gain_final().start()
        local.wait()
        gain_final().wait_send()

    checkpoint()

    @pl.when(jnp.logical_not(innet))
    def _():
        gain_final().wait_recv()
        for i in arrays:
            spread(i, 0)[0][2].wait_recv()
            pass_x(i)[1].wait_recv()
            pass_y(i)[1].wait_recv()
            for copy in pass_last(i):
                copy.wait_recv()

    @pl.when(innet)
    def _():
        for i in arrays:
            for copy in (pass_x(i)[1], pass_y(i)[1]) + pass_last(i):
                copy.wait_send()

    for j in (0, 1):
        @pl.when(z != 2 * c + j)
        def _():
            gain_z(j).wait_send()

    for t in range(T // 256):
        swap_low(t).wait_send()
        swap_out(t).wait_send()
    dx_save.wait()


def run_backward(x, kept, spare):
    T, D = x.shape
    TT = 2 * T
    w0, wo, w1, w2, w3 = kept[:5]
    wide, hidden = wo.shape[1], w1.shape[1]
    shapes = [(D, 2 * wide), (D, 2 * wide)] + [w.shape[1:] for w in (wo, w1, w2, w3)]
    q = [s[0] // 4 for s in shapes]
    h = [half_of(n) for n in q]
    cols = [s[1] for s in shapes]
    n = range(6)
    lands = [2] * 6
    extra = max(spare, 1)
    vmem = (
        [pltpu.VMEM((2,) + s, BF16) for s in shapes]
        + [pltpu.VMEM((lands[i], 2, h[i], cols[i]), BF16) for i in n]
        + [pltpu.VMEM((lands[i], 2, q[i] - h[i], cols[i]), BF16) for i in n]
        + [pltpu.VMEM((lands[i], h[i], cols[i]), BF16) for i in n]
        + [pltpu.VMEM((lands[i], q[i] - h[i], cols[i]), BF16) for i in n]
        + [pltpu.VMEM((3, q[i] if i < 5 else 4 * q[i], cols[i]), BF16) for i in n]
        + [
            pltpu.VMEM((T, D), F32),
            pltpu.VMEM((T, D), F32),
            pltpu.VMEM((T, D), BF16),
            pltpu.VMEM((T, D), BF16),
            pltpu.VMEM((T, D), BF16),
            pltpu.VMEM((T, D), F32),
            pltpu.VMEM((TT, D), BF16),
            pltpu.VMEM((2, 8, wide), F32),
            pltpu.VMEM((2, 8, wide), F32),
            pltpu.VMEM((2, 8, wide), F32),
            pltpu.VMEM((3, 8, wide), F32),
            pltpu.VMEM((extra, 8, wide), F32),
            pltpu.VMEM((1, wide), F32),
        ]
    )
    dma = pltpu.SemaphoreType.DMA
    sems = [
        dma((6, 2, 4)), dma((6, 2, 4)), dma((6, 2, 2)), dma((6, 2, 2)), dma((6, 2)), dma((6, 3)),
        dma((6,)), dma((6,)), dma((6,)), dma((6,)), dma((6, 2)), dma((6, 2)), dma((6, 5)), dma((6, 5)),
        dma((6, 2 + extra)), dma((6, extra)), dma((40,)), dma((8,)), dma((8,)), dma((8 + extra,)), dma((8 + extra,)),
    ]
    outs = [((T, D), F32), ((T, D), F32)] + [(s, BF16) for s in shapes] + [((1, wide), F32)]
    if spare:
        outs += [((spare, q[i], cols[i]), BF16) for i in n]
    return pl.pallas_call(
        functools.partial(backward_kernel, shapes, spare),
        out_shape=[jax.ShapeDtypeStruct(s, t) for s, t in outs],
        in_specs=any_spec(1 + len(kept)),
        out_specs=any_spec(len(outs)),
        scratch_shapes=vmem + sems,
        compiler_params=pltpu.CompilerParams(collective_id=1, has_side_effects=True, vmem_limit_bytes=VMEM_LIMIT),
        cost_estimate=pl.CostEstimate(flops=30 * 10**9, bytes_accessed=80 * 10**6, transcendentals=10**6),
        name="backward",
    )(x, *kept)


def finish_kernel(wide, *refs):
    ready, grads = refs[:2], refs[2:8]
    ready_out, outs = refs[8:10], refs[10:18]
    low, full = refs[18:24], refs[24:30]
    held = refs[30:32]
    sems, done = refs[32:]
    loads = [pltpu.make_async_copy(src, dst, sems.at[i]) for i, (src, dst) in enumerate(zip(grads, low))]
    moves = [pltpu.make_async_copy(src, dst, sems.at[6 + i]) for i, (src, dst) in enumerate(zip(ready, held))]
    for copy in loads[:1] + moves + loads[1:]:
        copy.start()
    saves = []

    def hand_out(i):
        moves[i].wait()
        copy = pltpu.make_async_copy(held[i], ready_out[i], done.at[8 + i])
        copy.start()
        saves.append(copy)
    for i in range(6):
        loads[i].wait()

        def widen(t, carry):
            rows = rows_of(t * 64, 64)
            full[i][rows, :] = low[i][rows, :].astype(F32)
            return carry

        lax.fori_loop(0, low[i].shape[0] // 64, widen, 0)
        if i < 2:
            parts = [(full[i].at[:, pl.ds(n * wide, wide)], outs[2 * i + n], done.at[2 * i + n]) for n in range(2)]
        else:
            parts = [(full[i], outs[2 + i], done.at[2 + i])]
        for part in parts:
            copy = pltpu.make_async_copy(*part)
            copy.start()
            saves.append(copy)
        if i < 2:
            hand_out(i)
    for copy in saves:
        copy.wait()


def run_finish(ready, grads, wide):
    shapes = [g.shape for g in grads]
    outs = [r.shape for r in ready] + [(shapes[0][0], wide)] * 4 + shapes[2:]
    return pl.pallas_call(
        functools.partial(finish_kernel, wide),
        out_shape=[jax.ShapeDtypeStruct(s, F32) for s in outs],
        in_specs=any_spec(8),
        out_specs=any_spec(len(outs)),
        scratch_shapes=[pltpu.VMEM(s, BF16) for s in shapes]
        + [pltpu.VMEM(s, F32) for s in shapes]
        + [pltpu.VMEM(r.shape, F32) for r in ready]
        + [pltpu.SemaphoreType.DMA((8,)), pltpu.SemaphoreType.DMA((10,))],
        compiler_params=pltpu.CompilerParams(vmem_limit_bytes=VMEM_LIMIT),
        cost_estimate=pl.CostEstimate(flops=0, bytes_accessed=30 * 10**6, transcendentals=0),
        name="finish",
    )(*ready, *grads)


def shards(
    inputs, w_query, w_key, w_value, w_gate, head_gain, w_out, w_first, w_second, w_third, cotangent
):
    wide = w_query.shape[1]
    weights = [w_query, w_key, w_value, w_gate, w_out, w_first.T, w_second.T, w_third]
    gain = head_gain.reshape(1, wide)
    kept = run_forward(inputs, cotangent, gain, weights)
    spare = (lax.axis_size("dp") // 8).bit_length() - 1
    results = run_backward(inputs, kept, spare)
    output, grad_inputs, *grads = run_finish(results[:2], results[2:8], wide)
    g_query, g_key, g_value, g_gate, g_out, g_first, g_second, g_third = grads
    g_gain = results[8].reshape(wide)
    return (
        output, grad_inputs, g_query, g_key, g_value, g_gate, g_gain, g_out, g_first.T, g_second.T, g_third
    )


def solution(mesh):
    rows, columns = P(("dp", "mp"), None), P(None, "mp")
    heads = P("mp", None)
    return jax.shard_map(
        shards,
        mesh=mesh,
        in_specs=(rows, columns, columns, columns, columns, P("mp"), heads, columns, columns, heads, rows),
        out_specs=(rows, rows, columns, columns, columns, columns, P("mp"), heads, columns, columns, heads),
        check_vma=False,
    )
```

```python
import functools

import jax
import jax.numpy as jnp
from jax import lax
from jax.experimental import pallas as pl
from jax.experimental.pallas import tpu as pltpu
from jax.sharding import PartitionSpec as P

DH = 64
BLK = 64
EPSILON = 1e-06
MESH = pl.DeviceIdType.MESH
F32 = jnp.float32
BF16 = jnp.bfloat16
UNIT = 128
VMEM_LIMIT = 61 * 2**20


GATHER = (
    (0, 1, 2, 3, 4, 16, 17, 18, 19,),
    (5, 33,),
    (32,),
    (),
    (34, 35,),
    (),
    (7,),
    (6,),
    (20,),
    (9,),
    (8,),
    (10,),
    (23, 22, 21,),
    (),
    (11,),
    (36,),
    (),
    (25,),
    (),
    (),
    (24, 26,),
    (),
    (),
    (38, 12, 37, 39,),
    (13, 27,),
    (42, 40, 41,),
    (28,),
    (29,),
    (),
    (),
    (),
    (),
    (43,),
    (44,),
    (45,),
)
LEAD = 3


def rms_factor(values):
    return lax.rsqrt(jnp.mean(values * values, axis=-1, keepdims=True) + EPSILON)


def dot(left, right):
    return jnp.dot(left, right, preferred_element_type=F32)


def dot_tn(left, right):
    return lax.dot_general(left, right, (((0,), (0,)), ((), ())), preferred_element_type=F32)


def dot_nt(left, right):
    return lax.dot_general(left, right, (((1,), (1,)), ((), ())), preferred_element_type=F32)


def remote(src, dst, send, recv, device):
    return pltpu.make_async_remote_copy(src, dst, send, recv, device_id=device, device_id_type=MESH)


def rows_of(start, count):
    return pl.ds(pl.multiple_of(start, 16), count)


class Place:
    def __init__(self):
        dp, self.z = lax.axis_index("dp"), lax.axis_index("mp")
        self.dp = dp
        self.c = dp % 2
        self.bx, self.by = (dp // 2) % 2, (dp // 4) % 2
        self.p = self.by * 2 + self.bx
        self.px, self.py = self.by * 2 + 1 - self.bx, (1 - self.by) * 2 + self.bx
        self.pd = (1 - self.by) * 2 + 1 - self.bx
        self.sib = (dp + 1 - 2 * self.c, self.z)
        self.xn = (dp + 2 - 4 * self.bx, self.z)
        self.yn = (dp + 4 - 8 * self.by, self.z)
        self.own = self.z % 2
        self.innet = self.z // 2 == self.c

    def up(self):
        return (self.dp, self.z + 1)

    def down(self):
        return (self.dp, self.z - 1)


def half_of(count):
    return (count // 2 + 15) // 16 * 16


def gather_plan(shapes):
    plan = []
    for i, (rows, _) in enumerate(shapes):
        quarter = rows // 4
        if i < 4:
            parts = [quarter]
        elif i == 4:
            parts = [quarter]
        else:
            third = (quarter // 3 + 15) // 16 * 16
            parts = [third, third, quarter - 2 * third]
        start = 0
        for count in parts:
            plan.append((i, max(i - 3, 0), i * shapes[0][1] if i < 4 else 0, start, count))
            start += count
    return plan


def forward_kernel(plan, shapes, *refs):
    nw = 8
    x_in, cot_in, gain_in = refs[:3]
    w_in = refs[3 : 3 + nw]
    outs = refs[3 + nw : 3 + nw + 19]
    (w_out, a_out, qkv_out, u_out, o_out, p_out, z_out, h_out, b_out, m_out, d1_out, d2_out, cot_out, gain_out, g3_out) = (
        outs[:5], *outs[5:]
    )
    scratch = refs[3 + nw + 19 :]
    bufs = scratch[:5]
    (x_ref, cot, a_ref, qkv, u_ref, o_ref, p_ref, z_ref, hs, hr, h_ref, b_ref, m_ref, d1, d2, gain, g3) = scratch[5:22]
    (zs, zr, fzs, xs, xr, ys, yr, fs, fr, loc, gs, gr, es, er, sv) = scratch[22:]
    me = Place()
    z, c, own, innet = me.z, me.c, me.own, me.innet
    T = x_in.shape[0]
    TT = 2 * T
    count = len(plan)
    wide = shapes[0][1]

    bar = pltpu.get_barrier_semaphore()
    for d in (me.sib, me.xn, me.yn):
        pl.semaphore_signal(bar, inc=1, device_id=d, device_id_type=MESH)

    @pl.when(z < 3)
    def _():
        pl.semaphore_signal(bar, inc=1, device_id=me.up(), device_id_type=MESH)

    @pl.when(z > 0)
    def _():
        pl.semaphore_signal(bar, inc=1, device_id=me.down(), device_id_type=MESH)

    pl.semaphore_wait(bar, 3 + jnp.where(z < 3, 1, 0) + jnp.where(z > 0, 1, 0))

    def z_only(k):
        return plan[k][4] == shapes[plan[k][0]][0]

    def piece(k, who):
        i, _, _, start, rows = plan[k]
        return (0 if z_only(k) else who * (shapes[i][0] // 4) + start), rows

    def part(j, k, row, rows):
        _, buf, col, _, _ = plan[k]
        ref = bufs[buf]
        if buf:
            return ref.at[j, rows_of(row, rows), :]
        return ref.at[j, rows_of(row, rows), pl.ds(col, wide)]

    def z_first(k, d):
        row, rows = piece(k, me.p)
        src = w_in[plan[k][0]].at[rows_of(row, rows), :]
        return remote(src, part(own, k, row, rows), zs.at[k, d], zr.at[k, own], (me.dp, z + 1 - 2 * d))

    def z_next(k, j, d):
        row, rows = piece(k, me.p)
        r = part(j, k, row, rows)
        return remote(r, r, fzs.at[k, j], zr.at[k, j], (me.dp, z + 1 - 2 * d))

    def to_x(k, j):
        row, rows = piece(k, me.p)
        r = part(j, k, row, rows)
        return remote(r, r, xs.at[k, j], xr.at[k, j], me.xn)

    def to_y(k, j):
        row, rows = piece(k, me.p)
        r = part(j, k, row, rows)
        return remote(r, r, ys.at[k, j], yr.at[k, j], me.yn)

    def x_then_y(k, j):
        row, rows = piece(k, me.px)
        r = part(j, k, row, half_of(rows))
        return remote(r, r, fs.at[0, k, j], fr.at[0, k, j], me.yn)

    def y_then_x(k, j):
        row, rows = piece(k, me.py)
        h = half_of(rows)
        r = part(j, k, row + h, rows - h)
        return remote(r, r, fs.at[1, k, j], fr.at[1, k, j], me.xn)

    def gain_copy(j, d, src):
        return remote(src, gain.at[j], gs.at[j, d], gr.at[j], (me.dp, z + 1 - 2 * d))

    def own_copies():
        copies = []
        for i in range(nw):
            dst = bufs[i - 3].at[own] if i > 3 else bufs[0].at[own, :, pl.ds(i * wide, wide)]
            copies.append(pltpu.make_async_copy(w_in[i], dst, loc.at[i]))
        copies.append(pltpu.make_async_copy(gain_in, gain.at[own], loc.at[nw]))
        return copies

    both = [
        remote(x_in, x_ref.at[pl.ds(T, T), :], es.at[0], er.at[0], me.sib),
        remote(cot_in, cot.at[pl.ds(T, T), :], es.at[1], er.at[1], me.sib),
    ]
    mine = [
        pltpu.make_async_copy(x_in, x_ref.at[pl.ds(0, T), :], loc.at[nw + 1]),
        pltpu.make_async_copy(cot_in, cot.at[pl.ds(0, T), :], loc.at[nw + 2]),
    ]
    mine[0].start()
    both[0].start()

    order = [code for codes in GATHER for code in codes if code < 16]

    def z_starts(k):
        @pl.when(z < 3)
        def _():
            z_first(k, 0).start()

        @pl.when(z > 0)
        def _():
            z_first(k, 1).start()

    @pl.when(innet)
    def _():
        @pl.when(z < 3)
        def _():
            gain_copy(own, 0, gain_in).start()

        @pl.when(z > 0)
        def _():
            gain_copy(own, 1, gain_in).start()

        for k in order[:LEAD]:
            z_starts(k)
        for copy in own_copies():
            copy.start()

    mine[1].start()
    both[1].start()

    def upward(j):
        return (z > 2 * c + j) & (z < 3)

    def downward(j):
        return (z < 2 * c + j) & (z > 0)

    def others(step, *args):
        for j in (0, 1):
            @pl.when(z != 2 * c + j)
            def _():
                step(*args, j)

    def step_gain(j):
        remote(gain.at[j], gain.at[j], gs.at[j, 0], gr.at[j], me.sib).wait_recv()

        @pl.when(upward(j))
        def _():
            gain_copy(j, 0, gain.at[j]).start()

        @pl.when(downward(j))
        def _():
            gain_copy(j, 1, gain.at[j]).start()

    def step_a(k, j):
        row, rows = piece(k, me.p)
        r = part(j, k, row, rows)
        remote(r, r, fzs.at[k, j], zr.at[k, j], me.sib).wait_recv()

        @pl.when(upward(j))
        def _():
            z_next(k, j, 0).start()

        @pl.when(downward(j))
        def _():
            z_next(k, j, 1).start()

        if not z_only(k):
            to_x(k, j).start()
            to_y(k, j).start()

    def step_b(k, j):
        to_x(k, j).wait_recv()
        x_then_y(k, j).start()
        to_y(k, j).wait_recv()
        y_then_x(k, j).start()

    def step_c(k, j):
        x_then_y(k, j).wait_recv()
        y_then_x(k, j).wait_recv()
        for copy in (to_x, to_y, x_then_y, y_then_x):
            copy(k, j).wait_send()

    mark = [0]

    def checkpoint():
        for code in GATHER[mark[0]]:
            others((step_a, step_b, step_c)[code // 16], code % 16)
            after = order.index(code) + LEAD if code < 16 else count
            if after < count:
                pl.when(innet)(functools.partial(z_starts, order[after]))
        mark[0] += 1

    saves = []

    def save(src, dst):
        copy = pltpu.make_async_copy(src, dst, sv.at[len(saves)])
        copy.start()
        saves.append(copy)

    checkpoint()
    mine[0].wait()
    both[0].wait_recv()
    checkpoint()

    def norm_rows(t, carry):
        rows = rows_of(t * UNIT, UNIT)
        values = x_ref[rows, :].astype(F32)
        a_ref[rows, :] = (values * rms_factor(values)).astype(BF16)
        return carry

    for n in range(2):
        lax.fori_loop(n * TT // UNIT // 2, (n + 1) * TT // UNIT // 2, norm_rows, 0)
        checkpoint()
    save(a_ref, a_out)

    @pl.when(innet)
    def _():
        for copy in own_copies():
            copy.wait()

    others(step_gain)

    lane = lax.broadcasted_iota(jnp.int32, (UNIT, UNIT), 1)
    low_half = lane < DH
    keep = [low_half.astype(F32).astype(BF16), (lane >= DH).astype(F32).astype(BF16)]
    row2 = lax.broadcasted_iota(jnp.int32, (2 * UNIT, UNIT), 0) % UNIT
    col2 = lax.broadcasted_iota(jnp.int32, (2 * UNIT, UNIT), 1)
    seen = (row2 // BLK == col2 // BLK) & (col2 <= row2)

    def attend(j):
        def project(r, carry):
            rows = rows_of(r * 256, 256)
            acc = dot(a_ref[rows, :], bufs[0][j])
            qkv[j, rows, :] = acc[:, : 3 * wide].astype(BF16)
            u_ref[j, rows, :] = acc[:, 3 * wide :]
            return carry

        lax.fori_loop(0, TT // 256, project, 0)
        checkpoint()

        def unit(t, carry):
            rows = rows_of(t * UNIT, UNIT)
            for pair in range(wide // UNIT):
                q, k, v = (qkv[j, rows, pl.ds(f * wide + pair * UNIT, UNIT)] for f in range(3))
                cols = pl.ds(pair * UNIT, UNIT)
                scores = dot_nt(jnp.concatenate([q * keep[0], q * keep[1]], axis=0), k) * DH ** (-0.5)
                scores = jnp.where(seen, scores, -1e30)
                shifted = jnp.exp(scores - jnp.max(scores, axis=-1, keepdims=True))
                soft = (shifted / jnp.sum(shifted, axis=-1, keepdims=True)).astype(BF16)
                p_ref[j, pair, t] = soft
                attended = dot(
                    jnp.concatenate([soft[:UNIT], soft[UNIT:]], axis=1),
                    jnp.concatenate([v * keep[0], v * keep[1]], axis=0),
                )
                o_ref[j, rows, cols] = attended
                square = attended * attended
                mean0 = jnp.sum(jnp.where(low_half, square, 0.0), axis=-1, keepdims=True) / DH
                mean1 = jnp.sum(jnp.where(low_half, 0.0, square), axis=-1, keepdims=True) / DH
                normed = attended * lax.rsqrt(jnp.where(low_half, mean0, mean1) + EPSILON)
                u = u_ref[j, rows, cols]
                g = gain[j, :, cols]
                z_ref[j, rows, cols] = (normed * g * (u * jax.nn.sigmoid(u))).astype(BF16)
            return carry

        span = TT // UNIT // 4
        for n in range(4):
            lax.fori_loop(n * span, n * span + span, unit, 0)
            checkpoint()

    checkpoint()
    attend(0)
    attend(1)
    checkpoint()
    for src, dst in ((qkv, qkv_out), (u_ref, u_out), (o_ref, o_out), (p_ref, p_out), (z_ref, z_out), (gain, gain_out)):
        save(src, dst)
    save(bufs[0], w_out[0])
    save(bufs[1], w_out[1])

    def out_rows(row):
        rows = rows_of(row, 256)
        return dot(z_ref[0, rows, :], bufs[1][0]) + dot(z_ref[1, rows, :], bufs[1][1])

    swaps = []
    for i in range(T // 256):
        hs[pl.ds(i * 256, 256), :] = out_rows(T + i * 256)
        part_rows = pl.ds(i * 256, 256)
        swaps.append(remote(hs.at[part_rows, :], hr.at[part_rows, :], es.at[2 + i], er.at[2 + i], me.sib))
        swaps[-1].start()
        checkpoint()
    for i in range(T // 256):
        h_ref[pl.ds(i * 256, 256), :] = x_ref[pl.ds(i * 256, 256), :].astype(F32) + out_rows(i * 256)
        checkpoint()
    checkpoint()
    for i, swap in enumerate(list(swaps)):
        swap.wait_recv()

        def add_rows(t, carry):
            rows = rows_of(i * 256 + t * UNIT, UNIT)
            values = h_ref[rows, :] + hr[rows, :]
            h_ref[rows, :] = values
            b_ref[rows, :] = (values * rms_factor(values)).astype(BF16)
            return carry

        lax.fori_loop(0, 256 // UNIT, add_rows, 0)
        b_rows = pl.ds(i * 256, 256)
        swaps.append(remote(b_ref.at[b_rows, :], b_ref.at[pl.ds(T + i * 256, 256), :], es.at[4 + i], er.at[4 + i], me.sib))
        swaps[-1].start()
        checkpoint()
    save(h_ref, h_out)
    for swap in swaps[len(swaps) // 2 :]:
        swap.wait_recv()
    save(b_ref, b_out)

    def rows_loop(body):
        lax.fori_loop(0, TT // 256, lambda r, carry: (body(rows_of(r * 256, 256)), carry)[1], 0)

    checkpoint()
    save(bufs[2], w_out[2])
    for j in (0, 1):
        def first(rows):
            d2[j, rows, :] = dot_nt(b_ref[rows, :], bufs[2][j]).astype(BF16)

        rows_loop(first)
        checkpoint()
    save(bufs[3], w_out[3])
    for j in (0, 1):
        def second(rows):
            g2 = dot_nt(b_ref[rows, :], bufs[3][j])
            d1[j, rows, :] = g2.astype(BF16)
            m_ref[j, rows, :] = (d2[j, rows, :].astype(F32) * g2).astype(BF16)

        rows_loop(second)
        checkpoint()
    for src, dst in ((m_ref, m_out), (d1, d1_out), (d2, d2_out)):
        save(src, dst)
    mine[1].wait()
    both[1].wait_recv()
    save(cot, cot_out)
    hidden = m_ref.shape[2]
    for j in (0, 1):
        for start in range(0, hidden, 256):
            size = min(256, hidden - start)
            g3[j, pl.ds(start, size), :] = dot_tn(m_ref[j, :, pl.ds(start, size)], cot[...]).astype(BF16)
            checkpoint()
    save(g3, g3_out)
    checkpoint()
    save(bufs[4], w_out[4])

    @pl.when(innet)
    def _():
        for d, inside in ((0, z < 3), (1, z > 0)):
            @pl.when(inside)
            def _():
                gain_copy(own, d, gain_in).wait_send()
                for k in range(count):
                    z_first(k, d).wait_send()

    def ends(j):
        @pl.when(upward(j) | downward(j))
        def _():
            for k in range(count):
                z_next(k, j, 0).wait_send()

        @pl.when(upward(j))
        def _():
            gain_copy(j, 0, gain.at[j]).wait_send()

        @pl.when(downward(j))
        def _():
            gain_copy(j, 1, gain.at[j]).wait_send()

    others(ends)
    for copy in both + swaps:
        copy.wait_send()
    for copy in saves:
        copy.wait()


def any_spec(count):
    return [pl.BlockSpec(memory_space=pl.ANY)] * count


def run_forward(x, cot, gain, weights):
    T, D = x.shape
    TT = 2 * T
    shapes = [w.shape for w in weights]
    plan = gather_plan(shapes)
    wide, hidden = shapes[0][1], shapes[5][0]
    units, pairs = TT // UNIT, wide // UNIT
    buffers = [(2, D, 4 * wide), (2, wide, D), (2, hidden, D), (2, hidden, D), (2, hidden, D)]
    kept = [
        ((TT, D), BF16),
        ((2, TT, 3 * wide), BF16),
        ((2, TT, wide), F32),
        ((2, TT, wide), F32),
        ((2, pairs, units, 2 * UNIT, UNIT), BF16),
        ((2, TT, wide), BF16),
        ((T, D), F32),
        ((TT, D), BF16),
        ((2, TT, hidden), BF16),
        ((2, TT, hidden), BF16),
        ((2, TT, hidden), BF16),
        ((TT, D), BF16),
        ((2, 1, wide), F32),
        ((2, hidden, D), BF16),
    ]
    vmem = [pltpu.VMEM(s, BF16) for s in buffers] + [
        pltpu.VMEM((TT, D), BF16),
        pltpu.VMEM((TT, D), BF16),
        pltpu.VMEM((TT, D), BF16),
        pltpu.VMEM((2, TT, 3 * wide), BF16),
        pltpu.VMEM((2, TT, wide), F32),
        pltpu.VMEM((2, TT, wide), F32),
        pltpu.VMEM((2, pairs, units, 2 * UNIT, UNIT), BF16),
        pltpu.VMEM((2, TT, wide), BF16),
        pltpu.VMEM((T, D), F32),
        pltpu.VMEM((T, D), F32),
        pltpu.VMEM((T, D), F32),
        pltpu.VMEM((TT, D), BF16),
        pltpu.VMEM((2, TT, hidden), BF16),
        pltpu.VMEM((2, TT, hidden), BF16),
        pltpu.VMEM((2, TT, hidden), BF16),
        pltpu.VMEM((2, 1, wide), F32),
        pltpu.VMEM((2, hidden, D), BF16),
    ]
    n = len(plan)
    dma = pltpu.SemaphoreType.DMA
    sems = [dma((n, 2))] * 7 + [dma((2, n, 2))] * 2 + [dma((11,)), dma((2, 2)), dma((2,)), dma((6,)), dma((6,)), dma((24,))]
    return pl.pallas_call(
        functools.partial(forward_kernel, plan, shapes),
        out_shape=[jax.ShapeDtypeStruct(s, BF16) for s in buffers] + [jax.ShapeDtypeStruct(s, t) for s, t in kept],
        in_specs=any_spec(3 + len(weights)),
        out_specs=any_spec(len(buffers) + len(kept)),
        scratch_shapes=vmem + sems,
        compiler_params=pltpu.CompilerParams(collective_id=0, has_side_effects=True, vmem_limit_bytes=VMEM_LIMIT),
        cost_estimate=pl.CostEstimate(flops=16 * 10**9, bytes_accessed=80 * 10**6, transcendentals=10**6),
        name="forward",
    )(x, cot, gain, *weights)


SCHEDULE = (
    (16,),
    (),
    (),
    (),
    (18,),
    (),
    (),
    (),
    (),
    (19,),
    (),
    (),
    (),
    (21,),
    (34,),
    (),
    (35, 32, 20,),
    (),
    (),
    (),
    (24,),
    (),
    (37,),
    (),
    (),
    (36,),
    (),
    (26,),
    (),
    (),
    (),
    (1, 22, 53, 40, 17, 27, 25, 48, 69, 23, 42, 38, 50, 33, 58, 51, 52, 43, 41, 64, 59, 39, 74, 66, 55, 56, 67, 68, 75, 65, 71, 80, 54, 57, 91, 85, 81, 84, 90, 87, 83, 72, 70, 73, 88, 82, 86, 89,),
)
Z_FIRST = 1


def backward_kernel(shapes, spare, *refs):
    (x_in, w0_in, wo_in, w1_in, w2_in, w3_in, a_in, qkv_in, u_in, o_in, p_in, z_in, h_in, b_in, m_in, d1_in, d2_in) = refs[:17]
    cot_in, gain_in, g3_in = refs[17:20]
    out_out, dx_out = refs[20:22]
    final = refs[22:28]
    gain_out = refs[28]
    scratch = refs[29:]
    if spare:
        rq, scratch = scratch[:6], scratch[6:]
    gb, ra1, rb1, ra2, rb2, rz = (scratch[6 * i : 6 * i + 6] for i in range(6))
    (hs, hr, es_da, er_da, er_out, dh, dhl, gacc, gx, gy, gz, gq, gain_sent) = scratch[36:49]
    (s1, r1, s2, r2, sz, rzs, sx, rx, sy, ry, sf, rf, ss, rs, sq, rqs, ld, es, er, gss, grs) = scratch[49:]
    me = Place()
    z, c, own, innet, p = me.z, me.c, me.own, me.innet, me.p
    bx, by = me.bx, me.by
    T, D = x_in.shape
    TT = 2 * T
    wide = wo_in.shape[1]
    hidden = w1_in.shape[1]
    arrays = range(6)
    third = 5

    def other_quad(e):
        bit = 8 << e
        return (me.dp + bit - 2 * bit * ((me.dp // bit) % 2), z)

    def other_z(t):
        return (me.dp, lax.rem(z + t, 4))

    g3_load = pltpu.make_async_copy(g3_in, gb[5], ld.at[32])
    g3_load.start()
    bar = pltpu.get_barrier_semaphore()
    greeted = [me.sib, me.xn, me.yn] + [other_z(t) for t in (1, 2, 3)] + [other_quad(e) for e in range(spare)]
    for d in greeted:
        pl.semaphore_signal(bar, inc=1, device_id=d, device_id_type=MESH)
    pl.semaphore_wait(bar, len(greeted))

    quarters = [s[0] // 4 for s in shapes]
    halves = [half_of(q) for q in quarters]

    def add_rows(dst, sources, rows):
        def body(t, carry):
            r = rows_of(t * 16, 16)
            total = dst[r, :].astype(F32)
            for src in sources:
                total = total + src[r, :].astype(F32)
            dst[r, :] = total.astype(BF16)
            return carry

        lax.fori_loop(0, rows // 16, body, 0)

    def z_first(i, j):
        return i == third and j == Z_FIRST

    def first_half(i, j, who):
        return gb[i].at[j, rows_of(who * quarters[i], halves[i]), :]

    def second_half(i, j, who):
        return gb[i].at[j, rows_of(who * quarters[i] + halves[i], quarters[i] - halves[i]), :]

    def whole(i, j, who):
        return gb[i].at[j, rows_of(who * quarters[i], quarters[i]), :]

    def round1(i, j):
        copies = []
        for b in (0, 1):
            copies.append(
                remote(first_half(i, j, b * 2 + 1 - bx), ra1[i].at[j, b], s1.at[i, j, b], r1.at[i, j, b], me.xn)
            )
            copies.append(
                remote(second_half(i, j, (1 - by) * 2 + b), rb1[i].at[j, b], s1.at[i, j, 2 + b], r1.at[i, j, 2 + b], me.yn)
            )
        return copies

    def round2(i, j):
        return [
            remote(first_half(i, j, (1 - by) * 2 + bx), ra2[i].at[j], s2.at[i, j, 0], r2.at[i, j, 0], me.yn),
            remote(second_half(i, j, by * 2 + 1 - bx), rb2[i].at[j], s2.at[i, j, 1], r2.at[i, j, 1], me.xn),
        ]

    def round_z(i, j):
        slot = lax.rem(z - (2 * c + j) + 3 + 4, 4)
        src = gb[i].at[j] if z_first(i, j) else whole(i, j, p)
        return remote(src, landing(i, j, slot), sz.at[i, j], rzs.at[i, slot], (me.dp, 2 * c + j))

    def landing(i, j, slot):
        if i == third and not z_first(i, j):
            return rz[i].at[slot, pl.ds(0, quarters[i]), :]
        return rz[i].at[slot]

    def landed_z(i, j, slot):
        return remote(landing(i, j, slot), landing(i, j, slot), sz.at[i, j], rzs.at[i, slot], me.sib)

    def spread(i, j):
        src = whole(i, j, p)
        dst = final[i].at[rows_of(p * quarters[i], quarters[i]), :]
        return [
            remote(src, dst, sx.at[i], rx.at[i], me.xn),
            remote(src, dst, sy.at[i], ry.at[i], me.yn),
            remote(src, dst, ss.at[i, 0], rs.at[i, 0], me.sib),
        ], pltpu.make_async_copy(src, dst, ld.at[33 + i])

    def quarter_rows(i, who, second=None):
        q, h = quarters[i], halves[i]
        if second is None:
            return final[i].at[rows_of(who * q, q), :]
        if second:
            return final[i].at[rows_of(who * q + h, q - h), :]
        return final[i].at[rows_of(who * q, h), :]

    def hand_on(i, slot, ref):
        return remote(ref, ref, ss.at[i, slot], rs.at[i, slot], me.sib)

    def pass_x(i):
        r = quarter_rows(i, me.px, False)
        return remote(r, r, sf.at[i, 0], rf.at[i, 0], me.yn), hand_on(i, 1, quarter_rows(i, me.px))

    def pass_y(i):
        r = quarter_rows(i, me.py, True)
        return remote(r, r, sf.at[i, 1], rf.at[i, 1], me.xn), hand_on(i, 2, quarter_rows(i, me.py))

    def pass_last(i):
        return hand_on(i, 3, quarter_rows(i, me.pd, False)), hand_on(i, 4, quarter_rows(i, me.pd, True))

    def step_1(i, j):
        for copy in round1(i, j):
            copy.start()

    def step_2(i, j):
        for copy in round1(i, j):
            copy.wait_recv()
        add_rows(first_half(i, j, (1 - by) * 2 + bx), [ra1[i].at[j, 1 - by]], halves[i])
        add_rows(second_half(i, j, by * 2 + 1 - bx), [rb1[i].at[j, 1 - bx]], quarters[i] - halves[i])
        for copy in round2(i, j):
            copy.start()

    def step_3(i, j):
        for copy in round2(i, j):
            copy.wait_recv()
        for copy in round1(i, j):
            copy.wait_send()
        add_rows(first_half(i, j, p), [ra1[i].at[j, by], ra2[i].at[j]], halves[i])
        add_rows(
            second_half(i, j, p), [rb1[i].at[j, bx], rb2[i].at[j]], quarters[i] - halves[i]
        )

    def step_z(i, j):
        for slot in range(3):
            landed_z(i, j, slot).wait_recv()
        sources = [landing(i, j, slot) for slot in range(3)]
        if z_first(i, j):
            add_rows(gb[i].at[j], sources, 4 * quarters[i])
        else:
            add_rows(whole(i, j, p), sources, quarters[i])

    def step_spread(i, j):
        for e in range(spare):
            copy = remote(whole(i, j, p), rq[i].at[e], sq.at[i, e], rqs.at[i, e], other_quad(e))
            copy.start()
            copy.wait()
            h = halves[i]
            for k, (part, src) in enumerate(
                (
                    (ra2[i].at[j], rq[i].at[e, pl.ds(0, h), :]),
                    (rb2[i].at[j], rq[i].at[e, pl.ds(h, quarters[i] - h), :]),
                )
            ):
                local = pltpu.make_async_copy(src, part, sq.at[i, spare + k])
                local.start()
                local.wait()
            add_rows(first_half(i, j, p), [ra2[i].at[j]], h)
            add_rows(second_half(i, j, p), [rb2[i].at[j]], quarters[i] - h)
        copies, local = spread(i, j)
        for copy in copies:
            copy.start()
        local.start()

    def step_5(i, j):
        copies, _ = spread(i, j)
        copies[0].wait_recv()
        for copy in pass_x(i):
            copy.start()
        copies[1].wait_recv()
        for copy in pass_y(i):
            copy.start()

    def step_6(i, j):
        pass_x(i)[0].wait_recv()
        pass_y(i)[0].wait_recv()
        for copy in pass_last(i):
            copy.start()
        copies, local = spread(i, j)
        local.wait()
        for copy in copies + [pass_x(i)[0], pass_y(i)[0]] + round2(i, j):
            copy.wait_send()

    items = [
        (5, 0), (5, 1), (3, 0), (4, 0), (3, 1), (4, 1), (2, 0), (2, 1), (0, 0), (1, 0), (0, 1), (1, 1)
    ]

    def send(i, j):
        if z_first(i, j):
            @pl.when(z != 2 * c + j)
            def _():
                round_z(i, j).start()
        else:
            step_1(i, j)

    def step(code):
        stage, (i, j) = code // 16, items[code % 16]
        mine = z == 2 * c + j
        if not z_first(i, j) and stage == 1:
            step_2(i, j)
        elif not z_first(i, j) and stage == 2:
            step_3(i, j)

            @pl.when(jnp.logical_not(mine))
            def _():
                round_z(i, j).start()
        else:
            order = {0: (step_z, step_1), 1: (step_2,), 2: (step_3, step_spread), 3: (step_z, step_spread)}

            @pl.when(mine)
            def _():
                for part in order.get(stage, (step_5,) if stage == 4 else (step_6,)):
                    part(i, j)

            if stage == 5:
                @pl.when(jnp.logical_not(mine))
                def _():
                    round_z(i, j).wait_send()
                    if not z_first(i, j):
                        for copy in round2(i, j):
                            copy.wait_send()

    mark = [0]

    def checkpoint():
        for code in SCHEDULE[mark[0]]:
            step(code)
        mark[0] += 1

    loads = [0]

    def load(src, dst):
        copy = pltpu.make_async_copy(src, dst, ld.at[loads[0]])
        copy.start()
        loads[0] += 1
        return copy


    def loop(count, body):
        lax.fori_loop(0, count, lambda t, carry: (body(t), carry)[1], 0)

    def feed_forward(b_ref, d1, d2):
        def grads(w3, cot):
            copies = [load(w3_in, w3), load(cot_in, cot), load(d1_in, d1), load(d2_in, d2)]
            b_load = load(b_in, b_ref)
            g3_load.wait()
            for j in (0, 1):
                send(5, j)
            for copy in copies:
                copy.wait()
            for j in (0, 1):
                def rows_body(t):
                    rows = rows_of(t * 256, 256)
                    dm = dot_nt(cot[rows, :], w3[j])
                    d1[j, rows, :] = (dm * d1[j, rows, :].astype(F32)).astype(BF16)
                    d2[j, rows, :] = (dm * d2[j, rows, :].astype(F32)).astype(BF16)

                loop(TT // 256, rows_body)
                if j == 0:
                    b_load.wait()
                for i, d in ((3, d1), (4, d2)):
                    for start in range(0, hidden, 256):
                        size = min(256, hidden - start)
                        gb[i][j, pl.ds(start, size), :] = dot_tn(d[j, :, pl.ds(start, size)], b_ref[...]).astype(BF16)
                    send(i, j)
                    checkpoint()

        pl.run_scoped(grads, pltpu.VMEM((2, hidden, D), BF16), pltpu.VMEM((TT, D), BF16))

        def first_two(w1, w2):
            for copy in (load(w1_in, w1), load(w2_in, w2)):
                copy.wait()

            def db_rows(row):
                rows = rows_of(row, 256)
                total = dot(d1[0, rows, :], w1[0]) + dot(d2[0, rows, :], w2[0])
                return total + dot(d1[1, rows, :], w1[1]) + dot(d2[1, rows, :], w2[1])

            for t in range(T // 256):
                part = pl.ds(t * 256, 256)
                hs[part, :] = db_rows(T + t * 256)
                swap(t).start()
                checkpoint()
            for t in range(T // 256):
                dh[pl.ds(t * 256, 256), :] = db_rows(t * 256)
                checkpoint()

        pl.run_scoped(first_two, pltpu.VMEM((2, hidden, D), BF16), pltpu.VMEM((2, hidden, D), BF16))

    def swap(t):
        part = pl.ds(t * 256, 256)
        return remote(hs.at[part, :], hr.at[part, :], es.at[t], er.at[t], me.sib)

    def swap_low(t):
        part = pl.ds(t * 256, 256)
        return remote(dhl.at[part, :], dhl.at[pl.ds(T + t * 256, 256), :], es.at[2 + t], er.at[2 + t], me.sib)

    def swap_da(t):
        part = pl.ds(t * 256, 256)
        return remote(es_da.at[part, :], er_da.at[part, :], es.at[4 + t], er.at[4 + t], me.sib)

    def swap_out(t):
        part = pl.ds(t * 256, 256)
        return remote(es_da.at[part, :], er_out.at[part, :], es.at[6 + t], er.at[6 + t], me.sib)

    pl.run_scoped(
        feed_forward, pltpu.VMEM((TT, D), BF16), pltpu.VMEM((2, TT, hidden), BF16), pltpu.VMEM((2, TT, hidden), BF16)
    )

    lane = lax.broadcasted_iota(jnp.int32, (UNIT, UNIT), 1)
    low_half = lane < DH
    keep = [low_half.astype(F32).astype(BF16), (lane >= DH).astype(F32).astype(BF16)]

    def stacked(values):
        return jnp.concatenate([values * keep[0], values * keep[1]], axis=0)

    def head_mean(values):
        mean0 = jnp.sum(jnp.where(low_half, values, 0.0), axis=-1, keepdims=True) / DH
        mean1 = jnp.sum(jnp.where(low_half, 0.0, values), axis=-1, keepdims=True) / DH
        return jnp.where(low_half, mean0, mean1)

    def attention(dproj, a_ref):
        a_load = load(a_in, a_ref)

        def inner(qkv, u_ref, o_ref, p_ref, wo, gain):
            copies = [
                load(src, dst)
                for src, dst in (
                    (wo_in, wo), (u_in, u_ref), (o_in, o_ref), (p_in, p_ref), (qkv_in, qkv), (gain_in, gain)
                )
            ]
            pl.run_scoped(hidden_grads, pltpu.VMEM((T, D), F32))
            for copy in copies:
                copy.wait()
            gacc[...] = jnp.zeros_like(gacc)
            pl.run_scoped(out_grads, pltpu.VMEM((2, TT, wide), BF16))
            pl.run_scoped(functools.partial(heads, qkv, u_ref, o_ref, p_ref, wo, gain), pltpu.VMEM((TT, wide), F32))

        def hidden_grads(h_ref):
            for copy in (load(h_in, h_ref), load(cot_in.at[pl.ds(0, T), :], es_da)):
                copy.wait()
            for t in range(T // 256):
                swap(t).wait_recv()

                def rows_body(r):
                    rows = rows_of(t * 256 + r * 64, 64)
                    db = dh[rows, :] + hr[rows, :]
                    h = h_ref[rows, :]
                    factor = rms_factor(h)
                    normed = h * factor
                    grad = es_da[rows, :].astype(F32) + factor * (
                        db - normed * jnp.mean(db * normed, axis=-1, keepdims=True)
                    )
                    dh[rows, :] = grad
                    dhl[rows, :] = grad.astype(BF16)

                loop(4, rows_body)
                swap_low(t).start()
                checkpoint()
        def out_grads(z_ref):
            z_load = load(z_in, z_ref)
            for t in range(T // 256):
                swap_low(t).wait_recv()
            z_load.wait()
            for j in (0, 1):
                gb[2][j] = dot_tn(z_ref[j], dhl[...]).astype(BF16)
                send(2, j)
                checkpoint()

        def heads(qkv, u_ref, o_ref, p_ref, wo, gain, dz_ref):
            for j in (0, 1):
                def dz_rows(t):
                    rows = rows_of(t * 256, 256)
                    dz_ref[rows, :] = dot_nt(dhl[rows, :], wo[j])

                loop(TT // 256, dz_rows)

                def unit(t):
                    rows = rows_of(t * UNIT, UNIT)
                    for pair in range(wide // UNIT):
                        cols = pl.ds(pair * UNIT, UNIT)
                        q, k, v = (qkv[j, rows, pl.ds(f * wide + pair * UNIT, UNIT)] for f in range(3))
                        o, u, dz = o_ref[j, rows, cols], u_ref[j, rows, cols], dz_ref[rows, cols]
                        gain_row = gain[j, :, cols]
                        factor = lax.rsqrt(head_mean(o * o) + EPSILON)
                        normed = o * factor
                        s = jax.nn.sigmoid(u)
                        act = u * s
                        dzn = dz * normed
                        gacc[j, :, cols] += jnp.sum((dzn * act).reshape(UNIT // 8, 8, UNIT), axis=0)
                        du = (dzn * gain_row * s * (1.0 + u * (1.0 - s))).astype(BF16)
                        dn = dz * act * gain_row
                        do = stacked((factor * (dn - normed * head_mean(dn * normed))).astype(BF16))
                        soft_low = p_ref[j, pair, t]
                        soft = soft_low.astype(F32)
                        dv = dot_tn(soft_low, do)
                        dp = dot_nt(do, v)
                        ds = (soft * (dp - jnp.sum(dp * soft, axis=-1, keepdims=True))).astype(BF16)
                        dq = dot(jnp.concatenate([ds[:UNIT], ds[UNIT:]], axis=1), stacked(k)) * DH ** (-0.5)
                        dk = dot_tn(ds, stacked(q)) * DH ** (-0.5)
                        for f, value in enumerate((dq, dk, dv)):
                            dproj[j, rows, pl.ds(f * wide + pair * UNIT, UNIT)] = value.astype(BF16)
                        dproj[j, rows, pl.ds(3 * wide + pair * UNIT, UNIT)] = du

                for part in range(2):
                    loop(TT // UNIT // 2, lambda t: unit(t + part * (TT // UNIT // 2)))
                    checkpoint()
                if j == 0:
                    a_load.wait()
                for i in (0, 1):
                    def block(t):
                        rows = pl.ds(pl.multiple_of(t * 256, 256), 256)
                        cols = pl.ds(i * 2 * wide, 2 * wide)
                        gb[i][j, rows, :] = dot_tn(a_ref[:, rows], dproj[j, :, cols]).astype(BF16)

                    loop(D // 256, block)
                    send(i, j)
                    checkpoint()

        pl.run_scoped(
            inner,
            pltpu.VMEM((2, TT, 3 * wide), BF16),
            pltpu.VMEM((2, TT, wide), F32),
            pltpu.VMEM((2, TT, wide), F32),
            pltpu.VMEM((2, wide // UNIT, TT // UNIT, 2 * UNIT, UNIT), BF16),
            pltpu.VMEM((2, wide, D), BF16),
            pltpu.VMEM((2, 1, wide), F32),
        )

        def inputs_part(w0, x_ref):
            for copy in (load(w0_in, w0), load(x_in, x_ref)):
                copy.wait()

            def da_rows(row):
                rows = rows_of(row, 256)
                return dot_nt(dproj[0, rows, :], w0[0]) + dot_nt(dproj[1, rows, :], w0[1])

            for t in range(T // 256):
                es_da[pl.ds(t * 256, 256), :] = da_rows(T + t * 256).astype(BF16)
                swap_da(t).start()
                checkpoint()
            for t in range(T // 256):
                hs[pl.ds(t * 256, 256), :] = da_rows(t * 256)
                checkpoint()
            for t in range(T // 256):
                swap_da(t).wait_recv()

                def rows_body(r):
                    rows = rows_of(t * 256 + r * 64, 64)
                    da = hs[rows, :] + er_da[rows, :].astype(F32)
                    x = x_ref[rows, :].astype(F32)
                    factor = rms_factor(x)
                    normed = x * factor
                    dh[rows, :] = dh[rows, :] + factor * (
                        da - normed * jnp.mean(da * normed, axis=-1, keepdims=True)
                    )

                loop(4, rows_body)
                checkpoint()

        for t in range(T // 256):
            swap(t).wait_send()
        pl.run_scoped(inputs_part, pltpu.VMEM((2, D, 4 * wide), BF16), pltpu.VMEM((T, D), BF16))

    pl.run_scoped(attention, pltpu.VMEM((2, TT, 4 * wide), BF16), pltpu.VMEM((TT, D), BF16))
    dx_save = load(dh, dx_out)

    def gain_sum(k, src, dst, device, total):
        copy = remote(src, dst, gss.at[k], grs.at[k], device)
        copy.start()
        copy.wait()
        total[...] += dst[...]

    gain_sum(0, gacc, gx, me.xn, gacc)
    checkpoint()
    gain_sum(1, gacc, gy, me.yn, gacc)

    def gain_z(j):
        slot = lax.rem(z - (2 * c + j) + 3 + 4, 4)
        return remote(gacc.at[j], gz.at[slot], gss.at[2 + j], grs.at[4 + slot], (me.dp, 2 * c + j))

    for j in (0, 1):
        @pl.when(z != 2 * c + j)
        def _():
            gain_z(j).start()

    def output_part(m_ref, w3, stage):
        for copy in (load(m_in, m_ref), load(w3_in, w3), load(h_in, stage)):
            copy.wait()
        for t in range(T // 256):
            swap_da(t).wait_send()

        def out_rows(row):
            rows = rows_of(row, 256)
            return dot(m_ref[0, rows, :], w3[0]) + dot(m_ref[1, rows, :], w3[1])

        for t in range(T // 256):
            es_da[pl.ds(t * 256, 256), :] = out_rows(T + t * 256).astype(BF16)
            swap_out(t).start()
            checkpoint()
        for t in range(T // 256):
            rows = pl.ds(t * 256, 256)
            stage[rows, :] = stage[rows, :] + out_rows(t * 256)
            checkpoint()
        for t in range(T // 256):
            swap_out(t).wait_recv()
            rows = pl.ds(t * 256, 256)
            stage[rows, :] = stage[rows, :] + er_out[rows, :].astype(F32)

        load(stage, out_out).wait()

    pl.run_scoped(
        output_part, pltpu.VMEM((2, TT, hidden), BF16), pltpu.VMEM((2, hidden, D), BF16), pltpu.VMEM((T, D), F32)
    )

    def gain_final():
        return remote(gain_sent, gain_out, gss.at[7], grs.at[7], me.sib)

    @pl.when(innet)
    def _():
        for slot in range(3):
            remote(gz.at[slot], gz.at[slot], gss.at[2], grs.at[4 + slot], me.sib).wait_recv()
            gacc[own] += gz[slot]
        for e in range(spare):
            copy = remote(gacc.at[own], gq.at[e], gss.at[8 + e], grs.at[8 + e], other_quad(e))
            copy.start()
            copy.wait()
            gacc[own] += gq[e]
        gain_sent[...] = jnp.sum(gacc[own], axis=0, keepdims=True)
        local = pltpu.make_async_copy(gain_sent, gain_out, ld.at[39])
        local.start()
        gain_final().start()
        local.wait()
        gain_final().wait_send()

    checkpoint()

    @pl.when(jnp.logical_not(innet))
    def _():
        gain_final().wait_recv()
        for i in arrays:
            spread(i, 0)[0][2].wait_recv()
            pass_x(i)[1].wait_recv()
            pass_y(i)[1].wait_recv()
            for copy in pass_last(i):
                copy.wait_recv()

    @pl.when(innet)
    def _():
        for i in arrays:
            for copy in (pass_x(i)[1], pass_y(i)[1]) + pass_last(i):
                copy.wait_send()

    for j in (0, 1):
        @pl.when(z != 2 * c + j)
        def _():
            gain_z(j).wait_send()

    for t in range(T // 256):
        swap_low(t).wait_send()
        swap_out(t).wait_send()
    dx_save.wait()


def run_backward(x, kept, spare):
    T, D = x.shape
    TT = 2 * T
    w0, wo, w1, w2, w3 = kept[:5]
    wide, hidden = wo.shape[1], w1.shape[1]
    shapes = [(D, 2 * wide), (D, 2 * wide)] + [w.shape[1:] for w in (wo, w1, w2, w3)]
    q = [s[0] // 4 for s in shapes]
    h = [half_of(n) for n in q]
    cols = [s[1] for s in shapes]
    n = range(6)
    lands = [2] * 6
    extra = max(spare, 1)
    vmem = (
        [pltpu.VMEM((2,) + s, BF16) for s in shapes]
        + [pltpu.VMEM((lands[i], 2, h[i], cols[i]), BF16) for i in n]
        + [pltpu.VMEM((lands[i], 2, q[i] - h[i], cols[i]), BF16) for i in n]
        + [pltpu.VMEM((lands[i], h[i], cols[i]), BF16) for i in n]
        + [pltpu.VMEM((lands[i], q[i] - h[i], cols[i]), BF16) for i in n]
        + [pltpu.VMEM((3, q[i] if i < 5 else 4 * q[i], cols[i]), BF16) for i in n]
        + [
            pltpu.VMEM((T, D), F32),
            pltpu.VMEM((T, D), F32),
            pltpu.VMEM((T, D), BF16),
            pltpu.VMEM((T, D), BF16),
            pltpu.VMEM((T, D), BF16),
            pltpu.VMEM((T, D), F32),
            pltpu.VMEM((TT, D), BF16),
            pltpu.VMEM((2, 8, wide), F32),
            pltpu.VMEM((2, 8, wide), F32),
            pltpu.VMEM((2, 8, wide), F32),
            pltpu.VMEM((3, 8, wide), F32),
            pltpu.VMEM((extra, 8, wide), F32),
            pltpu.VMEM((1, wide), F32),
        ]
    )
    dma = pltpu.SemaphoreType.DMA
    sems = [
        dma((6, 2, 4)), dma((6, 2, 4)), dma((6, 2, 2)), dma((6, 2, 2)), dma((6, 2)), dma((6, 3)),
        dma((6,)), dma((6,)), dma((6,)), dma((6,)), dma((6, 2)), dma((6, 2)), dma((6, 5)), dma((6, 5)),
        dma((6, 2 + extra)), dma((6, extra)), dma((40,)), dma((8,)), dma((8,)), dma((8 + extra,)), dma((8 + extra,)),
    ]
    outs = [((T, D), F32), ((T, D), F32)] + [(s, BF16) for s in shapes] + [((1, wide), F32)]
    if spare:
        outs += [((spare, q[i], cols[i]), BF16) for i in n]
    return pl.pallas_call(
        functools.partial(backward_kernel, shapes, spare),
        out_shape=[jax.ShapeDtypeStruct(s, t) for s, t in outs],
        in_specs=any_spec(1 + len(kept)),
        out_specs=any_spec(len(outs)),
        scratch_shapes=vmem + sems,
        compiler_params=pltpu.CompilerParams(collective_id=1, has_side_effects=True, vmem_limit_bytes=VMEM_LIMIT),
        cost_estimate=pl.CostEstimate(flops=30 * 10**9, bytes_accessed=80 * 10**6, transcendentals=10**6),
        name="backward",
    )(x, *kept)


def finish_kernel(wide, *refs):
    ready, grads = refs[:2], refs[2:8]
    ready_out, outs = refs[8:10], refs[10:18]
    low, full = refs[18:24], refs[24:30]
    held = refs[30:32]
    sems, done = refs[32:]
    loads = [pltpu.make_async_copy(src, dst, sems.at[i]) for i, (src, dst) in enumerate(zip(grads, low))]
    moves = [pltpu.make_async_copy(src, dst, sems.at[6 + i]) for i, (src, dst) in enumerate(zip(ready, held))]
    for copy in loads[:1] + moves + loads[1:]:
        copy.start()
    saves = []

    def hand_out(i):
        moves[i].wait()
        copy = pltpu.make_async_copy(held[i], ready_out[i], done.at[8 + i])
        copy.start()
        saves.append(copy)
    for i in range(6):
        loads[i].wait()

        def widen(t, carry):
            rows = rows_of(t * 64, 64)
            full[i][rows, :] = low[i][rows, :].astype(F32)
            return carry

        lax.fori_loop(0, low[i].shape[0] // 64, widen, 0)
        if i < 2:
            parts = [(full[i].at[:, pl.ds(n * wide, wide)], outs[2 * i + n], done.at[2 * i + n]) for n in range(2)]
        else:
            parts = [(full[i], outs[2 + i], done.at[2 + i])]
        for part in parts:
            copy = pltpu.make_async_copy(*part)
            copy.start()
            saves.append(copy)
        if i < 2:
            hand_out(i)
    for copy in saves:
        copy.wait()


def run_finish(ready, grads, wide):
    shapes = [g.shape for g in grads]
    outs = [r.shape for r in ready] + [(shapes[0][0], wide)] * 4 + shapes[2:]
    return pl.pallas_call(
        functools.partial(finish_kernel, wide),
        out_shape=[jax.ShapeDtypeStruct(s, F32) for s in outs],
        in_specs=any_spec(8),
        out_specs=any_spec(len(outs)),
        scratch_shapes=[pltpu.VMEM(s, BF16) for s in shapes]
        + [pltpu.VMEM(s, F32) for s in shapes]
        + [pltpu.VMEM(r.shape, F32) for r in ready]
        + [pltpu.SemaphoreType.DMA((8,)), pltpu.SemaphoreType.DMA((10,))],
        compiler_params=pltpu.CompilerParams(vmem_limit_bytes=VMEM_LIMIT),
        cost_estimate=pl.CostEstimate(flops=0, bytes_accessed=30 * 10**6, transcendentals=0),
        name="finish",
    )(*ready, *grads)


def shards(
    inputs, w_query, w_key, w_value, w_gate, head_gain, w_out, w_first, w_second, w_third, cotangent
):
    wide = w_query.shape[1]
    weights = [w_query, w_key, w_value, w_gate, w_out, w_first.T, w_second.T, w_third]
    gain = head_gain.reshape(1, wide)
    kept = run_forward(inputs, cotangent, gain, weights)
    spare = (lax.axis_size("dp") // 8).bit_length() - 1
    results = run_backward(inputs, kept, spare)
    output, grad_inputs, *grads = run_finish(results[:2], results[2:8], wide)
    g_query, g_key, g_value, g_gate, g_out, g_first, g_second, g_third = grads
    g_gain = results[8].reshape(wide)
    return (
        output, grad_inputs, g_query, g_key, g_value, g_gate, g_gain, g_out, g_first.T, g_second.T, g_third
    )


def solution(mesh):
    rows, columns = P(("dp", "mp"), None), P(None, "mp")
    heads = P("mp", None)
    return jax.shard_map(
        shards,
        mesh=mesh,
        in_specs=(rows, columns, columns, columns, columns, P("mp"), heads, columns, columns, heads, rows),
        out_specs=(rows, rows, columns, columns, columns, columns, P("mp"), heads, columns, columns, heads),
        check_vma=False,
    )
```
